32 devices in a mesh: dp: 8 (over z, y), tensor: 4 (over x, core).
Axes of the slice: x: 2, y: 2, z: 4, core: 2. Of those that a mesh axis runs over, the one named last changes fastest.
Arguments:
- prefill_rows: bfloat16 [4096, 2048], P(('dp', 'tensor')), may hold values from -6 to 6
- decode_rows: bfloat16 [64, 2048], P(('dp', 'tensor')), may hold values from -6 to 6
- deal_order: int32 [64], replicated, may hold values from 0 to 63, each once
- prefill_offset: int32 [8], P('dp'), may hold values from 0 to 1024, as said below
- cache_length: int32 [64], P('dp'), may hold values from 1 to 1024, as said below
- prefill_cache: bfloat16 [2, 8, 1024, 1024], P(None, 'dp', None, 'tensor'), may hold values from -480 to 480, as said below
- decode_cache: bfloat16 [2, 64, 1024, 1024], P(None, 'dp', None, 'tensor'), may hold values from -480 to 480, as said below
- qkv_weight: bfloat16 [2048, 8, 512], P(None, 'tensor'), may hold values from -0.125 to 0.125
- out_weight: bfloat16 [2048, 2048], P('tensor'), may hold values from -0.125 to 0.125
- attention_gain: float32 [2048], replicated, may hold values from 0.1 to 1.9
- forward_gain: float32 [2048], replicated, may hold values from 0.1 to 1.9
- gate_weight: bfloat16 [2048, 8192], P(None, 'tensor'), may hold values from -0.125 to 0.125
- up_weight: bfloat16 [2048, 8192], P(None, 'tensor'), may hold values from -0.125 to 0.125
- down_weight: bfloat16 [8192, 2048], P('tensor'), may hold values from -0.0625 to 0.0625
Outputs:
- prefill_out: bfloat16 [4096, 2048], P(('dp', 'tensor'))
- decode_out: bfloat16 [64, 2048], P(('dp', 'tensor'))
- prefill_entries: bfloat16 [2, 4096, 1024], P(None, 'dp', 'tensor')
- decode_entries: bfloat16 [2, 64, 1024], P(None, 'dp', 'tensor')
The draws below stay inside these ranges and needn't reach their ends.
Inputs may be any that keep to these rules, and one draw needn't show every extreme that they name: A permutation: request r is held in slot deal_order[r]; slot s belongs to request group s // 8. `prefill_offset`: stored positions of each prefill request; some request has exactly 1024. `cache_length`: stored positions of the decode request in each slot; some slot has exactly 1024. `prefill_cache`: stored rotated keys and values; positions at or past a request's stored count hold unrelated numbers. `decode_cache`: stored rotated keys and values; positions at or past a slot's stored count hold unrelated numbers.
All inputs are finite; a program needn't handle non-finite values.
Results may differ from the reference program's by a relative error of at most 0.015.
The reference program's roundings to bfloat16 on the way count: a program that leaves them out, or rounds other values in their place, can miss the bound.
Values may be sent and summed in bfloat16 or wider, within the bound.
No kernel may reach another device: no remote copies, remote signals or barrier semaphores. Data moves between devices by JAX's collectives and lax.ppermute only.
A program may use at most 128 MiB of HBM per device.

```python
import jax
import jax.numpy as jnp
from jax import lax

D = 2048
H = 16
KVH = 8
HD = 128
FF = 8192
PTOK = 512
PCACHE = 1024
CACHE = 1024
RDT = 2
NDEC = 64
NPRE = 8
N_DP = 8
N_TENSOR = 4


def cache_draw(key, entries, stored):
    noise = jax.random.normal(key, (2, entries, stored, KVH * HD), jnp.float32)
    noise = jnp.clip(noise, -6.0, 6.0)
    return noise


def draw_prefill_cache(key, part):
    return cache_draw(key, NPRE, PCACHE).astype(jnp.bfloat16)


def draw_decode_cache(key, part):
    return cache_draw(key, NDEC, CACHE).astype(jnp.bfloat16)


def draw_cache_length(key, part):
    first = jax.random.randint(jax.random.fold_in(key, 1), (NDEC,), 1, CACHE + 1)
    second = jax.random.randint(jax.random.fold_in(key, 2), (NDEC,), 1, CACHE + 1)
    lengths = jnp.minimum(first, second).astype(jnp.int32)
    pinned = jax.random.randint(jax.random.fold_in(key, 3), (), 0, NDEC)
    return lengths.at[pinned].set(CACHE)


def draw_prefill_offset(key, part):
    offsets = jax.random.randint(jax.random.fold_in(key, 4), (NPRE,), 0, PCACHE + 1).astype(jnp.int32)
    pinned = jax.random.randint(jax.random.fold_in(key, 5), (), 0, NPRE)
    return offsets.at[pinned].set(PCACHE)


def block_scale(stream_key, shape, cuts, least, largest):
    level = 1.0
    for dim, parts in cuts:
        steps = jax.random.uniform(jax.random.fold_in(jax.random.fold_in(stream_key, 6), dim), (parts,), jnp.float32, least / len(cuts), largest / len(cuts))
        level = level * jnp.repeat(jnp.exp(steps), shape[dim] // parts).reshape((-1,) + (1,) * (len(shape) - 1 - dim))
    return level


def bell_draw(key, shape, deviation, most, split=(), held_as=jnp.bfloat16):
    level = block_scale(key, shape, split, -0.22, 0.18) if split else 1.0
    drawn = jax.random.normal(key, shape, jnp.float32) * deviation * level
    return jnp.minimum(jnp.maximum(drawn, -most), most).astype(held_as)


def setup_inputs(seed: int = 0) -> dict:
    streams_of = jax.random.split(jax.random.key(seed), 15)
    prefill_rows = bell_draw(streams_of[0], (NPRE * PTOK, D), 1.0, 6.0, ((0, 32),))
    decode_rows = bell_draw(streams_of[1], (NDEC, D), 1.0, 6.0, ((0, 32),))
    deal_order = jax.random.permutation(streams_of[2], NDEC).astype(jnp.int32)
    prefill_offset = draw_prefill_offset(jax.random.fold_in(streams_of[14], 71), 0)
    cache_length = draw_cache_length(jax.random.fold_in(streams_of[14], 71), 0)
    prefill_cache = draw_prefill_cache(jax.random.fold_in(streams_of[14], 71), 0)
    decode_cache = draw_decode_cache(jax.random.fold_in(streams_of[14], 71), 0)
    qkv_weight = bell_draw(streams_of[7], (D, KVH, (H // KVH + 2) * HD), D ** -0.5, 0.125, ((1, 4),))
    out_weight = bell_draw(streams_of[8], (H * HD, D), (H * HD) ** -0.5, 0.125, ((0, 4),))
    attention_gain = jnp.clip(1.0 + 0.18 * jax.random.normal(streams_of[9], (D,), jnp.float32), 0.1, 1.9)
    forward_gain = jnp.clip(1.0 + 0.18 * jax.random.normal(streams_of[10], (D,), jnp.float32), 0.1, 1.9)
    gate_weight = bell_draw(streams_of[11], (D, FF), D ** -0.5, 0.125, ((1, 4),))
    up_weight = bell_draw(streams_of[12], (D, FF), D ** -0.5, 0.125, ((1, 4),))
    down_weight = bell_draw(streams_of[13], (FF, D), FF ** -0.5, 0.0625, ((0, 4),))
    return dict(prefill_rows=prefill_rows, decode_rows=decode_rows, deal_order=deal_order, prefill_offset=prefill_offset, cache_length=cache_length, prefill_cache=prefill_cache, decode_cache=decode_cache, qkv_weight=qkv_weight, out_weight=out_weight, attention_gain=attention_gain, forward_gain=forward_gain, gate_weight=gate_weight, up_weight=up_weight, down_weight=down_weight)


EPSILON = 1e-06
THETA = 1000000.0
NEGATIVE = -1e+30

def root_norm(rows, gain):
    values = rows.astype(jnp.float32)
    spread = lax.optimization_barrier(jnp.mean(values * values, axis=-1, keepdims=True))
    return (values * lax.rsqrt(spread + EPSILON) * gain.astype(jnp.float32)).astype(jnp.bfloat16)

def rotate(vectors, places):
    halfway = vectors.shape[-1] // 2
    powers = jnp.arange(halfway, dtype=jnp.float32) * (2.0 / vectors.shape[-1])
    inverse = THETA ** (-powers)
    angles = places.astype(jnp.float32)[:, None] * inverse[None, :]
    cosine = jnp.cos(angles)[:, None, :]
    sine_part = jnp.sin(angles)[:, None, :]
    leading = vectors[..., :halfway]
    trailing = vectors[..., halfway:]
    return jnp.concatenate([leading * cosine - trailing * sine_part, trailing * cosine + leading * sine_part], axis=-1)

def project(normed, places, qkv_weight):
    heads = qkv_weight.shape[1]
    width = qkv_weight.shape[2]
    groups = width // HD - 2
    count = normed.shape[0]
    mixed = jnp.dot(normed, qkv_weight.reshape(qkv_weight.shape[0], heads * width), preferred_element_type=jnp.float32)
    mixed = mixed.reshape(count, heads, groups + 2, HD)
    queries = rotate(mixed[:, :, :groups].reshape(count, heads * groups, HD), places)
    queries = queries.reshape(count, heads, groups, HD).astype(jnp.bfloat16)
    new_keys = rotate(mixed[:, :, groups], places).astype(jnp.bfloat16)
    new_values = mixed[:, :, groups + 1].astype(jnp.bfloat16)
    return (queries, new_keys, new_values)

def fill_attend(queries, new_keys, new_values, cache_keys, cache_values, offset):
    scaling = 1.0 / HD ** 0.5
    count = queries.shape[0]
    prior_count = cache_keys.shape[0]
    query_wide = queries.astype(jnp.float32)
    cached_scores = jnp.einsum('qkgd,skd->kgqs', query_wide, cache_keys.astype(jnp.float32)) * scaling
    fresh_scores = jnp.einsum('qkgd,skd->kgqs', query_wide, new_keys.astype(jnp.float32)) * scaling
    cached_allowed = jnp.arange(prior_count, dtype=jnp.int32)[None, :] < offset
    fresh_allowed = jnp.arange(count, dtype=jnp.int32)[None, :] <= jnp.arange(count, dtype=jnp.int32)[:, None]
    scores = jnp.concatenate([jnp.where(cached_allowed, cached_scores, NEGATIVE), jnp.where(fresh_allowed, fresh_scores, NEGATIVE)], axis=-1)
    row_top = lax.optimization_barrier(jnp.max(scores, axis=-1, keepdims=True))
    weights = jnp.exp(scores - row_top)
    weights = (weights / lax.optimization_barrier(jnp.sum(weights, axis=-1, keepdims=True))).astype(jnp.bfloat16).astype(jnp.float32)
    attended = jnp.einsum('kgqs,skd->qkgd', weights[..., :prior_count], cache_values.astype(jnp.float32))
    attended = attended + jnp.einsum('kgqs,skd->qkgd', weights[..., prior_count:], new_values.astype(jnp.float32))
    return attended.astype(jnp.bfloat16)

def step_attend(queries, new_keys, new_values, cache_keys, cache_values, lengths):
    scaling = 1.0 / HD ** 0.5
    stored = cache_keys.shape[1]
    query_wide = queries.astype(jnp.float32)
    cached_scores = jnp.einsum('nkgd,nskd->nkgs', query_wide, cache_keys.astype(jnp.float32)) * scaling
    own_scores = jnp.einsum('nkgd,nkd->nkg', query_wide, new_keys.astype(jnp.float32))[..., None] * scaling
    allowed = (jnp.arange(stored, dtype=jnp.int32)[None, :] < lengths[:, None])[:, None, None, :]
    scores = jnp.concatenate([jnp.where(allowed, cached_scores, NEGATIVE), own_scores], axis=-1)
    row_top = lax.optimization_barrier(jnp.max(scores, axis=-1, keepdims=True))
    weights = jnp.exp(scores - row_top)
    weights = (weights / lax.optimization_barrier(jnp.sum(weights, axis=-1, keepdims=True))).astype(jnp.bfloat16).astype(jnp.float32)
    attended = jnp.einsum('nkgs,nskd->nkgd', weights[..., :stored], cache_values.astype(jnp.float32))
    attended = attended + weights[..., stored:] * new_values.astype(jnp.float32)[:, :, None, :]
    return attended.astype(jnp.bfloat16)

def feed_forward(inner, gate_weight, up_weight, down_weight):
    gate_part = jnp.dot(inner, gate_weight, preferred_element_type=jnp.float32)
    up_part = jnp.dot(inner, up_weight, preferred_element_type=jnp.float32)
    hidden = (jax.nn.silu(gate_part) * up_part).astype(jnp.bfloat16)
    return jnp.dot(hidden, down_weight, preferred_element_type=jnp.float32)

def reference(prefill_rows, decode_rows, deal_order, prefill_offset, cache_length, prefill_cache, decode_cache, qkv_weight, out_weight, attention_gain, forward_gain, gate_weight, up_weight, down_weight):
    groups = H // KVH
    holder = jnp.zeros((NDEC,), jnp.int32).at[deal_order].set(jnp.arange(NDEC, dtype=jnp.int32))
    dealt = decode_rows[holder]
    fill_normed = root_norm(prefill_rows, attention_gain)
    step_normed = root_norm(dealt, attention_gain)
    fill_places = (prefill_offset[:, None] + jnp.arange(PTOK, dtype=jnp.int32)[None, :]).reshape(NPRE * PTOK)
    fill_query, fill_keys, fill_values = project(fill_normed, fill_places, qkv_weight)
    step_query, step_keys, step_values = project(step_normed, cache_length, qkv_weight)

    def one_request(members):
        return fill_attend(*members)
    fill_att = lax.map(one_request, (fill_query.reshape(NPRE, PTOK, KVH, groups, HD), fill_keys.reshape(NPRE, PTOK, KVH, HD), fill_values.reshape(NPRE, PTOK, KVH, HD), prefill_cache[0].reshape(NPRE, PCACHE, KVH, HD), prefill_cache[1].reshape(NPRE, PCACHE, KVH, HD), prefill_offset))
    fill_att = fill_att.reshape(NPRE * PTOK, H * HD)

    def one_group(members):
        return step_attend(*members)
    slot_group = RDT * N_TENSOR
    step_att = lax.map(one_group, (step_query.reshape(N_DP, slot_group, KVH, groups, HD), step_keys.reshape(N_DP, slot_group, KVH, HD), step_values.reshape(N_DP, slot_group, KVH, HD), decode_cache[0].reshape(N_DP, slot_group, CACHE, KVH, HD), decode_cache[1].reshape(N_DP, slot_group, CACHE, KVH, HD), cache_length.reshape(N_DP, slot_group)))
    step_att = step_att.reshape(NDEC, H * HD)
    fill_resid = (prefill_rows.astype(jnp.float32) + jnp.dot(fill_att, out_weight, preferred_element_type=jnp.float32)).astype(jnp.bfloat16)
    step_resid = (dealt.astype(jnp.float32) + jnp.dot(step_att, out_weight, preferred_element_type=jnp.float32)).astype(jnp.bfloat16)
    fill_final = (fill_resid.astype(jnp.float32) + feed_forward(root_norm(fill_resid, forward_gain), gate_weight, up_weight, down_weight)).astype(jnp.bfloat16)
    step_final = (step_resid.astype(jnp.float32) + feed_forward(root_norm(step_resid, forward_gain), gate_weight, up_weight, down_weight)).astype(jnp.bfloat16)
    decode_out = step_final[deal_order]
    prefill_entries = jnp.stack([fill_keys.reshape(NPRE * PTOK, KVH * HD), fill_values.reshape(NPRE * PTOK, KVH * HD)])
    decode_entries = jnp.stack([step_keys.reshape(NDEC, KVH * HD), step_values.reshape(NDEC, KVH * HD)])
    return (fill_final, decode_out, prefill_entries, decode_entries)
```

```python
import functools
import math

import jax
import jax.numpy as jnp
from jax import lax
from jax.experimental import pallas as pl
from jax.experimental.pallas import tpu as pltpu
from jax.sharding import PartitionSpec as P

HD = 128
EPSILON = 1e-06
THETA = 1000000.0
NEGATIVE = -1e30
MIB = 1 << 20


def swap_cores(value):
    count = lax.axis_size("tensor")
    return lax.ppermute(value, "tensor", [(i, i ^ 1) for i in range(count)])


def from_chip(value, step):
    count = lax.axis_size("tensor")
    chips = count // 2
    return lax.ppermute(
        value, "tensor", [(i, (i // 2 - step) % chips * 2 + i % 2) for i in range(count)]
    )


def swap_groups(value, mask):
    count = lax.axis_size("dp")
    return lax.ppermute(value, "dp", [(i, i ^ mask) for i in range(count)])


def whole(shape):
    return pl.BlockSpec(shape, lambda *_: (0,) * len(shape))


def params(mib):
    return pltpu.CompilerParams(vmem_limit_bytes=mib * MIB)


def cost(flops, moved, exps=0):
    return pl.CostEstimate(flops=int(flops), bytes_accessed=int(moved), transcendentals=int(exps))


def normed(values, gain):
    spread = jnp.mean(values * values, axis=-1, keepdims=True)
    return (values * lax.rsqrt(spread + EPSILON) * gain).astype(jnp.bfloat16)


def turn(vectors, cosine, sine):
    return vectors * cosine + pltpu.roll(vectors, HD // 2, 1) * sine


def project_kernel(n_dec, groups, place, *refs):
    refs = list(refs)
    mine, sib, gain, weight, cosine, sine = refs[:6]
    refs = refs[6:]
    if n_dec:
        dec, dec_cos, dec_sin = refs[:3]
        refs = refs[4:]
        query, entries, dec_query, dec_entries, inner = refs
    else:
        query, entries, inner = refs
    piece = mine.shape[0]
    core = place[0]

    @pl.when(pl.program_id(0) == 0)
    def _():
        scale = gain[...]
        for ref, at in ((mine, core), (sib, 1 - core)):
            start = pl.multiple_of(at * piece, piece)
            inner[pl.ds(start, piece), :] = normed(ref[...].astype(jnp.float32), scale)
        if n_dec:
            inner[2 * piece :, :] = normed(dec[...].astype(jnp.float32), scale)

    mixed = jnp.dot(inner[...], weight[...], preferred_element_type=jnp.float32)

    def put(rows, cos, sin, query_out, entry_out):
        for g in range(groups):
            part = rows[:, g * HD : (g + 1) * HD]
            query_out[:, g * HD : (g + 1) * HD] = turn(part, cos, sin).astype(jnp.bfloat16)
        key = rows[:, groups * HD : (groups + 1) * HD]
        entry_out[0] = turn(key, cos, sin).astype(jnp.bfloat16)
        entry_out[1] = rows[:, (groups + 1) * HD :].astype(jnp.bfloat16)

    put(mixed[: 2 * piece], cosine[...], sine[...], query, entries)
    if n_dec:
        put(mixed[2 * piece :], dec_cos[...], dec_sin[...], dec_query, dec_entries)


def project(place, mine, sib, gain, weight, tables, total, dec=None, dec_tables=None, entries=None):
    piece, width = mine.shape
    cosine, sine = tables
    depth = weight.shape[1] // total["heads"]
    heads = total["heads"]
    groups = depth // HD - 2
    block = 2 * piece
    n_dec = 0 if dec is None else dec.shape[0]
    at_block = pl.BlockSpec((block, HD), lambda j, s: (s[1], 0))
    in_specs = [
        whole((piece, width)),
        whole((piece, width)),
        whole((1, width)),
        pl.BlockSpec((width, depth), lambda j, s: (0, j)),
        at_block,
        at_block,
    ]
    args = [mine, sib, gain, weight, cosine, sine]
    out_shape = [
        jax.ShapeDtypeStruct((block, heads * groups * HD), jnp.bfloat16),
        jax.ShapeDtypeStruct((2, total["tokens"], heads * HD), jnp.bfloat16),
    ]
    out_specs = [
        pl.BlockSpec((block, groups * HD), lambda j, s: (0, j)),
        pl.BlockSpec((2, block, HD), lambda j, s: (0, s[1], j)),
    ]
    aliases = {}
    if n_dec:
        in_specs += [whole((n_dec, width)), whole((n_dec, HD)), whole((n_dec, HD))]
        args += [dec, *dec_tables]
        out_shape += [
            jax.ShapeDtypeStruct((n_dec, heads * groups * HD), jnp.bfloat16),
            jax.ShapeDtypeStruct((2, n_dec, heads * HD), jnp.bfloat16),
        ]
        out_specs += [
            pl.BlockSpec((n_dec, groups * HD), lambda j, s: (0, j)),
            pl.BlockSpec((2, n_dec, HD), lambda j, s: (0, 0, j)),
        ]
    if entries is not None:
        in_specs.append(pl.BlockSpec(memory_space=pl.ANY))
        args.append(entries)
        aliases = {len(args): 1}
    if n_dec and entries is None or entries is not None and not n_dec:
        kernel = functools.partial(project_kernel_plain, entries is not None, n_dec, groups)
    else:
        kernel = functools.partial(project_kernel, n_dec, groups)
    rows = block + n_dec
    return pl.pallas_call(
        kernel,
        out_shape=out_shape,
        grid_spec=pltpu.PrefetchScalarGridSpec(
            num_scalar_prefetch=1,
            grid=(heads,),
            in_specs=in_specs,
            out_specs=out_specs,
            scratch_shapes=[pltpu.VMEM((rows, width), jnp.bfloat16)],
        ),
        input_output_aliases=aliases,
        compiler_params=params(32),
        cost_estimate=cost(2 * rows * weight.size, 2 * (weight.size + 2 * rows * width)),
        name="project",
    )(place, *args)


def project_kernel_plain(has_entries, n_dec, groups, place, *refs):
    refs = list(refs)
    if has_entries:
        del refs[6]
        project_kernel(0, groups, place, *refs)
    else:
        refs.insert(9, None)
        project_kernel(n_dec, groups, place, *refs)


def fill_kernel(groups, place, query, cache_key, cache_value, new_key, new_value, out):
    scaling = 1.0 / math.sqrt(HD)
    count = query.shape[0]
    stored = cache_key.shape[2]
    fresh = new_key.shape[1]
    offset = place[2]
    start = place[1] * count
    old_seen = lax.broadcasted_iota(jnp.int32, (1, stored), 1) < offset
    new_seen = lax.broadcasted_iota(jnp.int32, (count, fresh), 1) <= (
        lax.broadcasted_iota(jnp.int32, (count, fresh), 0) + start
    )
    across = (((1,), (1,)), ((), ()))
    old_key, old_value = cache_key[0, 0], cache_value[0, 0]
    for g in range(groups):
        rows = query[:, g * HD : (g + 1) * HD]
        old = lax.dot_general(rows, old_key, across, preferred_element_type=jnp.float32)
        new = lax.dot_general(rows, new_key[0], across, preferred_element_type=jnp.float32)
        old = jnp.where(old_seen, old * scaling, NEGATIVE)
        new = jnp.where(new_seen, new * scaling, NEGATIVE)
        top = jnp.maximum(
            jnp.max(old, axis=-1, keepdims=True), jnp.max(new, axis=-1, keepdims=True)
        )
        old = jnp.exp(old - top)
        new = jnp.exp(new - top)
        total = jnp.sum(old, axis=-1, keepdims=True) + jnp.sum(new, axis=-1, keepdims=True)
        mix = jnp.dot(old.astype(jnp.bfloat16), old_value, preferred_element_type=jnp.float32)
        mix += jnp.dot(new.astype(jnp.bfloat16), new_value[0], preferred_element_type=jnp.float32)
        out[:, g * HD : (g + 1) * HD] = (mix / total).astype(jnp.bfloat16)


def fill_attend(place, query, cache, entries, heads):
    count = query.shape[0]
    groups = query.shape[1] // heads // HD
    stored = cache.shape[2]
    fresh = entries.shape[1]
    pairs = count * groups * heads * (stored + fresh)
    return pl.pallas_call(
        functools.partial(fill_kernel, groups),
        out_shape=jax.ShapeDtypeStruct(query.shape, jnp.bfloat16),
        grid_spec=pltpu.PrefetchScalarGridSpec(
            num_scalar_prefetch=1,
            grid=(heads,),
            in_specs=[
                pl.BlockSpec((count, groups * HD), lambda j, s: (0, j)),
                pl.BlockSpec((1, 1, stored, HD), lambda j, s: (0, 0, 0, j)),
                pl.BlockSpec((1, 1, stored, HD), lambda j, s: (1, 0, 0, j)),
                pl.BlockSpec((1, fresh, HD), lambda j, s: (0, 0, j)),
                pl.BlockSpec((1, fresh, HD), lambda j, s: (1, 0, j)),
            ],
            out_specs=pl.BlockSpec((count, groups * HD), lambda j, s: (0, j)),
        ),
        compiler_params=params(32),
        cost_estimate=cost(8 * pairs * HD, 2 * (cache.size + entries.size), pairs),
        name="fill_attend",
    )(place, query, cache, cache, entries, entries)


def step_kernel(heads, groups, lengths, query, cache_key, cache_value, new_key, new_value, out):
    scaling = 1.0 / math.sqrt(HD)
    stored = cache_key.shape[2]
    length = lengths[pl.program_id(0)]
    rows = query[0]
    old_key, old_value = cache_key[0, 0], cache_value[0, 0]
    across = (((1,), (1,)), ((), ()))
    old = lax.dot_general(rows, old_key, across, preferred_element_type=jnp.float32)
    seen = lax.broadcasted_iota(jnp.int32, (1, stored), 1) < length
    old = jnp.where(seen, old * scaling, NEGATIVE)
    own = jnp.sum(
        rows.astype(jnp.float32) * new_key[0].astype(jnp.float32), axis=-1, keepdims=True
    )
    own = own * scaling
    top = jnp.maximum(jnp.max(old, axis=-1, keepdims=True), own)
    old = jnp.exp(old - top)
    own = jnp.exp(own - top)
    total = jnp.sum(old, axis=-1, keepdims=True) + own
    mix = jnp.dot(
        (old / total).astype(jnp.bfloat16), old_value, preferred_element_type=jnp.float32
    )
    mix += (own / total).astype(jnp.bfloat16).astype(jnp.float32) * new_value[0].astype(jnp.float32)
    at = lax.broadcasted_iota(jnp.int32, (rows.shape[0], HD), 0) // groups
    picked = mix[:, :HD]
    for j in range(1, heads):
        picked = jnp.where(at == j, mix[:, j * HD : (j + 1) * HD], picked)
    out[0] = picked.astype(jnp.bfloat16)


def step_attend(lengths, query, cache, entries, slots, heads):
    groups = query.shape[1] // heads // HD
    stored = cache.shape[2]
    width = heads * HD
    pad = 16
    parts = query[:slots].reshape(slots, heads * groups, 1, HD)
    own = (
        jnp.arange(heads * groups, dtype=jnp.int32)[:, None] // groups
        == jnp.arange(heads, dtype=jnp.int32)[None, :]
    )
    spread = jnp.where(own[None, :, :, None], parts, jnp.bfloat16(0.0))
    spread = spread.reshape(slots, heads * groups, width)
    spread = jnp.pad(spread, ((0, 0), (0, pad - heads * groups), (0, 0)))
    new_key = entries[0, :slots].reshape(slots, 1, width)
    new_value = entries[1, :slots].reshape(slots, 1, width)
    out = pl.pallas_call(
        functools.partial(step_kernel, heads, groups),
        out_shape=jax.ShapeDtypeStruct((slots, pad, HD), jnp.bfloat16),
        grid_spec=pltpu.PrefetchScalarGridSpec(
            num_scalar_prefetch=1,
            grid=(slots,),
            in_specs=[
                pl.BlockSpec((1, pad, width), lambda s, n: (s, 0, 0)),
                pl.BlockSpec((1, 1, stored, width), lambda s, n: (0, s, 0, 0)),
                pl.BlockSpec((1, 1, stored, width), lambda s, n: (1, s, 0, 0)),
                pl.BlockSpec((1, 1, width), lambda s, n: (s, 0, 0)),
                pl.BlockSpec((1, 1, width), lambda s, n: (s, 0, 0)),
            ],
            out_specs=pl.BlockSpec((1, pad, HD), lambda s, n: (s, 0, 0)),
        ),
        compiler_params=params(32),
        cost_estimate=cost(64 * cache.size, 2 * cache.size, slots * stored * pad),
        name="step_attend",
    )(lengths, spread, cache, cache, new_key, new_value)
    return out[:, : heads * groups].reshape(slots, heads * groups * HD)


def out_kernel(place, mine, sib, weight, sib_weight, out):
    part = jnp.dot(mine[...], weight[...], preferred_element_type=jnp.float32)
    part += jnp.dot(sib[...], sib_weight[...], preferred_element_type=jnp.float32)
    out[...] = part.astype(jnp.bfloat16)


def out_project(place, mine, sib, weight, sib_weight):
    rows, depth = mine.shape
    half = weight.shape[1] // 2
    return pl.pallas_call(
        out_kernel,
        out_shape=jax.ShapeDtypeStruct((rows, half), jnp.bfloat16),
        grid_spec=pltpu.PrefetchScalarGridSpec(
            num_scalar_prefetch=1,
            grid=(1,),
            in_specs=[
                whole((rows, depth)),
                whole((rows, depth)),
                pl.BlockSpec((depth, half), lambda i, s: (0, s[0])),
                whole((depth, half)),
            ],
            out_specs=whole((rows, half)),
        ),
        compiler_params=params(32),
        cost_estimate=cost(4 * rows * depth * half, 4 * depth * half + 6 * rows * half),
        name="out_project",
    )(place, mine, sib, weight, sib_weight)


def forward_kernel(chips, n_dec, place, *refs):
    refs = list(refs)
    mine, sib = refs[:2]
    shares = refs[2 : 2 + 2 * chips]
    refs = refs[2 + 2 * chips :]
    if n_dec:
        dec, dec_shares = refs[0], refs[1 : 1 + 2 * chips]
        refs = refs[1 + 2 * chips :]
    gain, gate, up, down, keep, give, resid = refs[:7]
    refs = refs[7:]
    if n_dec:
        dec_out, dec_resid = refs[:2]
        refs = refs[2:]
    held, inner, total = refs
    piece = mine.shape[0]
    half = shares[0].shape[1]
    core = place[0]
    step = pl.program_id(0)

    @pl.when(step == 0)
    def _():
        jobs = [(mine, shares, core * piece, 0), (sib, shares, (1 - core) * piece, piece)]
        if n_dec:
            jobs.append((dec, dec_shares, 0, 2 * piece))
        for rows, parts, start, put in jobs:
            size = rows.shape[0]
            if not isinstance(start, int):
                start = pl.multiple_of(start, piece)
            for side in range(2):
                at = core if side == 0 else 1 - core
                cols = pl.ds(pl.multiple_of(at * half, half), half)
                added = parts[side][pl.ds(start, size), :].astype(jnp.float32)
                for k in range(1, chips):
                    added += parts[2 * k + side][pl.ds(start, size), :].astype(jnp.float32)
                value = rows[:, cols].astype(jnp.float32) + added
                held[put : put + size, cols] = value.astype(jnp.bfloat16)
            inner[put : put + size, :] = normed(
                held[put : put + size, :].astype(jnp.float32), gain[...]
            )
        resid[...] = held[:piece, :]
        if n_dec:
            dec_resid[...] = held[2 * piece :, :]

    rows = inner[...]
    gated = jnp.dot(rows, gate[...], preferred_element_type=jnp.float32)
    raised = jnp.dot(rows, up[...], preferred_element_type=jnp.float32)
    hidden = (gated / (1.0 + jnp.exp(-gated)) * raised).astype(jnp.bfloat16)
    part = jnp.dot(hidden, down[...], preferred_element_type=jnp.float32)

    @pl.when(step == 0)
    def _():
        total[...] = part

    @pl.when(step > 0)
    def _():
        total[...] += part

    @pl.when(step == pl.num_programs(0) - 1)
    def _():
        keep[...] = total[:piece, :].astype(jnp.bfloat16)
        give[...] = total[piece : 2 * piece, :].astype(jnp.bfloat16)
        if n_dec:
            dec_out[...] = total[2 * piece :, :].astype(jnp.bfloat16)


def feed_forward(place, mine, sib, shares, gain, gate, up, down, dec=None, dec_shares=None):
    piece, width = mine.shape
    chips = len(shares) // 2
    units = gate.shape[1]
    chunk = min(256, units)
    n_dec = 0 if dec is None else dec.shape[0]
    rows = 2 * piece + n_dec
    in_specs = [whole(mine.shape), whole(sib.shape)] + [whole(s.shape) for s in shares]
    args = [mine, sib, *shares]
    if n_dec:
        in_specs += [whole(dec.shape)] + [whole(s.shape) for s in dec_shares]
        args += [dec, *dec_shares]
    in_specs += [
        whole((1, width)),
        pl.BlockSpec((width, chunk), lambda i, s: (0, i)),
        pl.BlockSpec((width, chunk), lambda i, s: (0, i)),
        pl.BlockSpec((chunk, width), lambda i, s: (i, 0)),
    ]
    args += [gain, gate, up, down]
    sizes = [piece] * 3 + [n_dec] * 2 * bool(n_dec)
    return pl.pallas_call(
        functools.partial(forward_kernel, chips, n_dec),
        out_shape=[jax.ShapeDtypeStruct((n, width), jnp.bfloat16) for n in sizes],
        grid_spec=pltpu.PrefetchScalarGridSpec(
            num_scalar_prefetch=1,
            grid=(units // chunk,),
            in_specs=in_specs,
            out_specs=[whole((n, width)) for n in sizes],
            scratch_shapes=[
                pltpu.VMEM((rows, width), jnp.bfloat16),
                pltpu.VMEM((rows, width), jnp.bfloat16),
                pltpu.VMEM((rows, width), jnp.float32),
            ],
        ),
        compiler_params=params(48),
        cost_estimate=cost(6 * rows * width * units, 6 * width * units, rows * units),
        name="feed_forward",
    )(place, *args)


def angle_tables(places):
    halfway = HD // 2
    powers = jnp.arange(halfway, dtype=jnp.float32) * (2.0 / HD)
    inverse = THETA ** (-powers)
    angles = places.astype(jnp.float32)[:, None] * inverse[None, :]
    cosine, sine = jnp.cos(angles), jnp.sin(angles)
    return jnp.concatenate([cosine, cosine], axis=-1), jnp.concatenate([-sine, sine], axis=-1)


def add(*values):
    total = values[0].astype(jnp.float32)
    for value in values[1:]:
        total = total + value.astype(jnp.float32)
    return total.astype(jnp.bfloat16)


def on_device(
    prefill_rows,
    decode_rows,
    deal_order,
    prefill_offset,
    cache_length,
    prefill_cache,
    decode_cache,
    qkv_weight,
    out_weight,
    attention_gain,
    forward_gain,
    gate_weight,
    up_weight,
    down_weight,
):
    tensor_count = lax.axis_size("tensor")
    dp_count = lax.axis_size("dp")
    chips = tensor_count // 2
    tensor_place = lax.axis_index("tensor")
    group_place = lax.axis_index("dp")
    chip, core = tensor_place // 2, tensor_place % 2
    piece, width = prefill_rows.shape
    per_device = decode_rows.shape[0]
    requests = deal_order.shape[0]
    slots = cache_length.shape[0]
    padded = -(-slots // 16) * 16
    heads = qkv_weight.shape[1]
    tokens = piece * tensor_count
    half = width // 2

    def place_of(k):
        return jnp.stack([core, (chip + k) % chips, prefill_offset[0]]).astype(jnp.int32)

    places = [place_of(k) for k in range(chips)]

    mines = [prefill_rows] + [from_chip(prefill_rows, k) for k in range(1, chips)]
    sibs = [swap_cores(rows) for rows in mines]

    pool = decode_rows
    mask = 1
    while mask < dp_count:
        pool = jnp.concatenate([pool, swap_groups(pool, mask)], axis=0)
        mask *= 2
    index = jnp.arange(dp_count * per_device, dtype=jnp.int32)
    origin = jnp.bitwise_xor(group_place, index // per_device)
    request = (origin * tensor_count + tensor_place) * per_device + index % per_device
    slot_of = jnp.sum(
        jnp.where(
            request[:, None] == jnp.arange(requests, dtype=jnp.int32)[None, :],
            deal_order[None, :],
            0,
        ),
        axis=1,
    )
    in_group = slot_of - group_place * slots
    chooser = (jnp.arange(padded, dtype=jnp.int32)[:, None] == in_group[None, :]) & (
        in_group[None, :] < slots
    )
    dealt = jnp.dot(
        chooser.astype(jnp.bfloat16), pool, preferred_element_type=jnp.float32
    ).astype(jnp.bfloat16)
    dealt = add(dealt, swap_cores(dealt))
    dealt = add(dealt, *[from_chip(dealt, k) for k in range(1, chips)])

    weight = qkv_weight.reshape(width, -1)
    gain = attention_gain.reshape(1, width)
    tables = angle_tables(prefill_offset[0] + jnp.arange(tokens, dtype=jnp.int32))
    dec_tables = angle_tables(jnp.pad(cache_length, (0, padded - slots)))
    total = {"heads": heads, "tokens": tokens}
    queries = [None] * chips
    entries = None
    for k in range(chips):
        last = k == chips - 1
        got = project(
            places[k],
            mines[k],
            sibs[k],
            gain,
            weight,
            tables,
            total,
            dealt if last else None,
            dec_tables if last else None,
            entries,
        )
        queries[k], entries = got[:2]
        if last:
            dec_query, dec_entries = got[2:]

    col = pl.multiple_of((1 - core) * half, half)
    sib_weight = swap_cores(lax.dynamic_slice_in_dim(out_weight, col, half, 1))

    def finish(attended, place):
        return out_project(place, attended, swap_cores(attended), out_weight, sib_weight)

    parts = []
    for k in range(chips):
        attended = fill_attend(places[k], queries[k], prefill_cache, entries, heads)
        parts.append(finish(attended, places[k]))
    dec_att = step_attend(cache_length, dec_query, decode_cache, dec_entries, slots, heads)
    dec_att = jnp.pad(dec_att, ((0, padded - slots), (0, 0)))
    dec_part = finish(dec_att, places[0])

    def shares_of(own, others):
        pairs = []
        for value in [own, *others]:
            pairs += [value, swap_cores(value)]
        return pairs

    shares = []
    for b in range(chips):
        others = [from_chip(parts[(b - j) % chips], j) for j in range(1, chips)]
        shares.append(shares_of(parts[b], others))
    dec_shares = shares_of(dec_part, [from_chip(dec_part, j) for j in range(1, chips)])

    gain = forward_gain.reshape(1, width)
    arrived = []
    for n, b in enumerate([*range(1, chips), 0]):
        got = feed_forward(
            places[b],
            mines[b],
            sibs[b],
            shares[b],
            gain,
            gate_weight,
            up_weight,
            down_weight,
            dealt if n == 0 else None,
            dec_shares if n == 0 else None,
        )
        keep, give, resid = got[:3]
        if n == 0:
            dec_sum, dec_resid = got[3:]
        if b:
            arrived.append(from_chip(add(keep, swap_cores(give)), chips - b))
        else:
            prefill_out = add(resid, keep, swap_cores(give), *arrived)

    dec_sum = add(dec_sum, swap_cores(dec_sum))
    others = [from_chip(dec_sum, j) for j in range(1, chips)]
    final = add(dec_resid, dec_sum, *others)
    picker = in_group[:, None] == jnp.arange(padded, dtype=jnp.int32)[None, :]
    picker = picker & (in_group[:, None] < slots)
    routed = jnp.dot(
        picker.astype(jnp.bfloat16), final, preferred_element_type=jnp.float32
    ).astype(jnp.bfloat16)
    mask = dp_count // 2
    while mask:
        cut = mask * per_device
        routed = add(routed[:cut], swap_groups(routed[cut:], mask))
        mask //= 2
    return (prefill_out, routed, entries, dec_entries[:, :slots])


def solution(mesh):
    placed = (
        P(("dp", "tensor"), None),
        P(("dp", "tensor"), None),
        P(),
        P("dp"),
        P("dp"),
        P(None, "dp", None, "tensor"),
        P(None, "dp", None, "tensor"),
        P(None, "tensor", None),
        P("tensor", None),
        P(),
        P(),
        P(None, "tensor"),
        P(None, "tensor"),
        P("tensor", None),
    )
    return jax.shard_map(
        on_device,
        mesh=mesh,
        in_specs=placed,
        out_specs=(
            P(("dp", "tensor"), None),
            P(("dp", "tensor"), None),
            P(None, "dp", "tensor"),
            P(None, "dp", "tensor"),
        ),
        check_vma=False,
    )
```

```python
import functools
import math

import jax
import jax.numpy as jnp
from jax import lax
from jax.experimental import pallas as pl
from jax.experimental.pallas import tpu as pltpu
from jax.sharding import PartitionSpec as P

HD = 128
EPSILON = 1e-06
THETA = 1000000.0
NEGATIVE = -1e30
MIB = 1 << 20


def swap_cores(value):
    count = lax.axis_size("tensor")
    return lax.ppermute(value, "tensor", [(i, i ^ 1) for i in range(count)])


def from_chip(value, step):
    count = lax.axis_size("tensor")
    chips = count // 2
    return lax.ppermute(
        value, "tensor", [(i, (i // 2 - step) % chips * 2 + i % 2) for i in range(count)]
    )


def swap_groups(value, mask):
    count = lax.axis_size("dp")
    return lax.ppermute(value, "dp", [(i, i ^ mask) for i in range(count)])


def whole(shape):
    return pl.BlockSpec(shape, lambda *_: (0,) * len(shape))


def params(mib):
    return pltpu.CompilerParams(vmem_limit_bytes=mib * MIB)


def cost(flops, moved, exps=0):
    return pl.CostEstimate(flops=int(flops), bytes_accessed=int(moved), transcendentals=int(exps))


def normed(values, gain):
    spread = jnp.mean(values * values, axis=-1, keepdims=True)
    return (values * lax.rsqrt(spread + EPSILON) * gain).astype(jnp.bfloat16)


def turn(vectors, cosine, sine):
    return vectors * cosine + pltpu.roll(vectors, HD // 2, 1) * sine


def in_vmem(value):
    return pltpu.with_memory_space_constraint(value, pltpu.VMEM)


def in_hbm(value):
    return pltpu.with_memory_space_constraint(value, pltpu.HBM)


VMEM_WHOLE = pl.BlockSpec(memory_space=pltpu.VMEM)
SMEM_WHOLE = pl.BlockSpec(memory_space=pltpu.SMEM)
UNREAD = pl.BlockSpec(memory_space=pl.ANY)


def project_kernel(n_dec, n_after, groups, heads, place, *refs):
    refs = list(refs)
    mine, sib, gain, weight, cosine, sine = refs[:6]
    refs = refs[6:]
    if n_dec:
        dec, dec_cos, dec_sin = refs[:3]
        refs = refs[3:]
    refs = refs[n_after:]
    query, entries = refs[:2]
    if n_dec:
        dec_query, dec_entries = refs[2:4]
    inner = refs[-1]
    piece = mine.shape[0]
    core = place[0]
    scale = gain[...]
    for ref, at in ((mine, core), (sib, 1 - core)):
        start = pl.multiple_of(at * piece, piece)
        inner[pl.ds(start, piece), :] = normed(ref[...].astype(jnp.float32), scale)
    if n_dec:
        inner[2 * piece :, :] = normed(dec[...].astype(jnp.float32), scale)
    here = pl.ds(pl.multiple_of(place[1] * 2 * piece, 2 * piece), 2 * piece)
    depth = (groups + 2) * HD
    for j in range(heads):
        mixed = jnp.dot(
            inner[...],
            weight[:, j * depth : (j + 1) * depth],
            preferred_element_type=jnp.float32,
        )

        def put(rows, cos, sin, query_out, entry_out):
            for g in range(groups):
                part = rows[:, g * HD : (g + 1) * HD]
                at = (j * groups + g) * HD
                query_out[:, at : at + HD] = turn(part, cos, sin).astype(jnp.bfloat16)
            key = rows[:, groups * HD : (groups + 1) * HD]
            entry_out[0, :, j * HD : (j + 1) * HD] = turn(key, cos, sin).astype(jnp.bfloat16)
            entry_out[1, :, j * HD : (j + 1) * HD] = rows[:, (groups + 1) * HD :].astype(
                jnp.bfloat16
            )

        put(mixed[: 2 * piece], cosine[here, :], sine[here, :], query, entries)
        if n_dec:
            put(mixed[2 * piece :], dec_cos[...], dec_sin[...], dec_query, dec_entries)


def project(place, mine, sib, gain, weight, tables, heads, dec=None, dec_tables=None, after=()):
    piece, width = mine.shape
    depth = weight.shape[1] // heads
    groups = depth // HD - 2
    block = 2 * piece
    n_dec = 0 if dec is None else dec.shape[0]
    args = [mine, sib, gain, weight, *tables]
    if n_dec:
        args += [dec, *dec_tables]
    out_shape = []
    for n in [block] + [n_dec] * bool(n_dec):
        out_shape += [
            jax.ShapeDtypeStruct((n, heads * groups * HD), jnp.bfloat16),
            jax.ShapeDtypeStruct((2, n, heads * HD), jnp.bfloat16),
        ]
    rows = block + n_dec
    return pl.pallas_call(
        functools.partial(project_kernel, n_dec, len(after), groups, heads),
        out_shape=out_shape,
        in_specs=[SMEM_WHOLE] + [VMEM_WHOLE] * len(args) + [UNREAD] * len(after),
        out_specs=[VMEM_WHOLE] * len(out_shape),
        scratch_shapes=[pltpu.VMEM((rows, width), jnp.bfloat16)],
        compiler_params=params(8),
        cost_estimate=cost(2 * rows * weight.size, 2 * (weight.size + 2 * rows * width)),
        name="project",
    )(place, *args, *after)


def fill_kernel(groups, chips, place, query, cache_key, cache_value, *refs):
    new_keys, new_values, out = refs[:chips], refs[chips : 2 * chips], refs[2 * chips]
    scaling = 1.0 / math.sqrt(HD)
    count = query.shape[0]
    stored = cache_key.shape[2]
    old_seen = lax.broadcasted_iota(jnp.int32, (1, stored), 1) < place[2]
    ahead = lax.broadcasted_iota(jnp.int32, (count, count), 1) - lax.broadcasted_iota(
        jnp.int32, (count, count), 0
    )
    across = (((1,), (1,)), ((), ()))
    for g in range(groups):
        rows = query[:, g * HD : (g + 1) * HD]
        scores = lax.dot_general(
            rows, cache_key[0, 0], across, preferred_element_type=jnp.float32
        )
        scores = [jnp.where(old_seen, scores * scaling, NEGATIVE)]
        for k in range(chips):
            fresh = lax.dot_general(
                rows, new_keys[k][0], across, preferred_element_type=jnp.float32
            )
            gap = (place[1] - place[3 + k]) * count
            scores.append(jnp.where(ahead <= gap, fresh * scaling, NEGATIVE))
        top = jnp.max(scores[0], axis=-1, keepdims=True)
        for part in scores[1:]:
            top = jnp.maximum(top, jnp.max(part, axis=-1, keepdims=True))
        mix, total = 0.0, 0.0
        for part, values in zip(scores, [cache_value[0, 0], *[v[0] for v in new_values]]):
            weights = jnp.exp(part - top)
            total += jnp.sum(weights, axis=-1, keepdims=True)
            mix += jnp.dot(
                weights.astype(jnp.bfloat16), values, preferred_element_type=jnp.float32
            )
        out[:, g * HD : (g + 1) * HD] = (mix / total).astype(jnp.bfloat16)


def fill_attend(place, query, cache, entries, heads):
    count = query.shape[0]
    groups = query.shape[1] // heads // HD
    stored = cache.shape[2]
    chips = len(entries)
    pairs = count * groups * heads * (stored + chips * count)
    return pl.pallas_call(
        functools.partial(fill_kernel, groups, chips),
        out_shape=jax.ShapeDtypeStruct(query.shape, jnp.bfloat16),
        grid_spec=pltpu.PrefetchScalarGridSpec(
            num_scalar_prefetch=1,
            grid=(heads,),
            in_specs=[
                pl.BlockSpec((count, groups * HD), lambda j, s: (0, j)),
                pl.BlockSpec((1, 1, stored, HD), lambda j, s: (0, 0, 0, j)),
                pl.BlockSpec((1, 1, stored, HD), lambda j, s: (1, 0, 0, j)),
            ]
            + [pl.BlockSpec((1, count, HD), lambda j, s: (0, 0, j))] * chips
            + [pl.BlockSpec((1, count, HD), lambda j, s: (1, 0, j))] * chips,
            out_specs=pl.BlockSpec((count, groups * HD), lambda j, s: (0, j)),
        ),
        compiler_params=params(12),
        cost_estimate=cost(8 * pairs * HD, 2 * cache.size, pairs),
        name="fill_attend",
    )(place, query, cache, cache, *entries, *entries)


def step_kernel(heads, groups, lengths, query, cache_key, cache_value, new_key, new_value, out):
    scaling = 1.0 / math.sqrt(HD)
    stored = cache_key.shape[2]
    length = lengths[pl.program_id(0)]
    rows = query[0]
    old_key, old_value = cache_key[0, 0], cache_value[0, 0]
    across = (((1,), (1,)), ((), ()))
    old = lax.dot_general(rows, old_key, across, preferred_element_type=jnp.float32)
    seen = lax.broadcasted_iota(jnp.int32, (1, stored), 1) < length
    old = jnp.where(seen, old * scaling, NEGATIVE)
    own = jnp.sum(
        rows.astype(jnp.float32) * new_key[0].astype(jnp.float32), axis=-1, keepdims=True
    )
    own = own * scaling
    top = jnp.maximum(jnp.max(old, axis=-1, keepdims=True), own)
    old = jnp.exp(old - top)
    own = jnp.exp(own - top)
    total = jnp.sum(old, axis=-1, keepdims=True) + own
    mix = jnp.dot(
        (old / total).astype(jnp.bfloat16), old_value, preferred_element_type=jnp.float32
    )
    mix += (own / total).astype(jnp.bfloat16).astype(jnp.float32) * new_value[0].astype(jnp.float32)
    at = lax.broadcasted_iota(jnp.int32, (rows.shape[0], HD), 0) // groups
    picked = mix[:, :HD]
    for j in range(1, heads):
        picked = jnp.where(at == j, mix[:, j * HD : (j + 1) * HD], picked)
    out[0] = picked.astype(jnp.bfloat16)


def step_attend(lengths, query, cache, entries, slots, heads):
    groups = query.shape[1] // heads // HD
    stored = cache.shape[2]
    width = heads * HD
    pad = 16
    parts = query[:slots].reshape(slots, heads * groups, 1, HD)
    own = (
        jnp.arange(heads * groups, dtype=jnp.int32)[:, None] // groups
        == jnp.arange(heads, dtype=jnp.int32)[None, :]
    )
    spread = jnp.where(own[None, :, :, None], parts, jnp.bfloat16(0.0))
    spread = spread.reshape(slots, heads * groups, width)
    spread = jnp.pad(spread, ((0, 0), (0, pad - heads * groups), (0, 0)))
    new_key = entries[0, :slots].reshape(slots, 1, width)
    new_value = entries[1, :slots].reshape(slots, 1, width)
    out = pl.pallas_call(
        functools.partial(step_kernel, heads, groups),
        out_shape=jax.ShapeDtypeStruct((slots, pad, HD), jnp.bfloat16),
        grid_spec=pltpu.PrefetchScalarGridSpec(
            num_scalar_prefetch=1,
            grid=(slots,),
            in_specs=[
                pl.BlockSpec((1, pad, width), lambda s, n: (s, 0, 0)),
                pl.BlockSpec((1, 1, stored, width), lambda s, n: (0, s, 0, 0)),
                pl.BlockSpec((1, 1, stored, width), lambda s, n: (1, s, 0, 0)),
                pl.BlockSpec((1, 1, width), lambda s, n: (s, 0, 0)),
                pl.BlockSpec((1, 1, width), lambda s, n: (s, 0, 0)),
            ],
            out_specs=pl.BlockSpec((1, pad, HD), lambda s, n: (s, 0, 0)),
        ),
        compiler_params=params(8),
        cost_estimate=cost(64 * cache.size, 2 * cache.size, slots * stored * pad),
        name="step_attend",
    )(lengths, spread, cache, cache, new_key, new_value)
    return out[:, : heads * groups].reshape(slots, heads * groups * HD)


def out_kernel(place, mine, sib, weight, sib_weight, out):
    half = out.shape[1]
    cols = pl.ds(pl.multiple_of(place[0] * half, half), half)
    part = jnp.dot(mine[...], weight[:, cols], preferred_element_type=jnp.float32)
    part += jnp.dot(sib[...], sib_weight[...], preferred_element_type=jnp.float32)
    out[...] = part.astype(jnp.bfloat16)


def out_project(place, mine, sib, weight, sib_weight):
    rows, depth = mine.shape
    half = weight.shape[1] // 2
    return pl.pallas_call(
        out_kernel,
        out_shape=jax.ShapeDtypeStruct((rows, half), jnp.bfloat16),
        in_specs=[SMEM_WHOLE] + [VMEM_WHOLE] * 4,
        out_specs=VMEM_WHOLE,
        compiler_params=params(8),
        cost_estimate=cost(4 * rows * depth * half, 4 * depth * half + 6 * rows * half),
        name="out_project",
    )(place, mine, sib, weight, sib_weight)


def forward_kernel(chips, n_dec, n_after, chunk, place, *refs):
    refs = list(refs)
    mine, sib = refs[:2]
    shares = refs[2 : 2 + 2 * chips]
    refs = refs[2 + 2 * chips :]
    if n_dec:
        dec, dec_shares = refs[0], refs[1 : 1 + 2 * chips]
        refs = refs[1 + 2 * chips :]
    gain, gate, up, down = refs[:4]
    refs = refs[4 + n_after :]
    keep, give, resid = refs[:3]
    refs = refs[3:]
    if n_dec:
        dec_out, dec_resid = refs[:2]
        refs = refs[2:]
    held, inner, hidden = refs
    piece = mine.shape[0]
    half = shares[0].shape[1]
    core = place[0]
    jobs = [(mine, shares, core * piece, 0), (sib, shares, (1 - core) * piece, piece)]
    if n_dec:
        jobs.append((dec, dec_shares, 0, 2 * piece))
    for rows, parts, start, put in jobs:
        size = rows.shape[0]
        if not isinstance(start, int):
            start = pl.multiple_of(start, piece)
        for side in range(2):
            at = core if side == 0 else 1 - core
            cols = pl.ds(pl.multiple_of(at * half, half), half)
            added = parts[side][pl.ds(start, size), :].astype(jnp.float32)
            for k in range(1, chips):
                added += parts[2 * k + side][pl.ds(start, size), :].astype(jnp.float32)
            value = rows[:, cols].astype(jnp.float32) + added
            held[put : put + size, cols] = value.astype(jnp.bfloat16)
        inner[put : put + size, :] = normed(held[put : put + size, :].astype(jnp.float32), gain[...])
    resid[...] = held[:piece, :]
    if n_dec:
        dec_resid[...] = held[2 * piece :, :]

    @pl.loop(0, gate.shape[1] // chunk)
    def _(i):
        at = pl.ds(pl.multiple_of(i * chunk, chunk), chunk)
        gated = jnp.dot(inner[...], gate[:, at], preferred_element_type=jnp.float32)
        raised = jnp.dot(inner[...], up[:, at], preferred_element_type=jnp.float32)
        hidden[:, at] = (gated / (1.0 + jnp.exp(-gated)) * raised).astype(jnp.bfloat16)

    @pl.loop(0, down.shape[1] // chunk)
    def _(i):
        at = pl.ds(pl.multiple_of(i * chunk, chunk), chunk)
        part = jnp.dot(hidden[...], down[:, at], preferred_element_type=jnp.float32)
        part = part.astype(jnp.bfloat16)
        keep[:, at] = part[:piece]
        give[:, at] = part[piece : 2 * piece]
        if n_dec:
            dec_out[:, at] = part[2 * piece :]


def feed_forward(
    place, mine, sib, shares, gain, gate, up, down, dec=None, dec_shares=None, after=()
):
    piece, width = mine.shape
    chips = len(shares) // 2
    units = gate.shape[1]
    chunk = min(512, units)
    n_dec = 0 if dec is None else dec.shape[0]
    rows = 2 * piece + n_dec
    args = [mine, sib, *shares]
    if n_dec:
        args += [dec, *dec_shares]
    args += [gain, gate, up, down]
    sizes = [piece] * 3 + [n_dec] * 2 * bool(n_dec)
    return pl.pallas_call(
        functools.partial(forward_kernel, chips, n_dec, len(after), chunk),
        out_shape=[jax.ShapeDtypeStruct((n, width), jnp.bfloat16) for n in sizes],
        in_specs=[SMEM_WHOLE] + [VMEM_WHOLE] * len(args) + [UNREAD] * len(after),
        out_specs=[VMEM_WHOLE] * len(sizes),
        scratch_shapes=[
            pltpu.VMEM((rows, width), jnp.bfloat16),
            pltpu.VMEM((rows, width), jnp.bfloat16),
            pltpu.VMEM((rows, units), jnp.bfloat16),
        ],
        compiler_params=params(10),
        cost_estimate=cost(6 * rows * width * units, 6 * width * units, rows * units),
        name="feed_forward",
    )(place, *args, *after)


def angle_tables(places):
    halfway = HD // 2
    powers = jnp.arange(halfway, dtype=jnp.float32) * (2.0 / HD)
    inverse = THETA ** (-powers)
    angles = places.astype(jnp.float32)[:, None] * inverse[None, :]
    cosine, sine = jnp.cos(angles), jnp.sin(angles)
    return jnp.concatenate([cosine, cosine], axis=-1), jnp.concatenate([-sine, sine], axis=-1)


def add(*values):
    total = values[0].astype(jnp.float32)
    for value in values[1:]:
        total = total + value.astype(jnp.float32)
    return total.astype(jnp.bfloat16)


def on_device(
    prefill_rows,
    decode_rows,
    deal_order,
    prefill_offset,
    cache_length,
    prefill_cache,
    decode_cache,
    qkv_weight,
    out_weight,
    attention_gain,
    forward_gain,
    gate_weight,
    up_weight,
    down_weight,
):
    tensor_count = lax.axis_size("tensor")
    dp_count = lax.axis_size("dp")
    chips = tensor_count // 2
    tensor_place = lax.axis_index("tensor")
    group_place = lax.axis_index("dp")
    chip, core = tensor_place // 2, tensor_place % 2
    piece, width = prefill_rows.shape
    per_device = decode_rows.shape[0]
    requests = deal_order.shape[0]
    slots = cache_length.shape[0]
    padded = -(-slots // 16) * 16
    heads = qkv_weight.shape[1]
    tokens = piece * tensor_count
    half = width // 2

    def place_of(k):
        spots = [core, (chip + k) % chips, prefill_offset[0]]
        return jnp.stack(spots + [(chip + j) % chips for j in range(chips)]).astype(jnp.int32)

    places = [place_of(k) for k in range(chips)]
    weight = in_vmem(qkv_weight.reshape(width, -1))
    gate_weight, up_weight, down_weight = map(in_vmem, (gate_weight, up_weight, down_weight))
    prefill_cache, decode_cache = in_hbm(prefill_cache), in_hbm(decode_cache)

    mines = [prefill_rows] + [from_chip(prefill_rows, k) for k in range(1, chips)]
    sibs = [swap_cores(rows) for rows in mines]

    low = max(dp_count // 4, 1)
    pool = [decode_rows] + [swap_groups(decode_rows, i) for i in range(1, low)]
    pool = jnp.concatenate(pool, axis=0)
    pool = [pool] + [swap_groups(pool, i * low) for i in range(1, dp_count // low)]
    pool = jnp.concatenate(pool, axis=0)
    index = jnp.arange(dp_count * per_device, dtype=jnp.int32)
    origin = jnp.bitwise_xor(group_place, index // per_device)
    request = (origin * tensor_count + tensor_place) * per_device + index % per_device
    slot_of = jnp.sum(
        jnp.where(
            request[:, None] == jnp.arange(requests, dtype=jnp.int32)[None, :],
            deal_order[None, :],
            0,
        ),
        axis=1,
    )
    in_group = slot_of - group_place * slots
    chooser = (jnp.arange(padded, dtype=jnp.int32)[:, None] == in_group[None, :]) & (
        in_group[None, :] < slots
    )
    dealt = jnp.dot(
        chooser.astype(jnp.bfloat16), pool, preferred_element_type=jnp.float32
    ).astype(jnp.bfloat16)

    gain = attention_gain.reshape(1, width)
    tables = angle_tables(prefill_offset[0] + jnp.arange(tokens, dtype=jnp.int32))
    dec_tables = angle_tables(jnp.pad(cache_length, (0, padded - slots)))
    queries, entries = [None] * chips, [None] * chips
    for k in range(chips):
        last = k == chips - 1
        if last:
            dealt = add(dealt, swap_cores(dealt))
            dealt, queries[0] = lax.optimization_barrier((dealt, queries[0]))
            dealt = add(dealt, *[from_chip(dealt, j) for j in range(1, chips)])
        got = project(
            places[k],
            mines[k],
            sibs[k],
            gain,
            weight,
            tables,
            heads,
            dealt if last else None,
            dec_tables if last else None,
            [dealt] if k == 0 else [],
        )
        queries[k], entries[k] = got[:2]
        if last:
            dec_query, dec_entries = got[2:]

    col = pl.multiple_of((1 - core) * half, half)
    sib_weight = in_vmem(swap_cores(lax.dynamic_slice_in_dim(out_weight, col, half, 1)))
    out_weight = in_vmem(out_weight)

    def finish(attended, place):
        return out_project(place, attended, swap_cores(attended), out_weight, sib_weight)

    parts = []
    for k in range(chips):
        attended = fill_attend(places[k], queries[k], prefill_cache, entries, heads)
        parts.append(finish(attended, places[k]))
    dec_att = step_attend(cache_length, dec_query, decode_cache, dec_entries, slots, heads)
    dec_att = jnp.pad(dec_att, ((0, padded - slots), (0, 0)))
    dec_part = finish(dec_att, places[0])

    def shares_of(own, others):
        pairs = []
        for value in [own, *others]:
            pairs += [value, swap_cores(value)]
        return pairs

    dec_shares = shares_of(dec_part, [from_chip(dec_part, j) for j in range(1, chips)])
    gain = forward_gain.reshape(1, width)
    order = [*range(1, chips), 0]

    def fetch(b):
        return [from_chip(parts[(b - j) % chips], j) for j in range(1, chips)]

    theirs = fetch(order[0])
    arrived = []
    for n, b in enumerate(order):
        got = feed_forward(
            places[b],
            mines[b],
            sibs[b],
            shares_of(parts[b], theirs),
            gain,
            gate_weight,
            up_weight,
            down_weight,
            dealt if n == 0 else None,
            dec_shares if n == 0 else None,
            [routed] if n + 1 == chips else [],
        )
        keep, give, resid = got[:3]
        if n + 1 < chips:
            theirs = fetch(order[n + 1])
            arrived.append(from_chip(add(keep, swap_cores(give)), chips - b))
        if n == 0:
            dec_sum, dec_resid = got[3:]
            dec_sum = add(dec_sum, swap_cores(dec_sum))
            dec_sum, theirs = lax.optimization_barrier((dec_sum, theirs))
            final = add(dec_resid, dec_sum, *[from_chip(dec_sum, j) for j in range(1, chips)])
            picker = in_group[:, None] == jnp.arange(padded, dtype=jnp.int32)[None, :]
            picker = picker & (in_group[:, None] < slots)
            routed = jnp.dot(
                picker.astype(jnp.bfloat16), final, preferred_element_type=jnp.float32
            ).astype(jnp.bfloat16)
    give = jnp.concatenate([swap_cores(part) for part in jnp.split(give, 2, axis=1)], axis=1)
    prefill_out = add(resid, keep, give, *arrived)

    low = max(dp_count // 4, 1)
    pairs = routed.reshape(dp_count // low, low * per_device, width)
    rows = add(
        pairs[0], *[swap_groups(pairs[i], i * low) for i in range(1, dp_count // low)]
    )
    pairs = rows.reshape(low, per_device, width)
    routed = add(pairs[0], *[swap_groups(pairs[i], i) for i in range(1, low)])

    around = jnp.concatenate(entries + entries[:-1], axis=1)
    prefill_entries = lax.dynamic_slice_in_dim(
        around, (chips - chip) % chips * 2 * piece, tokens, 1
    )
    return (prefill_out, routed, prefill_entries, dec_entries[:, :slots])


def solution(mesh):
    placed = (
        P(("dp", "tensor"), None),
        P(("dp", "tensor"), None),
        P(),
        P("dp"),
        P("dp"),
        P(None, "dp", None, "tensor"),
        P(None, "dp", None, "tensor"),
        P(None, "tensor", None),
        P("tensor", None),
        P(),
        P(),
        P(None, "tensor"),
        P(None, "tensor"),
        P("tensor", None),
    )
    return jax.shard_map(
        on_device,
        mesh=mesh,
        in_specs=placed,
        out_specs=(
            P(("dp", "tensor"), None),
            P(("dp", "tensor"), None),
            P(None, "dp", "tensor"),
            P(None, "dp", "tensor"),
        ),
        check_vma=False,
    )
```

```python
import functools
import math

import jax
import jax.numpy as jnp
from jax import lax
from jax.experimental import pallas as pl
from jax.experimental.pallas import tpu as pltpu
from jax.sharding import PartitionSpec as P

HD = 128
EPSILON = 1e-06
THETA = 1000000.0
NEGATIVE = -1e30
MIB = 1 << 20


def swap_cores(value):
    count = lax.axis_size("tensor")
    return lax.ppermute(value, "tensor", [(i, i ^ 1) for i in range(count)])


def from_chip(value, step):
    count = lax.axis_size("tensor")
    chips = count // 2
    return lax.ppermute(
        value, "tensor", [(i, (i // 2 - step) % chips * 2 + i % 2) for i in range(count)]
    )


def from_other(value, step):
    count = lax.axis_size("tensor")
    return lax.ppermute(
        value, "tensor", [(i, (i // 2 - step) % (count // 2) * 2 + 1 - i % 2) for i in range(count)]
    )


def swap_groups(value, mask):
    count = lax.axis_size("dp")
    return lax.ppermute(value, "dp", [(i, i ^ mask) for i in range(count)])


def whole(shape):
    return pl.BlockSpec(shape, lambda *_: (0,) * len(shape))


def params(mib):
    return pltpu.CompilerParams(vmem_limit_bytes=mib * MIB)


def cost(flops, moved, exps=0):
    return pl.CostEstimate(flops=int(flops), bytes_accessed=int(moved), transcendentals=int(exps))


def normed(values, gain):
    spread = jnp.mean(values * values, axis=-1, keepdims=True)
    return (values * lax.rsqrt(spread + EPSILON) * gain).astype(jnp.bfloat16)


def turn(vectors, cosine, sine):
    return vectors * cosine + pltpu.roll(vectors, HD // 2, 1) * sine


def in_vmem(value):
    return pltpu.with_memory_space_constraint(value, pltpu.VMEM)


def in_hbm(value):
    return pltpu.with_memory_space_constraint(value, pltpu.HBM)


VMEM_WHOLE = pl.BlockSpec(memory_space=pltpu.VMEM)
SMEM_WHOLE = pl.BlockSpec(memory_space=pltpu.SMEM)
IN_PLACE = pl.BlockSpec(memory_space=pl.ANY)


def project_kernel(n_dec, n_after, groups, heads, place, *refs):
    refs = list(refs)
    mine, sib, gain, weight, cosine, sine = refs[:6]
    refs = refs[6:]
    if n_dec:
        dec, dec_cos, dec_sin = refs[:3]
        refs = refs[3:]
    refs = refs[n_after:]
    query, entries = refs[:2]
    if n_dec:
        dec_query, dec_entries = refs[2:4]
    inner = refs[-1]
    piece = mine.shape[0]
    core = place[0]
    scale = gain[...]
    for ref, at in ((mine, core), (sib, 1 - core)):
        start = pl.multiple_of(at * piece, piece)
        inner[pl.ds(start, piece), :] = normed(ref[...].astype(jnp.float32), scale)
    if n_dec:
        inner[2 * piece :, :] = normed(dec[...].astype(jnp.float32), scale)
    here = pl.ds(pl.multiple_of(place[1] * 2 * piece, 2 * piece), 2 * piece)
    depth = (groups + 2) * HD
    for j in range(heads):
        mixed = jnp.dot(
            inner[...],
            weight[:, j * depth : (j + 1) * depth],
            preferred_element_type=jnp.float32,
        )

        def put(rows, cos, sin, query_out, entry_out):
            for g in range(groups):
                part = rows[:, g * HD : (g + 1) * HD]
                at = (j * groups + g) * HD
                query_out[:, at : at + HD] = turn(part, cos, sin).astype(jnp.bfloat16)
            key = rows[:, groups * HD : (groups + 1) * HD]
            entry_out[0, :, j * HD : (j + 1) * HD] = turn(key, cos, sin).astype(jnp.bfloat16)
            entry_out[1, :, j * HD : (j + 1) * HD] = rows[:, (groups + 1) * HD :].astype(
                jnp.bfloat16
            )

        put(mixed[: 2 * piece], cosine[here, :], sine[here, :], query, entries)
        if n_dec:
            put(mixed[2 * piece :], dec_cos[...], dec_sin[...], dec_query, dec_entries)


def project(place, mine, sib, gain, weight, tables, heads, dec=None, dec_tables=None, after=()):
    piece, width = mine.shape
    depth = weight.shape[1] // heads
    groups = depth // HD - 2
    block = 2 * piece
    n_dec = 0 if dec is None else dec.shape[0]
    args = [mine, sib, gain, weight, *tables]
    if n_dec:
        args += [dec, *dec_tables]
    out_shape = []
    for n in [block] + [n_dec] * bool(n_dec):
        out_shape += [
            jax.ShapeDtypeStruct((n, heads * groups * HD), jnp.bfloat16),
            jax.ShapeDtypeStruct((2, n, heads * HD), jnp.bfloat16),
        ]
    rows = block + n_dec
    return pl.pallas_call(
        functools.partial(project_kernel, n_dec, len(after), groups, heads),
        out_shape=out_shape,
        in_specs=[SMEM_WHOLE] + [VMEM_WHOLE] * len(args) + [IN_PLACE] * len(after),
        out_specs=[VMEM_WHOLE] * len(out_shape),
        scratch_shapes=[pltpu.VMEM((rows, width), jnp.bfloat16)],
        compiler_params=params(8),
        cost_estimate=cost(2 * rows * weight.size, 2 * (weight.size + 2 * rows * width)),
        name="project",
    )(place, *args, *after)


def fill_kernel(groups, chips, place, query, cache_key, cache_value, *refs):
    new_keys, new_values, out = refs[:chips], refs[chips : 2 * chips], refs[2 * chips]
    scaling = 1.0 / math.sqrt(HD)
    count = query.shape[0]
    stored = cache_key.shape[2]
    old_seen = lax.broadcasted_iota(jnp.int32, (1, stored), 1) < place[2]
    ahead = lax.broadcasted_iota(jnp.int32, (count, count), 1) - lax.broadcasted_iota(
        jnp.int32, (count, count), 0
    )
    across = (((1,), (1,)), ((), ()))
    for g in range(groups):
        rows = query[:, g * HD : (g + 1) * HD]
        scores = lax.dot_general(
            rows, cache_key[0, 0], across, preferred_element_type=jnp.float32
        )
        scores = [jnp.where(old_seen, scores * scaling, NEGATIVE)]
        for k in range(chips):
            fresh = lax.dot_general(
                rows, new_keys[k][0], across, preferred_element_type=jnp.float32
            )
            gap = (place[1] - place[3 + k]) * count
            scores.append(jnp.where(ahead <= gap, fresh * scaling, NEGATIVE))
        top = jnp.max(scores[0], axis=-1, keepdims=True)
        for part in scores[1:]:
            top = jnp.maximum(top, jnp.max(part, axis=-1, keepdims=True))
        mix, total = 0.0, 0.0
        for part, values in zip(scores, [cache_value[0, 0], *[v[0] for v in new_values]]):
            weights = jnp.exp(part - top)
            total += jnp.sum(weights, axis=-1, keepdims=True)
            mix += jnp.dot(
                weights.astype(jnp.bfloat16), values, preferred_element_type=jnp.float32
            )
        out[:, g * HD : (g + 1) * HD] = (mix / total).astype(jnp.bfloat16)


def fill_attend(place, query, cache, entries, heads):
    count = query.shape[0]
    groups = query.shape[1] // heads // HD
    stored = cache.shape[2]
    chips = len(entries)
    pairs = count * groups * heads * (stored + chips * count)
    return pl.pallas_call(
        functools.partial(fill_kernel, groups, chips),
        out_shape=jax.ShapeDtypeStruct(query.shape, jnp.bfloat16),
        grid_spec=pltpu.PrefetchScalarGridSpec(
            num_scalar_prefetch=1,
            grid=(heads,),
            in_specs=[
                pl.BlockSpec((count, groups * HD), lambda j, s: (0, j)),
                pl.BlockSpec((1, 1, stored, HD), lambda j, s: (0, 0, 0, j)),
                pl.BlockSpec((1, 1, stored, HD), lambda j, s: (1, 0, 0, j)),
            ]
            + [pl.BlockSpec((1, count, HD), lambda j, s: (0, 0, j))] * chips
            + [pl.BlockSpec((1, count, HD), lambda j, s: (1, 0, j))] * chips,
            out_specs=pl.BlockSpec((count, groups * HD), lambda j, s: (0, j)),
        ),
        compiler_params=params(12),
        cost_estimate=cost(8 * pairs * HD, 2 * cache.size, pairs),
        name="fill_attend",
    )(place, query, cache, cache, *entries, *entries)


def step_kernel(heads, groups, lengths, query, cache, new_key, new_value, out, held, arrived):
    scaling = 1.0 / math.sqrt(HD)
    slots, stored = cache.shape[1], cache.shape[2]
    copies = [
        [pltpu.make_async_copy(cache.at[w, s], held.at[w, s], arrived.at[w, s]) for w in range(2)]
        for s in range(slots)
    ]
    for pair in copies:
        for copy in pair:
            copy.start()
    across = (((1,), (1,)), ((), ()))
    places = lax.broadcasted_iota(jnp.int32, (1, stored), 1)
    for s in range(slots):
        rows = query[s]
        copies[s][0].wait()
        old = lax.dot_general(rows, held[0, s], across, preferred_element_type=jnp.float32)
        old = jnp.where(places < lengths[s], old * scaling, NEGATIVE)
        own = jnp.sum(
            rows.astype(jnp.float32) * new_key[s].astype(jnp.float32), axis=-1, keepdims=True
        )
        own = own * scaling
        top = jnp.maximum(jnp.max(old, axis=-1, keepdims=True), own)
        old = jnp.exp(old - top)
        own = jnp.exp(own - top)
        total = jnp.sum(old, axis=-1, keepdims=True) + own
        copies[s][1].wait()
        mix = jnp.dot(
            (old / total).astype(jnp.bfloat16), held[1, s], preferred_element_type=jnp.float32
        )
        own = (own / total).astype(jnp.bfloat16).astype(jnp.float32)
        mix += own * new_value[s].astype(jnp.float32)
        at = lax.broadcasted_iota(jnp.int32, (rows.shape[0], HD), 0) // groups
        picked = mix[:, :HD]
        for j in range(1, heads):
            picked = jnp.where(at == j, mix[:, j * HD : (j + 1) * HD], picked)
        out[s] = picked.astype(jnp.bfloat16)


def step_attend(lengths, query, cache, entries, slots, heads):
    groups = query.shape[1] // heads // HD
    stored = cache.shape[2]
    width = heads * HD
    pad = 16
    parts = query[:slots].reshape(slots, heads * groups, 1, HD)
    own = (
        jnp.arange(heads * groups, dtype=jnp.int32)[:, None] // groups
        == jnp.arange(heads, dtype=jnp.int32)[None, :]
    )
    spread = jnp.where(own[None, :, :, None], parts, jnp.bfloat16(0.0))
    spread = spread.reshape(slots, heads * groups, width)
    spread = jnp.pad(spread, ((0, 0), (0, pad - heads * groups), (0, 0)))
    new_key = entries[0, :slots].reshape(slots, 1, width)
    new_value = entries[1, :slots].reshape(slots, 1, width)
    out = pl.pallas_call(
        functools.partial(step_kernel, heads, groups),
        out_shape=jax.ShapeDtypeStruct((slots, pad, HD), jnp.bfloat16),
        in_specs=[SMEM_WHOLE, VMEM_WHOLE, IN_PLACE, VMEM_WHOLE, VMEM_WHOLE],
        out_specs=VMEM_WHOLE,
        scratch_shapes=[
            pltpu.VMEM(cache.shape, jnp.bfloat16),
            pltpu.SemaphoreType.DMA((2, slots)),
        ],
        compiler_params=params(16),
        cost_estimate=cost(64 * cache.size, 2 * cache.size, slots * stored * pad),
        name="step_attend",
    )(lengths, spread, cache, new_key, new_value)
    return out[:, : heads * groups].reshape(slots, heads * groups * HD)


def out_kernel(place, mine, sib, weight, sib_weight, out):
    half = out.shape[1]
    cols = pl.ds(pl.multiple_of(place[0] * half, half), half)
    part = jnp.dot(mine[...], weight[:, cols], preferred_element_type=jnp.float32)
    part += jnp.dot(sib[...], sib_weight[:, cols], preferred_element_type=jnp.float32)
    out[...] = part.astype(jnp.bfloat16)


def out_project(place, mine, sib, weight, sib_weight):
    rows, depth = mine.shape
    half = weight.shape[1] // 2
    return pl.pallas_call(
        out_kernel,
        out_shape=jax.ShapeDtypeStruct((rows, half), jnp.bfloat16),
        in_specs=[SMEM_WHOLE] + [VMEM_WHOLE] * 4,
        out_specs=VMEM_WHOLE,
        compiler_params=params(8),
        cost_estimate=cost(4 * rows * depth * half, 4 * depth * half + 6 * rows * half),
        name="out_project",
    )(place, mine, sib, weight, sib_weight)


def forward_kernel(chips, n_dec, n_after, chunk, place, *refs):
    refs = list(refs)
    mine, sib = refs[:2]
    shares = refs[2 : 2 + 2 * chips]
    refs = refs[2 + 2 * chips :]
    if n_dec:
        dec, dec_shares = refs[0], refs[1 : 1 + 2 * chips]
        refs = refs[1 + 2 * chips :]
    gain, *weights = refs[:4]
    refs = refs[4 + n_after :]
    keep, give, resid = refs[:3]
    refs = refs[3:]
    if n_dec:
        dec_out, dec_resid = refs[:2]
        refs = refs[2:]
    held, inner, hidden, gate, up, down, arrived = refs
    chunks = gate.shape[0]
    copies = [
        [
            pltpu.make_async_copy(
                source.at[:, pl.ds(i * chunk, chunk)], target.at[i], arrived.at[w, i]
            )
            for i in range(chunks)
        ]
        for w, (source, target) in enumerate(zip(weights, (gate, up, down)))
    ]
    for i in range(chunks):
        copies[0][i].start()
        copies[1][i].start()
    for i in range(chunks):
        copies[2][i].start()
    piece = mine.shape[0]
    half = shares[0].shape[1]
    core = place[0]
    jobs = [(mine, shares, core * piece, 0), (sib, shares, (1 - core) * piece, piece)]
    if n_dec:
        jobs.append((dec, dec_shares, 0, 2 * piece))
    for rows, parts, start, put in jobs:
        size = rows.shape[0]
        if not isinstance(start, int):
            start = pl.multiple_of(start, piece)
        for side in range(2):
            at = core if side == 0 else 1 - core
            cols = pl.ds(pl.multiple_of(at * half, half), half)
            added = parts[side][pl.ds(start, size), :].astype(jnp.float32)
            for k in range(1, chips):
                added += parts[2 * k + side][pl.ds(start, size), :].astype(jnp.float32)
            value = rows[:, cols].astype(jnp.float32) + added
            held[put : put + size, cols] = value.astype(jnp.bfloat16)
        inner[put : put + size, :] = normed(held[put : put + size, :].astype(jnp.float32), gain[...])
    resid[...] = held[:piece, :]
    if n_dec:
        dec_resid[...] = held[2 * piece :, :]

    for i in range(chunks):
        at = slice(i * chunk, (i + 1) * chunk)
        copies[0][i].wait()
        gated = jnp.dot(inner[...], gate[i], preferred_element_type=jnp.float32)
        copies[1][i].wait()
        raised = jnp.dot(inner[...], up[i], preferred_element_type=jnp.float32)
        hidden[:, at] = (gated / (1.0 + jnp.exp(-gated)) * raised).astype(jnp.bfloat16)
    for i in range(chunks):
        at = slice(i * chunk, (i + 1) * chunk)
        copies[2][i].wait()
        part = jnp.dot(hidden[...], down[i], preferred_element_type=jnp.float32)
        part = part.astype(jnp.bfloat16)
        keep[:, at] = part[:piece]
        give[:, at] = part[piece : 2 * piece]
        if n_dec:
            dec_out[:, at] = part[2 * piece :]


def feed_forward(
    place, mine, sib, shares, gain, gate, up, down, dec=None, dec_shares=None, after=()
):
    piece, width = mine.shape
    chips = len(shares) // 2
    units = gate.shape[1]
    chunks = 4
    chunk = width // chunks
    n_dec = 0 if dec is None else dec.shape[0]
    rows = 2 * piece + n_dec
    args = [mine, sib, *shares]
    if n_dec:
        args += [dec, *dec_shares]
    n_whole = len(args) + 1
    args += [gain, gate, up, down]
    sizes = [piece] * 3 + [n_dec] * 2 * bool(n_dec)
    return pl.pallas_call(
        functools.partial(forward_kernel, chips, n_dec, len(after), chunk),
        out_shape=[jax.ShapeDtypeStruct((n, width), jnp.bfloat16) for n in sizes],
        in_specs=[SMEM_WHOLE] + [VMEM_WHOLE] * n_whole + [IN_PLACE] * (3 + len(after)),
        out_specs=[VMEM_WHOLE] * len(sizes),
        scratch_shapes=[
            pltpu.VMEM((rows, width), jnp.bfloat16),
            pltpu.VMEM((rows, width), jnp.bfloat16),
            pltpu.VMEM((rows, units), jnp.bfloat16),
            pltpu.VMEM((units // chunk, width, chunk), jnp.bfloat16),
            pltpu.VMEM((units // chunk, width, chunk), jnp.bfloat16),
            pltpu.VMEM((chunks, units, chunk), jnp.bfloat16),
            pltpu.SemaphoreType.DMA((3, chunks)),
        ],
        compiler_params=params(40),
        cost_estimate=cost(6 * rows * width * units, 6 * width * units, rows * units),
        name="feed_forward",
    )(place, *args, *after)


def angle_tables(places):
    halfway = HD // 2
    powers = jnp.arange(halfway, dtype=jnp.float32) * (2.0 / HD)
    inverse = THETA ** (-powers)
    angles = places.astype(jnp.float32)[:, None] * inverse[None, :]
    cosine, sine = jnp.cos(angles), jnp.sin(angles)
    return jnp.concatenate([cosine, cosine], axis=-1), jnp.concatenate([-sine, sine], axis=-1)


def add(*values):
    total = values[0].astype(jnp.float32)
    for value in values[1:]:
        total = total + value.astype(jnp.float32)
    return total.astype(jnp.bfloat16)


def on_device(
    prefill_rows,
    decode_rows,
    deal_order,
    prefill_offset,
    cache_length,
    prefill_cache,
    decode_cache,
    qkv_weight,
    out_weight,
    attention_gain,
    forward_gain,
    gate_weight,
    up_weight,
    down_weight,
):
    tensor_count = lax.axis_size("tensor")
    dp_count = lax.axis_size("dp")
    chips = tensor_count // 2
    tensor_place = lax.axis_index("tensor")
    group_place = lax.axis_index("dp")
    chip, core = tensor_place // 2, tensor_place % 2
    piece, width = prefill_rows.shape
    per_device = decode_rows.shape[0]
    requests = deal_order.shape[0]
    slots = cache_length.shape[0]
    padded = -(-slots // 16) * 16
    heads = qkv_weight.shape[1]
    tokens = piece * tensor_count

    def place_of(k):
        spots = [core, (chip + k) % chips, prefill_offset[0]]
        return jnp.stack(spots + [(chip + j) % chips for j in range(chips)]).astype(jnp.int32)

    places = [place_of(k) for k in range(chips)]
    weight = in_vmem(qkv_weight.reshape(width, -1))
    gate_weight, up_weight, down_weight = map(in_hbm, (gate_weight, up_weight, down_weight))
    prefill_cache, decode_cache = in_hbm(prefill_cache), in_hbm(decode_cache)

    mines = [prefill_rows] + [from_chip(prefill_rows, k) for k in range(1, chips)]
    sibs = [swap_cores(rows) for rows in mines]

    low = max(dp_count // 4, 1)
    pool = [decode_rows] + [swap_groups(decode_rows, i) for i in range(1, low)]
    pool = jnp.concatenate(pool, axis=0)
    pool = [pool] + [swap_groups(pool, i * low) for i in range(1, dp_count // low)]
    pool = jnp.concatenate(pool, axis=0)
    index = jnp.arange(dp_count * per_device, dtype=jnp.int32)
    origin = jnp.bitwise_xor(group_place, index // per_device)
    request = (origin * tensor_count + tensor_place) * per_device + index % per_device
    slot_of = jnp.sum(
        jnp.where(
            request[:, None] == jnp.arange(requests, dtype=jnp.int32)[None, :],
            deal_order[None, :],
            0,
        ),
        axis=1,
    )
    in_group = slot_of - group_place * slots
    chooser = (jnp.arange(padded, dtype=jnp.int32)[:, None] == in_group[None, :]) & (
        in_group[None, :] < slots
    )
    dealt = jnp.dot(
        chooser.astype(jnp.bfloat16), pool, preferred_element_type=jnp.float32
    ).astype(jnp.bfloat16)

    gain = attention_gain.reshape(1, width)
    tables = angle_tables(prefill_offset[0] + jnp.arange(tokens, dtype=jnp.int32))
    dec_tables = angle_tables(jnp.pad(cache_length, (0, padded - slots)))
    queries, entries = [None] * chips, [None] * chips
    for k in range(chips):
        last = k == chips - 1
        if last:
            others = [from_chip(dealt, j) for j in range(1, chips)]
            others += [from_other(dealt, j) for j in range(chips)]
            dealt = add(dealt, *others)
        got = project(
            places[k],
            mines[k],
            sibs[k],
            gain,
            weight,
            tables,
            heads,
            dealt if last else None,
            dec_tables if last else None,
            [dealt] if k == 0 else [],
        )
        queries[k], entries[k] = got[:2]
        if last:
            dec_query, dec_entries = got[2:]

    sib_weight = in_vmem(swap_cores(out_weight))
    out_weight = in_vmem(out_weight)

    def finish(attended, place):
        return out_project(place, attended, swap_cores(attended), out_weight, sib_weight)

    parts = []
    for k in range(chips):
        attended = fill_attend(places[k], queries[k], prefill_cache, entries, heads)
        parts.append(finish(attended, places[k]))
    dec_att = step_attend(cache_length, dec_query, decode_cache, dec_entries, slots, heads)
    dec_att = jnp.pad(dec_att, ((0, padded - slots), (0, 0)))
    dec_part = finish(dec_att, places[0])

    def shares_of(own, others):
        pairs = []
        for value in [own, *others]:
            pairs += [value, swap_cores(value)]
        return pairs

    dec_shares = shares_of(dec_part, [from_chip(dec_part, j) for j in range(1, chips)])
    gain = forward_gain.reshape(1, width)
    order = [*range(1, chips), 0]

    def fetch(b):
        return [from_chip(parts[(b - j) % chips], j) for j in range(1, chips)]

    theirs = fetch(order[0])
    arrived = []
    for n, b in enumerate(order):
        got = feed_forward(
            places[b],
            mines[b],
            sibs[b],
            shares_of(parts[b], theirs),
            gain,
            gate_weight,
            up_weight,
            down_weight,
            dealt if n == 0 else None,
            dec_shares if n == 0 else None,
            [routed] if n + 1 == chips else [],
        )
        keep, give, resid = got[:3]
        if n + 1 < chips:
            theirs = fetch(order[n + 1])
            arrived.append(from_chip(add(keep, swap_cores(give)), chips - b))
        if n == 0:
            dec_sum, dec_resid = got[3:]
            dec_sum = add(dec_sum, swap_cores(dec_sum))
            dec_sum, theirs = lax.optimization_barrier((dec_sum, theirs))
            final = add(dec_resid, dec_sum, *[from_chip(dec_sum, j) for j in range(1, chips)])
            picker = in_group[:, None] == jnp.arange(padded, dtype=jnp.int32)[None, :]
            picker = picker & (in_group[:, None] < slots)
            routed = jnp.dot(
                picker.astype(jnp.bfloat16), final, preferred_element_type=jnp.float32
            ).astype(jnp.bfloat16)
    give = jnp.concatenate([swap_cores(part) for part in jnp.split(give, 2, axis=1)], axis=1)
    prefill_out = add(resid, keep, give, *arrived)

    low = max(dp_count // 4, 1)
    pairs = routed.reshape(dp_count // low, low * per_device, width)
    rows = add(
        pairs[0], *[swap_groups(pairs[i], i * low) for i in range(1, dp_count // low)]
    )
    pairs = rows.reshape(low, per_device, width)
    routed = add(pairs[0], *[swap_groups(pairs[i], i) for i in range(1, low)])

    around = jnp.concatenate(entries + entries[:-1], axis=1)
    prefill_entries = lax.dynamic_slice_in_dim(
        around, (chips - chip) % chips * 2 * piece, tokens, 1
    )
    return (prefill_out, routed, prefill_entries, dec_entries[:, :slots])


def solution(mesh):
    placed = (
        P(("dp", "tensor"), None),
        P(("dp", "tensor"), None),
        P(),
        P("dp"),
        P("dp"),
        P(None, "dp", None, "tensor"),
        P(None, "dp", None, "tensor"),
        P(None, "tensor", None),
        P("tensor", None),
        P(),
        P(),
        P(None, "tensor"),
        P(None, "tensor"),
        P("tensor", None),
    )
    return jax.shard_map(
        on_device,
        mesh=mesh,
        in_specs=placed,
        out_specs=(
            P(("dp", "tensor"), None),
            P(("dp", "tensor"), None),
            P(None, "dp", "tensor"),
            P(None, "dp", "tensor"),
        ),
        check_vma=False,
    )
```

```python
import functools
import math

import jax
import jax.numpy as jnp
from jax import lax
from jax.experimental import pallas as pl
from jax.experimental.pallas import tpu as pltpu
from jax.sharding import PartitionSpec as P

HD = 128
EPSILON = 1e-06
THETA = 1000000.0
NEGATIVE = -1e30
MIB = 1 << 20


def swap_cores(value):
    count = lax.axis_size("tensor")
    return lax.ppermute(value, "tensor", [(i, i ^ 1) for i in range(count)])


def from_chip(value, step):
    count = lax.axis_size("tensor")
    chips = count // 2
    return lax.ppermute(
        value, "tensor", [(i, (i // 2 - step) % chips * 2 + i % 2) for i in range(count)]
    )


def from_other(value, step):
    count = lax.axis_size("tensor")
    return lax.ppermute(
        value, "tensor", [(i, (i // 2 - step) % (count // 2) * 2 + 1 - i % 2) for i in range(count)]
    )


def from_rest(value):
    chips = lax.axis_size("tensor") // 2
    return [from_chip(value, k) for k in range(1, chips)] + [from_other(value, k) for k in range(chips)]


def swap_groups(value, mask):
    count = lax.axis_size("dp")
    return lax.ppermute(value, "dp", [(i, i ^ mask) for i in range(count)])


def whole(shape):
    return pl.BlockSpec(shape, lambda *_: (0,) * len(shape))


def params(mib):
    return pltpu.CompilerParams(vmem_limit_bytes=mib * MIB)


def cost(flops, moved, exps=0):
    return pl.CostEstimate(flops=int(flops), bytes_accessed=int(moved), transcendentals=int(exps))


def normed(values, gain):
    spread = jnp.mean(values * values, axis=-1, keepdims=True)
    return (values * lax.rsqrt(spread + EPSILON) * gain).astype(jnp.bfloat16)


def turn(vectors, cosine, sine):
    return vectors * cosine + pltpu.roll(vectors, HD // 2, 1) * sine


def in_vmem(value):
    return pltpu.with_memory_space_constraint(value, pltpu.VMEM)


def in_hbm(value):
    return pltpu.with_memory_space_constraint(value, pltpu.HBM)


VMEM_WHOLE = pl.BlockSpec(memory_space=pltpu.VMEM)
SMEM_WHOLE = pl.BlockSpec(memory_space=pltpu.SMEM)
IN_PLACE = pl.BlockSpec(memory_space=pl.ANY)


def project_kernel(n_dec, n_after, groups, heads, place, *refs):
    refs = list(refs)
    mine, sib, weight, gain, cosine, sine = refs[:6]
    refs = refs[6:]
    if n_dec:
        dec, dec_cos, dec_sin = refs[:3]
        refs = refs[3:]
    refs = refs[n_after:]
    query, entries, everything = refs[:3]
    if n_dec:
        dec_query, dec_entries = refs[3:5]
    inner, rows_held, weight_held, row_sems, weight_sems, out_sem = refs[-6:]
    piece = mine.shape[0]
    core = place[0]
    scale = gain[...]
    depth = (groups + 2) * HD
    row_copies = [
        pltpu.make_async_copy(ref, rows_held.at[i], row_sems.at[i])
        for i, ref in enumerate((mine, sib))
    ]
    weight_copies = [
        pltpu.make_async_copy(
            weight.at[:, pl.ds(j * depth, depth)], weight_held.at[j], weight_sems.at[j]
        )
        for j in range(heads)
    ]
    for copy in row_copies + weight_copies:
        copy.start()
    for i, at in enumerate((core, 1 - core)):
        row_copies[i].wait()
        start = pl.multiple_of(at * piece, piece)
        inner[pl.ds(start, piece), :] = normed(rows_held[i].astype(jnp.float32), scale)
    if n_dec:
        inner[2 * piece :, :] = normed(dec[...].astype(jnp.float32), scale)
    here = pl.ds(pl.multiple_of(place[1] * 2 * piece, 2 * piece), 2 * piece)
    for j in range(heads):
        weight_copies[j].wait()
        mixed = jnp.dot(inner[...], weight_held[j], preferred_element_type=jnp.float32)

        def put(rows, cos, sin, query_out, entry_out):
            for g in range(groups):
                part = rows[:, g * HD : (g + 1) * HD]
                at = (j * groups + g) * HD
                turned = turn(part, cos, sin).astype(jnp.bfloat16)
                query_out[:, at : at + HD] = turned.astype(query_out.dtype)
            key = turn(rows[:, groups * HD : (groups + 1) * HD], cos, sin).astype(jnp.bfloat16)
            value = rows[:, (groups + 1) * HD :].astype(jnp.bfloat16)
            size = entry_out.shape[1]
            entry_out[0, :, j * HD : (j + 1) * HD] = key[:size]
            entry_out[1, :, j * HD : (j + 1) * HD] = value[:size]

        put(mixed[: 2 * piece], cosine[here, :], sine[here, :], query, entries)
        if n_dec:
            put(mixed[2 * piece :], dec_cos[...], dec_sin[...], dec_query, dec_entries)
    keep = pltpu.make_async_copy(entries, everything.at[:, here, :], out_sem)
    keep.start()
    keep.wait()


def project(
    place, mine, sib, gain, weight, tables, heads, everything, dec=None, dec_tables=None, slots=0, after=()
):
    piece, width = mine.shape
    depth = weight.shape[1] // heads
    groups = depth // HD - 2
    block = 2 * piece
    n_dec = 0 if dec is None else dec.shape[0]
    args = [mine, sib, weight, gain, *tables]
    if n_dec:
        args += [dec, *dec_tables]
    n_operands = len(args)
    after = list(after)
    aliases = {}
    if everything is not None:
        after.append(everything)
        aliases = {n_operands + len(after): 2}
    wide = heads * groups * HD
    out_shape = [
        jax.ShapeDtypeStruct((block, wide), jnp.bfloat16),
        jax.ShapeDtypeStruct((2, block, heads * HD), jnp.bfloat16),
        jax.ShapeDtypeStruct((2, tables[0].shape[0], heads * HD), jnp.bfloat16),
    ]
    if n_dec:
        out_shape += [
            jax.ShapeDtypeStruct((n_dec, wide), jnp.float32),
            jax.ShapeDtypeStruct((2, slots, heads * HD), jnp.bfloat16),
        ]
    rows = block + n_dec
    return pl.pallas_call(
        functools.partial(project_kernel, n_dec, len(after), groups, heads),
        out_shape=out_shape,
        in_specs=[SMEM_WHOLE]
        + [IN_PLACE] * 3
        + [VMEM_WHOLE] * (len(args) - 3)
        + [IN_PLACE] * len(after),
        out_specs=[VMEM_WHOLE] * 2 + [IN_PLACE] + [VMEM_WHOLE] * (len(out_shape) - 3),
        scratch_shapes=[
            pltpu.VMEM((rows, width), jnp.bfloat16),
            pltpu.VMEM((2, piece, width), jnp.bfloat16),
            pltpu.VMEM((heads, width, depth), jnp.bfloat16),
            pltpu.SemaphoreType.DMA((2,)),
            pltpu.SemaphoreType.DMA((heads,)),
            pltpu.SemaphoreType.DMA(()),
        ],
        input_output_aliases=aliases,
        compiler_params=params(20),
        cost_estimate=cost(2 * rows * weight.size, 2 * (weight.size + 2 * rows * width)),
        name="project",
    )(place, *args, *after)


def fill_kernel(groups, chips, place, query, cache_key, cache_value, *refs):
    new_keys, new_values, out = refs[:chips], refs[chips : 2 * chips], refs[-1]
    scaling = 1.0 / math.sqrt(HD)
    count = query.shape[0]
    stored = cache_key.shape[2]
    old_seen = lax.broadcasted_iota(jnp.int32, (1, stored), 1) < place[2]
    ahead = lax.broadcasted_iota(jnp.int32, (count, count), 1) - lax.broadcasted_iota(
        jnp.int32, (count, count), 0
    )
    across = (((1,), (1,)), ((), ()))
    for g in range(groups):
        rows = query[:, g * HD : (g + 1) * HD]
        scores = lax.dot_general(
            rows, cache_key[0, 0], across, preferred_element_type=jnp.float32
        )
        scores = [jnp.where(old_seen, scores * scaling, NEGATIVE)]
        for k in range(chips):
            fresh = lax.dot_general(
                rows, new_keys[k][0], across, preferred_element_type=jnp.float32
            )
            gap = (place[1] - place[3 + k]) * count
            scores.append(jnp.where(ahead <= gap, fresh * scaling, NEGATIVE))
        top = jnp.max(scores[0], axis=-1, keepdims=True)
        for part in scores[1:]:
            top = jnp.maximum(top, jnp.max(part, axis=-1, keepdims=True))
        mix, total = 0.0, 0.0
        for part, values in zip(scores, [cache_value[0, 0], *[v[0] for v in new_values]]):
            weights = jnp.exp(part - top)
            total += jnp.sum(weights, axis=-1, keepdims=True)
            mix += jnp.dot(
                weights.astype(jnp.bfloat16), values, preferred_element_type=jnp.float32
            )
        out[:, g * HD : (g + 1) * HD] = (mix / total).astype(jnp.bfloat16)


def fill_attend(place, query, cache, entries, heads, after=()):
    count = query.shape[0]
    groups = query.shape[1] // heads // HD
    stored = cache.shape[2]
    chips = len(entries)
    pairs = count * groups * heads * (stored + chips * count)
    return pl.pallas_call(
        functools.partial(fill_kernel, groups, chips),
        out_shape=jax.ShapeDtypeStruct(query.shape, jnp.bfloat16),
        grid_spec=pltpu.PrefetchScalarGridSpec(
            num_scalar_prefetch=1,
            grid=(heads,),
            in_specs=[
                pl.BlockSpec((count, groups * HD), lambda j, s: (0, j)),
                pl.BlockSpec((1, 1, stored, HD), lambda j, s: (0, 0, 0, j)),
                pl.BlockSpec((1, 1, stored, HD), lambda j, s: (1, 0, 0, j)),
            ]
            + [pl.BlockSpec((1, count, HD), lambda j, s: (0, 0, j))] * chips
            + [pl.BlockSpec((1, count, HD), lambda j, s: (1, 0, j))] * chips
            + [IN_PLACE] * len(after),
            out_specs=pl.BlockSpec((count, groups * HD), lambda j, s: (0, j)),
        ),
        compiler_params=params(12),
        cost_estimate=cost(8 * pairs * HD, 2 * cache.size, pairs),
        name="fill_attend",
    )(place, query, cache, cache, *entries, *entries, *after)


def step_kernel(
    heads, lengths, query, entries, cache, weight, out, held, scores, shares, weight_held, arrived, weight_sem
):
    scaling = 1.0 / math.sqrt(HD)
    slots, stored, width = cache.shape[1:]
    groups = query.shape[1] // width
    lanes = 8
    copies = [
        [pltpu.make_async_copy(cache.at[w, s], held.at[w, s], arrived.at[w, s]) for s in range(slots)]
        for w in range(2)
    ]
    weight_copy = pltpu.make_async_copy(weight, weight_held, weight_sem)
    for copy in copies[0] + copies[1] + [weight_copy]:
        copy.start()
    across = (((1,), (1,)), ((), ()))
    places = lax.broadcasted_iota(jnp.int32, (1, stored), 1)
    blank = jnp.zeros((1, HD), jnp.float32)
    new_keys = entries[0].astype(jnp.float32)
    new_values = entries[1].astype(jnp.float32)
    own_scores = []
    for s in range(slots):
        rows = []
        for j in range(heads):
            for g in range(groups):
                at = (j * groups + g) * HD
                part = query[s : s + 1, at : at + HD]
                rows.append(
                    jnp.concatenate([part if i == j else blank for i in range(heads)], axis=1)
                )
        rows.append(jnp.zeros((lanes - heads * groups, width), jnp.float32))
        rows = jnp.concatenate(rows, axis=0)
        own_scores.append(jnp.sum(rows * new_keys[s : s + 1], axis=-1, keepdims=True))
        copies[0][s].wait()
        old = lax.dot_general(
            rows.astype(jnp.bfloat16), held[0, s], across, preferred_element_type=jnp.float32
        )
        scores[s * lanes : (s + 1) * lanes, :] = jnp.where(
            places < lengths[s], old * scaling, NEGATIVE
        )
    old = scores[...]
    own = jnp.concatenate(own_scores, axis=0) * scaling
    top = jnp.maximum(jnp.max(old, axis=-1, keepdims=True), own)
    old = jnp.exp(old - top)
    own = jnp.exp(own - top)
    total = jnp.sum(old, axis=-1, keepdims=True) + own
    shares[...] = old / total
    own = (own / total).astype(jnp.bfloat16).astype(jnp.float32)
    attended = []
    for s in range(slots):
        copies[1][s].wait()
        here = slice(s * lanes, (s + 1) * lanes)
        mix = jnp.dot(
            shares[here, :].astype(jnp.bfloat16), held[1, s], preferred_element_type=jnp.float32
        )
        mix += own[here] * new_values[s : s + 1]
        parts = []
        for j in range(heads):
            for g in range(groups):
                row = j * groups + g
                parts.append(mix[row : row + 1, j * HD : (j + 1) * HD])
        attended.append(jnp.concatenate(parts, axis=1))
    if out.shape[0] > slots:
        attended.append(jnp.zeros((out.shape[0] - slots, query.shape[1]), jnp.float32))
    attended = jnp.concatenate(attended, axis=0).astype(jnp.bfloat16)
    weight_copy.wait()
    part = jnp.dot(attended, weight_held[...], preferred_element_type=jnp.float32)
    out[...] = part.astype(jnp.bfloat16)


def step_attend(lengths, query, entries, cache, weight, heads):
    slots, stored = cache.shape[1:3]
    padded = query.shape[0]
    rows = slots * 8
    return pl.pallas_call(
        functools.partial(step_kernel, heads),
        out_shape=jax.ShapeDtypeStruct((padded, weight.shape[1]), jnp.bfloat16),
        in_specs=[SMEM_WHOLE, VMEM_WHOLE, VMEM_WHOLE, IN_PLACE, IN_PLACE],
        out_specs=VMEM_WHOLE,
        scratch_shapes=[
            pltpu.VMEM(cache.shape, jnp.bfloat16),
            pltpu.VMEM((rows, stored), jnp.float32),
            pltpu.VMEM((rows, stored), jnp.float32),
            pltpu.VMEM(weight.shape, jnp.bfloat16),
            pltpu.SemaphoreType.DMA((2, slots)),
            pltpu.SemaphoreType.DMA(()),
        ],
        compiler_params=params(20),
        cost_estimate=cost(16 * cache.size, 2 * cache.size, rows * stored),
        name="step_attend",
    )(lengths, query, entries, cache, weight)


def out_kernel(place, mine, sib, weight, sib_weight, *refs):
    out = refs[-1]
    half = out.shape[1]
    cols = pl.ds(pl.multiple_of(place[0] * half, half), half)
    part = jnp.dot(mine[...], weight[:, cols], preferred_element_type=jnp.float32)
    part += jnp.dot(sib[...], sib_weight[:, cols], preferred_element_type=jnp.float32)
    out[...] = part.astype(jnp.bfloat16)


def out_project(place, mine, sib, weight, sib_weight, after=()):
    rows, depth = mine.shape
    half = weight.shape[1] // 2
    return pl.pallas_call(
        out_kernel,
        out_shape=jax.ShapeDtypeStruct((rows, half), jnp.bfloat16),
        in_specs=[SMEM_WHOLE] + [VMEM_WHOLE] * 4 + [IN_PLACE] * len(after),
        out_specs=VMEM_WHOLE,
        compiler_params=params(8),
        cost_estimate=cost(4 * rows * depth * half, 4 * depth * half + 6 * rows * half),
        name="out_project",
    )(place, mine, sib, weight, sib_weight, *after)


def forward_kernel(chips, n_dec, n_after, chunk, place, *refs):
    refs = list(refs)
    mine, sib = refs[:2]
    shares = refs[2 : 2 + 2 * chips]
    refs = refs[2 + 2 * chips :]
    if n_dec:
        dec, dec_shares = refs[0], refs[1 : 1 + 2 * chips]
        refs = refs[1 + 2 * chips :]
    gain, *weights = refs[:4]
    refs = refs[4 + n_after :]
    keep, give, resid = refs[:3]
    refs = refs[3:]
    if n_dec:
        dec_out, dec_resid = refs[:2]
        refs = refs[2:]
    held, inner, hidden, gate, up, down, arrived = refs
    chunks = gate.shape[0]
    copies = [
        [
            pltpu.make_async_copy(
                source.at[:, pl.ds(i * chunk, chunk)], target.at[i], arrived.at[w, i]
            )
            for i in range(chunks)
        ]
        for w, (source, target) in enumerate(zip(weights, (gate, up, down)))
    ]
    for i in range(chunks):
        copies[0][i].start()
        copies[1][i].start()
    for i in range(chunks):
        copies[2][i].start()
    piece = mine.shape[0]
    half = shares[0].shape[1]
    core = place[0]
    for rows, at_rows, put in ((mine, core, 0), (sib, 1 - core, piece)):
        here = pl.ds(pl.multiple_of(at_rows * piece, piece), piece)
        for side in range(2):
            at = core if side == 0 else 1 - core
            cols = pl.ds(pl.multiple_of(at * half, half), half)
            added = shares[side][here, :].astype(jnp.float32)
            for k in range(1, chips):
                added += shares[2 * k + side][here, :].astype(jnp.float32)
            value = rows[:, cols].astype(jnp.float32) + added
            held[put : put + piece, cols] = value.astype(jnp.bfloat16)
    if n_dec:
        added = dec_shares[0][...].astype(jnp.float32)
        for share in dec_shares[1:]:
            added += share[...].astype(jnp.float32)
        held[2 * piece :, :] = (dec[...].astype(jnp.float32) + added).astype(jnp.bfloat16)
    for put in range(0, held.shape[0], piece):
        here = slice(put, min(put + piece, held.shape[0]))
        inner[here, :] = normed(held[here, :].astype(jnp.float32), gain[...])
    resid[...] = held[:piece, :]
    if n_dec:
        dec_resid[...] = held[2 * piece :, :]

    for i in range(chunks):
        at = slice(i * chunk, (i + 1) * chunk)
        copies[0][i].wait()
        gated = jnp.dot(inner[...], gate[i], preferred_element_type=jnp.float32)
        copies[1][i].wait()
        raised = jnp.dot(inner[...], up[i], preferred_element_type=jnp.float32)
        hidden[:, at] = (gated / (1.0 + jnp.exp(-gated)) * raised).astype(jnp.bfloat16)
    for i in range(chunks):
        at = slice(i * chunk, (i + 1) * chunk)
        copies[2][i].wait()
        part = jnp.dot(hidden[...], down[i], preferred_element_type=jnp.float32)
        part = part.astype(jnp.bfloat16)
        keep[:, at] = part[:piece]
        give[:, at] = part[piece : 2 * piece]
        if n_dec:
            dec_out[:, at] = part[2 * piece :]


def feed_forward(
    place, mine, sib, shares, gain, gate, up, down, dec=None, dec_shares=None, after=()
):
    piece, width = mine.shape
    chips = len(shares) // 2
    units = gate.shape[1]
    chunks = 4
    chunk = width // chunks
    n_dec = 0 if dec is None else dec.shape[0]
    rows = 2 * piece + n_dec
    args = [mine, sib, *shares]
    if n_dec:
        args += [dec, *dec_shares]
    n_whole = len(args) + 1
    args += [gain, gate, up, down]
    sizes = [piece] * 3 + [n_dec] * 2 * bool(n_dec)
    return pl.pallas_call(
        functools.partial(forward_kernel, chips, n_dec, len(after), chunk),
        out_shape=[jax.ShapeDtypeStruct((n, width), jnp.bfloat16) for n in sizes],
        in_specs=[SMEM_WHOLE] + [VMEM_WHOLE] * n_whole + [IN_PLACE] * (3 + len(after)),
        out_specs=[VMEM_WHOLE] * len(sizes),
        scratch_shapes=[
            pltpu.VMEM((rows, width), jnp.bfloat16),
            pltpu.VMEM((rows, width), jnp.bfloat16),
            pltpu.VMEM((rows, units), jnp.bfloat16),
            pltpu.VMEM((units // chunk, width, chunk), jnp.bfloat16),
            pltpu.VMEM((units // chunk, width, chunk), jnp.bfloat16),
            pltpu.VMEM((chunks, units, chunk), jnp.bfloat16),
            pltpu.SemaphoreType.DMA((3, chunks)),
        ],
        compiler_params=params(40),
        cost_estimate=cost(6 * rows * width * units, 6 * width * units, rows * units),
        name="feed_forward",
    )(place, *args, *after)


def angle_tables(places):
    halfway = HD // 2
    powers = jnp.arange(halfway, dtype=jnp.float32) * (2.0 / HD)
    inverse = THETA ** (-powers)
    angles = places.astype(jnp.float32)[:, None] * inverse[None, :]
    cosine, sine = jnp.cos(angles), jnp.sin(angles)
    return jnp.concatenate([cosine, cosine], axis=-1), jnp.concatenate([-sine, sine], axis=-1)


def add(*values):
    total = values[0].astype(jnp.float32)
    for value in values[1:]:
        total = total + value.astype(jnp.float32)
    return total.astype(jnp.bfloat16)


def on_device(
    prefill_rows,
    decode_rows,
    deal_order,
    prefill_offset,
    cache_length,
    prefill_cache,
    decode_cache,
    qkv_weight,
    out_weight,
    attention_gain,
    forward_gain,
    gate_weight,
    up_weight,
    down_weight,
):
    tensor_count = lax.axis_size("tensor")
    dp_count = lax.axis_size("dp")
    chips = tensor_count // 2
    tensor_place = lax.axis_index("tensor")
    group_place = lax.axis_index("dp")
    chip, core = tensor_place // 2, tensor_place % 2
    piece, width = prefill_rows.shape
    per_device = decode_rows.shape[0]
    requests = deal_order.shape[0]
    slots = cache_length.shape[0]
    padded = -(-slots // 16) * 16
    heads = qkv_weight.shape[1]
    tokens = piece * tensor_count

    def place_of(k):
        spots = [core, (chip + k) % chips, prefill_offset[0]]
        return jnp.stack(spots + [(chip + j) % chips for j in range(chips)]).astype(jnp.int32)

    places = [place_of(k) for k in range(chips)]
    weight = in_hbm(qkv_weight.reshape(width, -1))
    gate_weight, up_weight, down_weight = map(in_hbm, (gate_weight, up_weight, down_weight))
    prefill_cache, decode_cache = in_hbm(prefill_cache), in_hbm(decode_cache)

    mines = [prefill_rows] + [from_chip(prefill_rows, k) for k in range(1, chips)]
    sibs = [swap_cores(rows) for rows in mines]

    low = max(dp_count // 4, 1)
    pool = [decode_rows] + [swap_groups(decode_rows, i) for i in range(1, low)]
    pool = jnp.concatenate(pool, axis=0)
    pool = [pool] + [swap_groups(pool, i * low) for i in range(1, dp_count // low)]
    pool = jnp.concatenate(pool, axis=0)
    index = jnp.arange(dp_count * per_device, dtype=jnp.int32)
    origin = jnp.bitwise_xor(group_place, index // per_device)
    request = (origin * tensor_count + tensor_place) * per_device + index % per_device
    slot_of = jnp.sum(
        jnp.where(
            request[:, None] == jnp.arange(requests, dtype=jnp.int32)[None, :],
            deal_order[None, :],
            0,
        ),
        axis=1,
    )
    in_group = slot_of - group_place * slots
    chooser = (jnp.arange(padded, dtype=jnp.int32)[:, None] == in_group[None, :]) & (
        in_group[None, :] < slots
    )
    dealt = jnp.dot(
        chooser.astype(jnp.bfloat16), pool, preferred_element_type=jnp.float32
    ).astype(jnp.bfloat16)

    gain = attention_gain.reshape(1, width)
    tables = angle_tables(prefill_offset[0] + jnp.arange(tokens, dtype=jnp.int32))
    dec_tables = angle_tables(jnp.pad(cache_length, (0, padded - slots)))
    queries, entries, everything = [None] * chips, [None] * chips, None
    for k in range(chips):
        last = k == chips - 1
        if last:
            dealt = add(dealt, *from_rest(dealt))
        got = project(
            places[k],
            in_hbm(mines[k]),
            in_hbm(sibs[k]),
            gain,
            weight,
            tables,
            heads,
            everything,
            dealt if last else None,
            dec_tables if last else None,
            slots,
            [queries[k - 1]] if k else [dealt],
        )
        queries[k], entries[k], everything = got[:3]
        if last:
            dec_query, dec_entries = got[3:]

    out_share = out_weight
    sib_weight, queries[-1] = lax.optimization_barrier((out_weight, queries[-1]))
    sib_weight = in_vmem(swap_cores(sib_weight))
    out_weight = in_vmem(out_weight)

    def finish(attended, place, after):
        sib = swap_cores(attended)
        return out_project(place, attended, sib, out_weight, sib_weight, after)

    parts = []
    dec_shares = []
    for k in range(chips):
        attended = fill_attend(
            places[k], queries[k], prefill_cache, entries, heads, dec_shares[:1]
        )
        parts.append(finish(attended, places[k], dec_shares[1:]))
        if k == 0:
            lengths, parts[0] = lax.optimization_barrier((cache_length, parts[0]))
            dec_part = step_attend(
                lengths, dec_query, dec_entries, decode_cache, in_hbm(out_share), heads
            )
            dec_shares = [dec_part, *from_rest(dec_part)]

    def shares_of(own, others):
        pairs = []
        for value in [own, *others]:
            pairs += [value, swap_cores(value)]
        return pairs

    gain = forward_gain.reshape(1, width)
    order = [*range(1, chips), 0]

    def fetch(b):
        return [from_chip(parts[(b - j) % chips], j) for j in range(1, chips)]

    theirs = fetch(order[0])
    arrived = []
    for n, b in enumerate(order):
        got = feed_forward(
            places[b],
            mines[b],
            sibs[b],
            shares_of(parts[b], theirs),
            gain,
            gate_weight,
            up_weight,
            down_weight,
            dealt if n == 0 else None,
            dec_shares if n == 0 else None,
        )
        keep, give, resid = got[:3]
        if n + 1 < chips:
            theirs = fetch(order[n + 1])
            arrived.append(from_chip(add(keep, swap_cores(give)), chips - b))
        if n == 0:
            dec_sum, dec_resid = got[3:]
            dec_others = from_rest(dec_sum)
    dec_sum, arrived[0] = lax.optimization_barrier((dec_sum, arrived[0]))
    final = add(dec_resid, dec_sum, *dec_others)
    picker = in_group[:, None] == jnp.arange(padded, dtype=jnp.int32)[None, :]
    picker = picker & (in_group[:, None] < slots)
    routed = jnp.dot(
        picker.astype(jnp.bfloat16), final, preferred_element_type=jnp.float32
    ).astype(jnp.bfloat16)
    give = jnp.concatenate([swap_cores(part) for part in jnp.split(give, 2, axis=1)], axis=1)
    prefill_out = add(resid, keep, give, *arrived)

    low = max(dp_count // 4, 1)
    pairs = routed.reshape(dp_count // low, low * per_device, width)
    rows = add(
        pairs[0], *[swap_groups(pairs[i], i * low) for i in range(1, dp_count // low)]
    )
    pairs = rows.reshape(low, per_device, width)
    routed = add(pairs[0], *[swap_groups(pairs[i], i) for i in range(1, low)])

    return (prefill_out, routed, everything, dec_entries)


def solution(mesh):
    placed = (
        P(("dp", "tensor"), None),
        P(("dp", "tensor"), None),
        P(),
        P("dp"),
        P("dp"),
        P(None, "dp", None, "tensor"),
        P(None, "dp", None, "tensor"),
        P(None, "tensor", None),
        P("tensor", None),
        P(),
        P(),
        P(None, "tensor"),
        P(None, "tensor"),
        P("tensor", None),
    )
    return jax.shard_map(
        on_device,
        mesh=mesh,
        in_specs=placed,
        out_specs=(
            P(("dp", "tensor"), None),
            P(("dp", "tensor"), None),
            P(None, "dp", "tensor"),
            P(None, "dp", "tensor"),
        ),
        check_vma=False,
    )
```

```python
import functools
import math

import jax
import jax.numpy as jnp
from jax import lax
from jax.experimental import pallas as pl
from jax.experimental.pallas import tpu as pltpu
from jax.sharding import PartitionSpec as P

HD = 128
EPSILON = 1e-06
THETA = 1000000.0
NEGATIVE = -1e30
MIB = 1 << 20


def swap_cores(value):
    count = lax.axis_size("tensor")
    return lax.ppermute(value, "tensor", [(i, i ^ 1) for i in range(count)])


def from_chip(value, step):
    count = lax.axis_size("tensor")
    chips = count // 2
    return lax.ppermute(
        value, "tensor", [(i, (i // 2 - step) % chips * 2 + i % 2) for i in range(count)]
    )


def from_other(value, step):
    count = lax.axis_size("tensor")
    return lax.ppermute(
        value, "tensor", [(i, (i // 2 - step) % (count // 2) * 2 + 1 - i % 2) for i in range(count)]
    )


def from_rest(value):
    chips = lax.axis_size("tensor") // 2
    return [from_chip(value, k) for k in range(1, chips)] + [from_other(value, k) for k in range(chips)]


def swap_groups(value, mask):
    count = lax.axis_size("dp")
    return lax.ppermute(value, "dp", [(i, i ^ mask) for i in range(count)])


def whole(shape):
    return pl.BlockSpec(shape, lambda *_: (0,) * len(shape))


def params(mib):
    return pltpu.CompilerParams(vmem_limit_bytes=mib * MIB)


def cost(flops, moved, exps=0):
    return pl.CostEstimate(flops=int(flops), bytes_accessed=int(moved), transcendentals=int(exps))


def normed(values, gain):
    spread = jnp.mean(values * values, axis=-1, keepdims=True)
    return (values * lax.rsqrt(spread + EPSILON) * gain).astype(jnp.bfloat16)


def turn(vectors, cosine, sine):
    return vectors * cosine + pltpu.roll(vectors, HD // 2, 1) * sine


def in_vmem(value):
    return pltpu.with_memory_space_constraint(value, pltpu.VMEM)


def in_hbm(value):
    return pltpu.with_memory_space_constraint(value, pltpu.HBM)


VMEM_WHOLE = pl.BlockSpec(memory_space=pltpu.VMEM)
SMEM_WHOLE = pl.BlockSpec(memory_space=pltpu.SMEM)
IN_PLACE = pl.BlockSpec(memory_space=pl.ANY)


def project_kernel(n_dec, n_after, groups, heads, place, *refs):
    refs = list(refs)
    mine, sib, weight, gain, cosine, sine = refs[:6]
    refs = refs[6:]
    if n_dec:
        dec, dec_cos, dec_sin = refs[:3]
        refs = refs[3:]
    refs = refs[n_after:]
    query, entries, everything = refs[:3]
    if n_dec:
        dec_query, dec_entries = refs[3:5]
    inner, rows_held, weight_held, row_sems, weight_sems, out_sem = refs[-6:]
    piece = mine.shape[0]
    core = place[0]
    scale = gain[...]
    depth = (groups + 2) * HD
    row_copies = [
        pltpu.make_async_copy(ref, rows_held.at[i], row_sems.at[i])
        for i, ref in enumerate((mine, sib))
    ]
    weight_copies = [
        pltpu.make_async_copy(
            weight.at[:, pl.ds(j * depth, depth)], weight_held.at[j], weight_sems.at[j]
        )
        for j in range(heads)
    ]
    for copy in row_copies + weight_copies:
        copy.start()
    for i, at in enumerate((core, 1 - core)):
        row_copies[i].wait()
        start = pl.multiple_of(at * piece, piece)
        inner[pl.ds(start, piece), :] = normed(rows_held[i].astype(jnp.float32), scale)
    if n_dec:
        inner[2 * piece :, :] = normed(dec[...].astype(jnp.float32), scale)
    here = pl.ds(pl.multiple_of(place[1] * 2 * piece, 2 * piece), 2 * piece)
    for j in range(heads):
        weight_copies[j].wait()
        mixed = jnp.dot(inner[...], weight_held[j], preferred_element_type=jnp.float32)

        def put(rows, cos, sin, query_out, entry_out):
            for g in range(groups):
                part = rows[:, g * HD : (g + 1) * HD]
                at = (j * groups + g) * HD
                turned = turn(part, cos, sin).astype(jnp.bfloat16)
                query_out[:, at : at + HD] = turned.astype(query_out.dtype)
            key = turn(rows[:, groups * HD : (groups + 1) * HD], cos, sin).astype(jnp.bfloat16)
            value = rows[:, (groups + 1) * HD :].astype(jnp.bfloat16)
            size = entry_out.shape[1]
            entry_out[0, :, j * HD : (j + 1) * HD] = key[:size]
            entry_out[1, :, j * HD : (j + 1) * HD] = value[:size]

        put(mixed[: 2 * piece], cosine[here, :], sine[here, :], query, entries)
        if n_dec:
            put(mixed[2 * piece :], dec_cos[...], dec_sin[...], dec_query, dec_entries)
    keep = pltpu.make_async_copy(entries, everything.at[:, here, :], out_sem)
    keep.start()
    keep.wait()


def project(
    place, mine, sib, gain, weight, tables, heads, everything, dec=None, dec_tables=None, slots=0, after=()
):
    piece, width = mine.shape
    depth = weight.shape[1] // heads
    groups = depth // HD - 2
    block = 2 * piece
    n_dec = 0 if dec is None else dec.shape[0]
    args = [mine, sib, weight, gain, *tables]
    if n_dec:
        args += [dec, *dec_tables]
    n_operands = len(args)
    after = list(after)
    aliases = {}
    if everything is not None:
        after.append(everything)
        aliases = {n_operands + len(after): 2}
    wide = heads * groups * HD
    out_shape = [
        jax.ShapeDtypeStruct((block, wide), jnp.bfloat16),
        jax.ShapeDtypeStruct((2, block, heads * HD), jnp.bfloat16),
        jax.ShapeDtypeStruct((2, tables[0].shape[0], heads * HD), jnp.bfloat16),
    ]
    if n_dec:
        out_shape += [
            jax.ShapeDtypeStruct((n_dec, wide), jnp.float32),
            jax.ShapeDtypeStruct((2, slots, heads * HD), jnp.bfloat16),
        ]
    rows = block + n_dec
    return pl.pallas_call(
        functools.partial(project_kernel, n_dec, len(after), groups, heads),
        out_shape=out_shape,
        in_specs=[SMEM_WHOLE]
        + [IN_PLACE] * 3
        + [VMEM_WHOLE] * (len(args) - 3)
        + [IN_PLACE] * len(after),
        out_specs=[VMEM_WHOLE] * 2 + [IN_PLACE] + [VMEM_WHOLE] * (len(out_shape) - 3),
        scratch_shapes=[
            pltpu.VMEM((rows, width), jnp.bfloat16),
            pltpu.VMEM((2, piece, width), jnp.bfloat16),
            pltpu.VMEM((heads, width, depth), jnp.bfloat16),
            pltpu.SemaphoreType.DMA((2,)),
            pltpu.SemaphoreType.DMA((heads,)),
            pltpu.SemaphoreType.DMA(()),
        ],
        input_output_aliases=aliases,
        compiler_params=params(20),
        cost_estimate=cost(2 * rows * weight.size, 2 * (weight.size + 2 * rows * width)),
        name="project",
    )(place, *args, *after)


def fill_kernel(groups, chips, place, query, cache_key, cache_value, *refs):
    new_keys, new_values, out = refs[:chips], refs[chips : 2 * chips], refs[-1]
    scaling = 1.0 / math.sqrt(HD)
    count = query.shape[0]
    stored = cache_key.shape[2]
    old_seen = lax.broadcasted_iota(jnp.int32, (1, stored), 1) < place[2]
    ahead = lax.broadcasted_iota(jnp.int32, (count, count), 1) - lax.broadcasted_iota(
        jnp.int32, (count, count), 0
    )
    across = (((1,), (1,)), ((), ()))
    rows = jnp.concatenate([query[:, g * HD : (g + 1) * HD] for g in range(groups)], axis=0)
    ahead = jnp.concatenate([ahead] * groups, axis=0)
    scores = lax.dot_general(rows, cache_key[0, 0], across, preferred_element_type=jnp.float32)
    scores = [jnp.where(old_seen, scores * scaling, NEGATIVE)]
    for k in range(chips):
        fresh = lax.dot_general(rows, new_keys[k][0], across, preferred_element_type=jnp.float32)
        gap = (place[1] - place[3 + k]) * count
        scores.append(jnp.where(ahead <= gap, fresh * scaling, NEGATIVE))
    top = jnp.max(scores[0], axis=-1, keepdims=True)
    for part in scores[1:]:
        top = jnp.maximum(top, jnp.max(part, axis=-1, keepdims=True))
    mix, total = 0.0, 0.0
    for part, values in zip(scores, [cache_value[0, 0], *[v[0] for v in new_values]]):
        weights = jnp.exp(part - top)
        total += jnp.sum(weights, axis=-1, keepdims=True)
        mix += jnp.dot(weights.astype(jnp.bfloat16), values, preferred_element_type=jnp.float32)
    mix = (mix / total).astype(jnp.bfloat16)
    for g in range(groups):
        out[:, g * HD : (g + 1) * HD] = mix[g * count : (g + 1) * count]


def fill_attend(place, query, cache, entries, heads, after=()):
    count = query.shape[0]
    groups = query.shape[1] // heads // HD
    stored = cache.shape[2]
    chips = len(entries)
    pairs = count * groups * heads * (stored + chips * count)
    return pl.pallas_call(
        functools.partial(fill_kernel, groups, chips),
        out_shape=jax.ShapeDtypeStruct(query.shape, jnp.bfloat16),
        grid_spec=pltpu.PrefetchScalarGridSpec(
            num_scalar_prefetch=1,
            grid=(heads,),
            in_specs=[
                pl.BlockSpec((count, groups * HD), lambda j, s: (0, j)),
                pl.BlockSpec((1, 1, stored, HD), lambda j, s: (0, 0, 0, j)),
                pl.BlockSpec((1, 1, stored, HD), lambda j, s: (1, 0, 0, j)),
            ]
            + [pl.BlockSpec((1, count, HD), lambda j, s: (0, 0, j))] * chips
            + [pl.BlockSpec((1, count, HD), lambda j, s: (1, 0, j))] * chips
            + [IN_PLACE] * len(after),
            out_specs=pl.BlockSpec((count, groups * HD), lambda j, s: (0, j)),
        ),
        compiler_params=params(24),
        cost_estimate=cost(8 * pairs * HD, 2 * cache.size, pairs),
        name="fill_attend",
    )(place, query, cache, cache, *entries, *entries, *after)


def step_kernel(
    heads, lengths, query, entries, cache, weight, out, held, scores, shares, weight_held, arrived, weight_sem
):
    scaling = 1.0 / math.sqrt(HD)
    slots, stored, width = cache.shape[1:]
    groups = query.shape[1] // width
    lanes = 8
    copies = [
        [pltpu.make_async_copy(cache.at[w, s], held.at[w, s], arrived.at[w, s]) for s in range(slots)]
        for w in range(2)
    ]
    weight_copy = pltpu.make_async_copy(weight, weight_held, weight_sem)
    for copy in copies[0] + copies[1] + [weight_copy]:
        copy.start()
    across = (((1,), (1,)), ((), ()))
    places = lax.broadcasted_iota(jnp.int32, (1, stored), 1)
    blank = jnp.zeros((1, HD), jnp.float32)
    new_keys = entries[0].astype(jnp.float32)
    new_values = entries[1].astype(jnp.float32)
    own_scores = []
    for s in range(slots):
        rows = []
        for j in range(heads):
            for g in range(groups):
                at = (j * groups + g) * HD
                part = query[s : s + 1, at : at + HD]
                rows.append(
                    jnp.concatenate([part if i == j else blank for i in range(heads)], axis=1)
                )
        rows.append(jnp.zeros((lanes - heads * groups, width), jnp.float32))
        rows = jnp.concatenate(rows, axis=0)
        own_scores.append(jnp.sum(rows * new_keys[s : s + 1], axis=-1, keepdims=True))
        copies[0][s].wait()
        old = lax.dot_general(
            rows.astype(jnp.bfloat16), held[0, s], across, preferred_element_type=jnp.float32
        )
        scores[s * lanes : (s + 1) * lanes, :] = jnp.where(
            places < lengths[s], old * scaling, NEGATIVE
        )
    old = scores[...]
    own = jnp.concatenate(own_scores, axis=0) * scaling
    top = jnp.maximum(jnp.max(old, axis=-1, keepdims=True), own)
    old = jnp.exp(old - top)
    own = jnp.exp(own - top)
    total = jnp.sum(old, axis=-1, keepdims=True) + own
    shares[...] = old / total
    own = (own / total).astype(jnp.bfloat16).astype(jnp.float32)
    attended = []
    for s in range(slots):
        copies[1][s].wait()
        here = slice(s * lanes, (s + 1) * lanes)
        mix = jnp.dot(
            shares[here, :].astype(jnp.bfloat16), held[1, s], preferred_element_type=jnp.float32
        )
        mix += own[here] * new_values[s : s + 1]
        parts = []
        for j in range(heads):
            for g in range(groups):
                row = j * groups + g
                parts.append(mix[row : row + 1, j * HD : (j + 1) * HD])
        attended.append(jnp.concatenate(parts, axis=1))
    if out.shape[0] > slots:
        attended.append(jnp.zeros((out.shape[0] - slots, query.shape[1]), jnp.float32))
    attended = jnp.concatenate(attended, axis=0).astype(jnp.bfloat16)
    weight_copy.wait()
    part = jnp.dot(attended, weight_held[...], preferred_element_type=jnp.float32)
    out[...] = part.astype(jnp.bfloat16)


def step_attend(lengths, query, entries, cache, weight, heads):
    slots, stored = cache.shape[1:3]
    padded = query.shape[0]
    rows = slots * 8
    return pl.pallas_call(
        functools.partial(step_kernel, heads),
        out_shape=jax.ShapeDtypeStruct((padded, weight.shape[1]), jnp.bfloat16),
        in_specs=[SMEM_WHOLE, VMEM_WHOLE, VMEM_WHOLE, IN_PLACE, IN_PLACE],
        out_specs=VMEM_WHOLE,
        scratch_shapes=[
            pltpu.VMEM(cache.shape, jnp.bfloat16),
            pltpu.VMEM((rows, stored), jnp.float32),
            pltpu.VMEM((rows, stored), jnp.float32),
            pltpu.VMEM(weight.shape, jnp.bfloat16),
            pltpu.SemaphoreType.DMA((2, slots)),
            pltpu.SemaphoreType.DMA(()),
        ],
        compiler_params=params(20),
        cost_estimate=cost(16 * cache.size, 2 * cache.size, rows * stored),
        name="step_attend",
    )(lengths, query, entries, cache, weight)


def out_kernel(place, mine, sib, weight, sib_weight, *refs):
    out = refs[-1]
    half = out.shape[1]
    cols = pl.ds(pl.multiple_of(place[0] * half, half), half)
    part = jnp.dot(mine[...], weight[:, cols], preferred_element_type=jnp.float32)
    part += jnp.dot(sib[...], sib_weight[:, cols], preferred_element_type=jnp.float32)
    out[...] = part.astype(jnp.bfloat16)


def out_project(place, mine, sib, weight, sib_weight, after=()):
    rows, depth = mine.shape
    half = weight.shape[1] // 2
    return pl.pallas_call(
        out_kernel,
        out_shape=jax.ShapeDtypeStruct((rows, half), jnp.bfloat16),
        in_specs=[SMEM_WHOLE] + [VMEM_WHOLE] * 4 + [IN_PLACE] * len(after),
        out_specs=VMEM_WHOLE,
        compiler_params=params(8),
        cost_estimate=cost(4 * rows * depth * half, 4 * depth * half + 6 * rows * half),
        name="out_project",
    )(place, mine, sib, weight, sib_weight, *after)


def forward_kernel(split, chips, n_dec, n_after, chunk, place, *refs):
    refs = list(refs)
    mine, sib = refs[:2]
    shares = refs[2 : 2 + 2 * chips]
    refs = refs[2 + 2 * chips :]
    if n_dec:
        dec, dec_shares = refs[0], refs[1 : 1 + 2 * chips]
        refs = refs[1 + 2 * chips :]
    gain, *weights = refs[: 3 if split else 4]
    refs = refs[(3 if split else 4) + n_after :]
    if split:
        resid, hidden = refs[:2]
        held, inner, gate, up, arrived = refs[2:]
        down = ()
    else:
        keep, give, resid = refs[:3]
        refs = refs[3:]
        if n_dec:
            dec_out, dec_resid = refs[:2]
            refs = refs[2:]
        held, inner, hidden, gate, up, down, arrived = refs
    copies = [
        [
            pltpu.make_async_copy(
                source.at[:, pl.ds(i * chunk, chunk)], target.at[i], arrived.at[w, i]
            )
            for i in range(target.shape[0])
        ]
        for w, (source, target) in enumerate(zip(weights, [gate, up, down]))
    ]
    for pair in zip(copies[0], copies[1]):
        for copy in pair:
            copy.start()
    for rest in copies[2:]:
        for copy in rest:
            copy.start()
    piece = mine.shape[0]
    half = shares[0].shape[1]
    core = place[0]
    for rows, at_rows, put in ((mine, core, 0), (sib, 1 - core, piece)):
        here = pl.ds(pl.multiple_of(at_rows * piece, piece), piece)
        for side in range(2):
            at = core if side == 0 else 1 - core
            cols = pl.ds(pl.multiple_of(at * half, half), half)
            added = shares[side][here, :].astype(jnp.float32)
            for k in range(1, chips):
                added += shares[2 * k + side][here, :].astype(jnp.float32)
            value = rows[:, cols].astype(jnp.float32) + added
            held[put : put + piece, cols] = value.astype(jnp.bfloat16)
    if n_dec:
        added = dec_shares[0][...].astype(jnp.float32)
        for share in dec_shares[1:]:
            added += share[...].astype(jnp.float32)
        held[2 * piece :, :] = (dec[...].astype(jnp.float32) + added).astype(jnp.bfloat16)
    for put in range(0, held.shape[0], piece):
        here = slice(put, min(put + piece, held.shape[0]))
        inner[here, :] = normed(held[here, :].astype(jnp.float32), gain[...])
    resid[...] = held[:piece, :]
    if n_dec:
        dec_resid[...] = held[2 * piece :, :]

    for i in range(gate.shape[0]):
        at = slice(i * chunk, (i + 1) * chunk)
        copies[0][i].wait()
        gated = jnp.dot(inner[...], gate[i], preferred_element_type=jnp.float32)
        copies[1][i].wait()
        raised = jnp.dot(inner[...], up[i], preferred_element_type=jnp.float32)
        hidden[:, at] = (gated / (1.0 + jnp.exp(-gated)) * raised).astype(jnp.bfloat16)
    for i in range(0 if split else down.shape[0]):
        at = slice(i * chunk, (i + 1) * chunk)
        copies[2][i].wait()
        part = jnp.dot(hidden[...], down[i], preferred_element_type=jnp.float32)
        part = part.astype(jnp.bfloat16)
        keep[:, at] = part[:piece]
        give[:, at] = part[piece : 2 * piece]
        if n_dec:
            dec_out[:, at] = part[2 * piece :]


def lower_kernel(chunk, hidden, weight, *refs):
    keep, give, down, arrived = refs[-4:]
    piece = keep.shape[0]
    copies = [
        pltpu.make_async_copy(weight.at[:, pl.ds(i * chunk, chunk)], down.at[i], arrived.at[i])
        for i in range(down.shape[0])
    ]
    for copy in copies:
        copy.start()
    for i, copy in enumerate(copies):
        at = slice(i * chunk, (i + 1) * chunk)
        copy.wait()
        part = jnp.dot(hidden[...], down[i], preferred_element_type=jnp.float32)
        part = part.astype(jnp.bfloat16)
        keep[:, at] = part[:piece]
        give[:, at] = part[piece:]


def lower(hidden, weight, after):
    rows, units = hidden.shape
    width = weight.shape[1]
    chunk = width // 4
    return pl.pallas_call(
        functools.partial(lower_kernel, chunk),
        out_shape=[jax.ShapeDtypeStruct((rows // 2, width), jnp.bfloat16)] * 2,
        in_specs=[VMEM_WHOLE] + [IN_PLACE] * (1 + len(after)),
        out_specs=[VMEM_WHOLE] * 2,
        scratch_shapes=[
            pltpu.VMEM((4, units, chunk), jnp.bfloat16),
            pltpu.SemaphoreType.DMA((4,)),
        ],
        compiler_params=params(24),
        cost_estimate=cost(2 * rows * width * units, 2 * width * units),
        name="lower",
    )(hidden, weight, *after)


def feed_forward(
    place, mine, sib, shares, gain, gate, up, down=None, dec=None, dec_shares=None, after=()
):
    piece, width = mine.shape
    chips = len(shares) // 2
    units = gate.shape[1]
    chunks = 4
    chunk = width // chunks
    n_dec = 0 if dec is None else dec.shape[0]
    rows = 2 * piece + n_dec
    args = [mine, sib, *shares]
    if n_dec:
        args += [dec, *dec_shares]
    n_whole = len(args) + 1
    split = down is None
    args += [gain, gate, up] + [down] * (not split)
    if split:
        shapes = [(piece, width), (rows, units)]
    else:
        shapes = [(n, width) for n in [piece] * 3 + [n_dec] * 2 * bool(n_dec)]
    n_weights = 2 if split else 3
    return pl.pallas_call(
        functools.partial(forward_kernel, split, chips, n_dec, len(after), chunk),
        out_shape=[jax.ShapeDtypeStruct(shape, jnp.bfloat16) for shape in shapes],
        in_specs=[SMEM_WHOLE] + [VMEM_WHOLE] * n_whole + [IN_PLACE] * (n_weights + len(after)),
        out_specs=[VMEM_WHOLE] * len(shapes),
        scratch_shapes=[
            pltpu.VMEM((rows, width), jnp.bfloat16),
            pltpu.VMEM((rows, width), jnp.bfloat16),
        ]
        + [pltpu.VMEM((rows, units), jnp.bfloat16)] * (not split)
        + [pltpu.VMEM((units // chunk, width, chunk), jnp.bfloat16)] * 2
        + [pltpu.VMEM((chunks, units, chunk), jnp.bfloat16)] * (not split)
        + [pltpu.SemaphoreType.DMA((n_weights, chunks))],
        compiler_params=params(40),
        cost_estimate=cost(6 * rows * width * units, 6 * width * units, rows * units),
        name="feed_forward",
    )(place, *args, *after)


def angle_tables(places):
    halfway = HD // 2
    powers = jnp.arange(halfway, dtype=jnp.float32) * (2.0 / HD)
    inverse = THETA ** (-powers)
    angles = places.astype(jnp.float32)[:, None] * inverse[None, :]
    cosine, sine = jnp.cos(angles), jnp.sin(angles)
    return jnp.concatenate([cosine, cosine], axis=-1), jnp.concatenate([-sine, sine], axis=-1)


def add(*values):
    total = values[0].astype(jnp.float32)
    for value in values[1:]:
        total = total + value.astype(jnp.float32)
    return total.astype(jnp.bfloat16)


def on_device(
    prefill_rows,
    decode_rows,
    deal_order,
    prefill_offset,
    cache_length,
    prefill_cache,
    decode_cache,
    qkv_weight,
    out_weight,
    attention_gain,
    forward_gain,
    gate_weight,
    up_weight,
    down_weight,
):
    tensor_count = lax.axis_size("tensor")
    dp_count = lax.axis_size("dp")
    chips = tensor_count // 2
    tensor_place = lax.axis_index("tensor")
    group_place = lax.axis_index("dp")
    chip, core = tensor_place // 2, tensor_place % 2
    piece, width = prefill_rows.shape
    per_device = decode_rows.shape[0]
    requests = deal_order.shape[0]
    slots = cache_length.shape[0]
    padded = -(-slots // 16) * 16
    heads = qkv_weight.shape[1]
    tokens = piece * tensor_count

    def place_of(k):
        spots = [core, (chip + k) % chips, prefill_offset[0]]
        return jnp.stack(spots + [(chip + j) % chips for j in range(chips)]).astype(jnp.int32)

    places = [place_of(k) for k in range(chips)]
    weight = in_hbm(qkv_weight.reshape(width, -1))
    gate_weight, up_weight, down_weight = map(in_hbm, (gate_weight, up_weight, down_weight))
    prefill_cache, decode_cache = in_hbm(prefill_cache), in_hbm(decode_cache)

    mines = [prefill_rows] + [from_chip(prefill_rows, k) for k in range(1, chips)]
    sibs = [swap_cores(rows) for rows in mines]

    low = max(dp_count // 4, 1)
    pool = [decode_rows] + [swap_groups(decode_rows, i) for i in range(1, low)]
    pool = jnp.concatenate(pool, axis=0)
    pool = [pool] + [swap_groups(pool, i * low) for i in range(1, dp_count // low)]
    pool = jnp.concatenate(pool, axis=0)
    index = jnp.arange(dp_count * per_device, dtype=jnp.int32)
    origin = jnp.bitwise_xor(group_place, index // per_device)
    request = (origin * tensor_count + tensor_place) * per_device + index % per_device
    slot_of = jnp.sum(
        jnp.where(
            request[:, None] == jnp.arange(requests, dtype=jnp.int32)[None, :],
            deal_order[None, :],
            0,
        ),
        axis=1,
    )
    in_group = slot_of - group_place * slots
    chooser = (jnp.arange(padded, dtype=jnp.int32)[:, None] == in_group[None, :]) & (
        in_group[None, :] < slots
    )
    dealt = jnp.dot(
        chooser.astype(jnp.bfloat16), pool, preferred_element_type=jnp.float32
    ).astype(jnp.bfloat16)

    gain = attention_gain.reshape(1, width)
    tables = angle_tables(prefill_offset[0] + jnp.arange(tokens, dtype=jnp.int32))
    dec_tables = angle_tables(jnp.pad(cache_length, (0, padded - slots)))
    queries, entries, everything = [None] * chips, [None] * chips, None
    for k in range(chips):
        last = k == chips - 1
        if last:
            others = from_rest(dealt)
            if k:
                *others, queries[k - 1] = lax.optimization_barrier((*others, queries[k - 1]))
            dealt = add(dealt, *others)
        got = project(
            places[k],
            in_hbm(mines[k]),
            in_hbm(sibs[k]),
            gain,
            weight,
            tables,
            heads,
            everything,
            dealt if last else None,
            dec_tables if last else None,
            slots,
            [queries[k - 1]] if k else [dealt],
        )
        queries[k], entries[k], everything = got[:3]
        if last:
            dec_query, dec_entries = got[3:]

    out_share = out_weight
    sib_weight, queries[-1] = lax.optimization_barrier((out_weight, queries[-1]))
    sib_weight = in_vmem(swap_cores(sib_weight))
    out_weight = in_vmem(out_weight)

    def finish(attended, place, before):
        attended, *before = lax.optimization_barrier((attended, *before))
        sib = swap_cores(attended)
        return out_project(place, attended, sib, out_weight, sib_weight), before

    parts = []
    dec_shares = []
    for k in range(chips):
        attended = fill_attend(
            places[k], queries[k], prefill_cache, entries, heads, dec_shares[:1]
        )
        part, dec_shares[1:] = finish(attended, places[k], dec_shares[1:])
        parts.append(part)
        if k == 0:
            lengths, parts[0] = lax.optimization_barrier((cache_length, parts[0]))
            dec_part = step_attend(
                lengths, dec_query, dec_entries, decode_cache, in_hbm(out_share), heads
            )
            dec_shares = [dec_part, *from_rest(dec_part)]

    def shares_of(own, others):
        pairs = []
        for value in [own, *others]:
            pairs += [value, swap_cores(value)]
        return pairs

    gain = forward_gain.reshape(1, width)
    order = [*range(1, chips), 0]

    def fetch(b):
        return [from_chip(parts[(b - j) % chips], j) for j in range(1, chips)]

    theirs = fetch(order[0])
    arrived = []
    for n, b in enumerate(order):
        got = feed_forward(
            places[b],
            mines[b],
            sibs[b],
            shares_of(parts[b], theirs),
            gain,
            gate_weight,
            up_weight,
            down_weight if n + 1 < chips else None,
            dealt if n == 0 else None,
            dec_shares if n == 0 else None,
        )
        if n + 1 < chips:
            keep, give = got[:2]
            *theirs, keep = lax.optimization_barrier((*fetch(order[n + 1]), keep))
            both = add(keep, swap_cores(give))
            arrived.append(from_chip(both, chips - b))
        if n == 0:
            dec_sum, dec_resid = got[3:]
            dec_others = from_rest(dec_sum)
    resid, hidden = got
    dec_sum, hidden = lax.optimization_barrier((dec_sum, hidden))
    final = add(dec_resid, dec_sum, *dec_others)
    picker = in_group[:, None] == jnp.arange(padded, dtype=jnp.int32)[None, :]
    picker = picker & (in_group[:, None] < slots)
    routed = jnp.dot(
        picker.astype(jnp.bfloat16), final, preferred_element_type=jnp.float32
    ).astype(jnp.bfloat16)
    keep, give = lower(hidden, down_weight, [routed])
    low = max(dp_count // 4, 1)
    pairs = routed.reshape(dp_count // low, low * per_device, width)
    rows = add(
        pairs[0], *[swap_groups(pairs[i], i * low) for i in range(1, dp_count // low)]
    )
    *arrived, rows, give = lax.optimization_barrier((*arrived, rows, give))
    pairs = rows.reshape(low, per_device, width)
    routed = add(pairs[0], *[swap_groups(pairs[i], i) for i in range(1, low)])

    prefill_out = add(resid, keep, swap_cores(give), *arrived)
    return (prefill_out, routed, everything, dec_entries)


def solution(mesh):
    placed = (
        P(("dp", "tensor"), None),
        P(("dp", "tensor"), None),
        P(),
        P("dp"),
        P("dp"),
        P(None, "dp", None, "tensor"),
        P(None, "dp", None, "tensor"),
        P(None, "tensor", None),
        P("tensor", None),
        P(),
        P(),
        P(None, "tensor"),
        P(None, "tensor"),
        P("tensor", None),
    )
    return jax.shard_map(
        on_device,
        mesh=mesh,
        in_specs=placed,
        out_specs=(
            P(("dp", "tensor"), None),
            P(("dp", "tensor"), None),
            P(None, "dp", "tensor"),
            P(None, "dp", "tensor"),
        ),
        check_vma=False,
    )
```

```python
import functools
import math

import jax
import jax.numpy as jnp
from jax import lax
from jax.experimental import pallas as pl
from jax.experimental.pallas import tpu as pltpu
from jax.sharding import PartitionSpec as P

HD = 128
EPSILON = 1e-06
THETA = 1000000.0
NEGATIVE = -1e30
MIB = 1 << 20


def swap_cores(value):
    count = lax.axis_size("tensor")
    return lax.ppermute(value, "tensor", [(i, i ^ 1) for i in range(count)])


def from_chip(value, step):
    count = lax.axis_size("tensor")
    chips = count // 2
    return lax.ppermute(
        value, "tensor", [(i, (i // 2 - step) % chips * 2 + i % 2) for i in range(count)]
    )


def from_other(value, step):
    count = lax.axis_size("tensor")
    return lax.ppermute(
        value, "tensor", [(i, (i // 2 - step) % (count // 2) * 2 + 1 - i % 2) for i in range(count)]
    )


def from_rest(value):
    chips = lax.axis_size("tensor") // 2
    return [from_chip(value, k) for k in range(1, chips)] + [from_other(value, k) for k in range(chips)]


def swap_groups(value, mask):
    count = lax.axis_size("dp")
    return lax.ppermute(value, "dp", [(i, i ^ mask) for i in range(count)])


def whole(shape):
    return pl.BlockSpec(shape, lambda *_: (0,) * len(shape))


def params(mib):
    return pltpu.CompilerParams(vmem_limit_bytes=mib * MIB)


def cost(flops, moved, exps=0):
    return pl.CostEstimate(flops=int(flops), bytes_accessed=int(moved), transcendentals=int(exps))


def normed(values, gain):
    spread = jnp.mean(values * values, axis=-1, keepdims=True)
    return (values * lax.rsqrt(spread + EPSILON) * gain).astype(jnp.bfloat16)


def turn(vectors, cosine, sine):
    return vectors * cosine + pltpu.roll(vectors, HD // 2, 1) * sine


def in_vmem(value):
    return pltpu.with_memory_space_constraint(value, pltpu.VMEM)


def in_hbm(value):
    return pltpu.with_memory_space_constraint(value, pltpu.HBM)


VMEM_WHOLE = pl.BlockSpec(memory_space=pltpu.VMEM)
SMEM_WHOLE = pl.BlockSpec(memory_space=pltpu.SMEM)
IN_PLACE = pl.BlockSpec(memory_space=pl.ANY)


def project_kernel(groups, heads, place, mine, sib, weight, gain, cosine, sine, *refs):
    query, entries, everything, inner, rows_held, weight_held, row_sems, weight_sems, out_sem = refs[-9:]
    piece = mine.shape[0]
    core = place[0]
    scale = gain[...]
    depth = (groups + 2) * HD
    row_copies = [
        pltpu.make_async_copy(ref, rows_held.at[i], row_sems.at[i])
        for i, ref in enumerate((mine, sib))
    ]
    weight_copies = [
        pltpu.make_async_copy(
            weight.at[:, pl.ds(j * depth, depth)], weight_held.at[j], weight_sems.at[j]
        )
        for j in range(heads)
    ]
    for copy in row_copies + weight_copies:
        copy.start()
    for i, at in enumerate((core, 1 - core)):
        row_copies[i].wait()
        start = pl.multiple_of(at * piece, piece)
        inner[pl.ds(start, piece), :] = normed(rows_held[i].astype(jnp.float32), scale)
    here = pl.ds(pl.multiple_of(place[1] * 2 * piece, 2 * piece), 2 * piece)
    cos, sin = cosine[here, :], sine[here, :]
    for j in range(heads):
        weight_copies[j].wait()
        mixed = jnp.dot(inner[...], weight_held[j], preferred_element_type=jnp.float32)
        for g in range(groups):
            at = (j * groups + g) * HD
            part = mixed[:, g * HD : (g + 1) * HD]
            query[:, at : at + HD] = turn(part, cos, sin).astype(jnp.bfloat16)
        at = slice(j * HD, (j + 1) * HD)
        key = mixed[:, groups * HD : (groups + 1) * HD]
        entries[0, :, at] = turn(key, cos, sin).astype(jnp.bfloat16)
        entries[1, :, at] = mixed[:, (groups + 1) * HD :].astype(jnp.bfloat16)
    keep = pltpu.make_async_copy(entries, everything.at[:, here, :], out_sem)
    keep.start()
    keep.wait()


def project(place, mine, sib, gain, weight, tables, heads, everything, after=()):
    piece, width = mine.shape
    depth = weight.shape[1] // heads
    groups = depth // HD - 2
    block = 2 * piece
    args = [mine, sib, weight, gain, *tables]
    extra = list(after)
    aliases = {}
    if everything is not None:
        extra.append(everything)
        aliases = {len(args) + len(extra): 2}
    return pl.pallas_call(
        functools.partial(project_kernel, groups, heads),
        out_shape=[
            jax.ShapeDtypeStruct((block, heads * groups * HD), jnp.bfloat16),
            jax.ShapeDtypeStruct((2, block, heads * HD), jnp.bfloat16),
            jax.ShapeDtypeStruct((2, tables[0].shape[0], heads * HD), jnp.bfloat16),
        ],
        in_specs=[SMEM_WHOLE] + [IN_PLACE] * 3 + [VMEM_WHOLE] * 3 + [IN_PLACE] * len(extra),
        out_specs=[VMEM_WHOLE, VMEM_WHOLE, IN_PLACE],
        scratch_shapes=[
            pltpu.VMEM((block, width), jnp.bfloat16),
            pltpu.VMEM((2, piece, width), jnp.bfloat16),
            pltpu.VMEM((heads, width, depth), jnp.bfloat16),
            pltpu.SemaphoreType.DMA((2,)),
            pltpu.SemaphoreType.DMA((heads,)),
            pltpu.SemaphoreType.DMA(()),
        ],
        input_output_aliases=aliases,
        compiler_params=params(20),
        cost_estimate=cost(2 * block * weight.size, 2 * (weight.size + 2 * block * width)),
        name="project",
    )(place, *args, *extra)


def fill_kernel(groups, chips, place, query, cache_key, cache_value, *refs):
    new_keys, new_values, out = refs[:chips], refs[chips : 2 * chips], refs[-1]
    scaling = math.log2(math.e) / math.sqrt(HD)
    count = query.shape[0]
    stored = cache_key.shape[2]
    old_seen = lax.broadcasted_iota(jnp.int32, (1, stored), 1) < place[2]
    ahead = lax.broadcasted_iota(jnp.int32, (count, count), 1) - lax.broadcasted_iota(
        jnp.int32, (count, count), 0
    )
    across = (((1,), (1,)), ((), ()))
    for g in range(groups):
        rows = query[:, g * HD : (g + 1) * HD]
        scores = lax.dot_general(rows, cache_key[0, 0], across, preferred_element_type=jnp.float32)
        scores = [jnp.where(old_seen, scores * scaling, NEGATIVE)]
        for k in range(chips):
            fresh = lax.dot_general(
                rows, new_keys[k][0], across, preferred_element_type=jnp.float32
            )
            gap = (place[1] - place[3 + k]) * count
            scores.append(jnp.where(ahead <= gap, fresh * scaling, NEGATIVE))
        top = jnp.max(scores[0], axis=-1, keepdims=True)
        for part in scores[1:]:
            top = jnp.maximum(top, jnp.max(part, axis=-1, keepdims=True))
        mix, total = 0.0, 0.0
        for part, values in zip(scores, [cache_value[0, 0], *[v[0] for v in new_values]]):
            weights = jnp.exp2(part - top)
            total += jnp.sum(weights, axis=-1, keepdims=True)
            mix += jnp.dot(weights.astype(jnp.bfloat16), values, preferred_element_type=jnp.float32)
        out[:, g * HD : (g + 1) * HD] = (mix / total).astype(jnp.bfloat16)


def fill_attend(place, query, cache, entries, heads, after=()):
    count = query.shape[0]
    groups = query.shape[1] // heads // HD
    stored = cache.shape[2]
    chips = len(entries)
    pairs = count * groups * heads * (stored + chips * count)
    return pl.pallas_call(
        functools.partial(fill_kernel, groups, chips),
        out_shape=jax.ShapeDtypeStruct(query.shape, jnp.bfloat16),
        grid_spec=pltpu.PrefetchScalarGridSpec(
            num_scalar_prefetch=1,
            grid=(heads,),
            in_specs=[
                pl.BlockSpec((count, groups * HD), lambda j, s: (0, j)),
                pl.BlockSpec((1, 1, stored, HD), lambda j, s: (0, 0, 0, j)),
                pl.BlockSpec((1, 1, stored, HD), lambda j, s: (1, 0, 0, j)),
            ]
            + [pl.BlockSpec((1, count, HD), lambda j, s: (0, 0, j))] * chips
            + [pl.BlockSpec((1, count, HD), lambda j, s: (1, 0, j))] * chips
            + [IN_PLACE] * len(after),
            out_specs=pl.BlockSpec((count, groups * HD), lambda j, s: (0, j)),
        ),
        compiler_params=params(16),
        cost_estimate=cost(8 * pairs * HD, 2 * cache.size, pairs),
        name="fill_attend",
    )(place, query, cache, cache, *entries, *entries, *after)


def step_kernel(heads, pieces, lengths, gain, cosine, sine, *refs):
    dealt_parts, refs = refs[:pieces], refs[pieces:]
    qkv, cache, weight, out, dealt, entries = refs[:6]
    held, scores, shares, qkv_held, weight_held, arrived, qkv_sems, weight_sem = refs[6:]
    scaling = 1.0 / math.sqrt(HD)
    slots, stored, width = cache.shape[1:]
    depth = qkv.shape[1] // heads
    groups = depth // HD - 2
    lanes = 8
    qkv_copies = [
        pltpu.make_async_copy(qkv.at[:, pl.ds(j * depth, depth)], qkv_held.at[j], qkv_sems.at[j])
        for j in range(heads)
    ]
    copies = [
        [pltpu.make_async_copy(cache.at[w, s], held.at[w, s], arrived.at[w, s]) for s in range(slots)]
        for w in range(2)
    ]
    weight_copy = pltpu.make_async_copy(weight, weight_held, weight_sem)
    for copy in qkv_copies + copies[0] + copies[1] + [weight_copy]:
        copy.start()
    rows = dealt_parts[0][...].astype(jnp.float32)
    for part in dealt_parts[1:]:
        rows += part[...].astype(jnp.float32)
    dealt[...] = rows.astype(jnp.bfloat16)
    inner = normed(rows, gain[...])
    cos, sin = cosine[...], sine[...]
    queries, new_keys, new_values = [], [], []
    for j in range(heads):
        qkv_copies[j].wait()
        mixed = jnp.dot(inner, qkv_held[j], preferred_element_type=jnp.float32)
        for g in range(groups):
            part = turn(mixed[:, g * HD : (g + 1) * HD], cos, sin)
            queries.append(part.astype(jnp.bfloat16).astype(jnp.float32))
        at = slice(j * HD, (j + 1) * HD)
        key = turn(mixed[:, groups * HD : (groups + 1) * HD], cos, sin).astype(jnp.bfloat16)
        value = mixed[:, (groups + 1) * HD :].astype(jnp.bfloat16)
        entries[0, :, at] = key[:slots]
        entries[1, :, at] = value[:slots]
        new_keys.append(key.astype(jnp.float32))
        new_values.append(value.astype(jnp.float32))
    new_keys = jnp.concatenate(new_keys, axis=1)
    new_values = jnp.concatenate(new_values, axis=1)
    across = (((1,), (1,)), ((), ()))
    places = lax.broadcasted_iota(jnp.int32, (1, stored), 1)
    blank = jnp.zeros((1, HD), jnp.float32)
    own_scores = []
    for s in range(slots):
        rows = []
        for j in range(heads):
            for g in range(groups):
                part = queries[j * groups + g][s : s + 1]
                rows.append(
                    jnp.concatenate([part if i == j else blank for i in range(heads)], axis=1)
                )
        rows.append(jnp.zeros((lanes - heads * groups, width), jnp.float32))
        rows = jnp.concatenate(rows, axis=0)
        own_scores.append(jnp.sum(rows * new_keys[s : s + 1], axis=-1, keepdims=True))
        copies[0][s].wait()
        old = lax.dot_general(
            rows.astype(jnp.bfloat16), held[0, s], across, preferred_element_type=jnp.float32
        )
        scores[s * lanes : (s + 1) * lanes, :] = jnp.where(
            places < lengths[s], old * scaling, NEGATIVE
        )
    old = scores[...]
    own = jnp.concatenate(own_scores, axis=0) * scaling
    top = jnp.maximum(jnp.max(old, axis=-1, keepdims=True), own)
    old = jnp.exp(old - top)
    own = jnp.exp(own - top)
    total = jnp.sum(old, axis=-1, keepdims=True) + own
    shares[...] = old / total
    own = (own / total).astype(jnp.bfloat16).astype(jnp.float32)
    attended = []
    for s in range(slots):
        copies[1][s].wait()
        here = slice(s * lanes, (s + 1) * lanes)
        mix = jnp.dot(
            shares[here, :].astype(jnp.bfloat16), held[1, s], preferred_element_type=jnp.float32
        )
        mix += own[here] * new_values[s : s + 1]
        parts = []
        for j in range(heads):
            for g in range(groups):
                row = j * groups + g
                parts.append(mix[row : row + 1, j * HD : (j + 1) * HD])
        attended.append(jnp.concatenate(parts, axis=1))
    if out.shape[0] > slots:
        attended.append(jnp.zeros((out.shape[0] - slots, groups * width), jnp.float32))
    attended = jnp.concatenate(attended, axis=0).astype(jnp.bfloat16)
    weight_copy.wait()
    part = jnp.dot(attended, weight_held[...], preferred_element_type=jnp.float32)
    out[...] = part.astype(jnp.bfloat16)


def step_attend(lengths, dealt_parts, gain, tables, qkv, cache, weight, heads):
    slots, stored, width = cache.shape[1:]
    padded, model = dealt_parts[0].shape
    rows = slots * 8
    pieces = len(dealt_parts)
    return pl.pallas_call(
        functools.partial(step_kernel, heads, pieces),
        out_shape=[
            jax.ShapeDtypeStruct((padded, model), jnp.bfloat16),
            jax.ShapeDtypeStruct((padded, model), jnp.bfloat16),
            jax.ShapeDtypeStruct((2, slots, width), jnp.bfloat16),
        ],
        in_specs=[SMEM_WHOLE] + [VMEM_WHOLE] * (3 + pieces) + [IN_PLACE] * 3,
        out_specs=[VMEM_WHOLE] * 3,
        scratch_shapes=[
            pltpu.VMEM(cache.shape, jnp.bfloat16),
            pltpu.VMEM((rows, stored), jnp.float32),
            pltpu.VMEM((rows, stored), jnp.float32),
            pltpu.VMEM((heads, model, qkv.shape[1] // heads), jnp.bfloat16),
            pltpu.VMEM(weight.shape, jnp.bfloat16),
            pltpu.SemaphoreType.DMA((2, slots)),
            pltpu.SemaphoreType.DMA((heads,)),
            pltpu.SemaphoreType.DMA(()),
        ],
        compiler_params=params(24),
        cost_estimate=cost(16 * cache.size, 3 * cache.size, rows * stored),
        name="step_attend",
    )(lengths, gain, *tables, *dealt_parts, qkv, cache, weight)


def out_kernel(place, mine, sib, weight, sib_weight, *refs):
    out = refs[-1]
    half = out.shape[1]
    cols = pl.ds(pl.multiple_of(place[0] * half, half), half)
    part = jnp.dot(mine[...], weight[:, cols], preferred_element_type=jnp.float32)
    part += jnp.dot(sib[...], sib_weight[:, cols], preferred_element_type=jnp.float32)
    out[...] = part.astype(jnp.bfloat16)


def out_project(place, mine, sib, weight, sib_weight, after=()):
    rows, depth = mine.shape
    half = weight.shape[1] // 2
    return pl.pallas_call(
        out_kernel,
        out_shape=jax.ShapeDtypeStruct((rows, half), jnp.bfloat16),
        in_specs=[SMEM_WHOLE] + [VMEM_WHOLE] * 4 + [IN_PLACE] * len(after),
        out_specs=VMEM_WHOLE,
        compiler_params=params(8),
        cost_estimate=cost(4 * rows * depth * half, 4 * depth * half + 6 * rows * half),
        name="out_project",
    )(place, mine, sib, weight, sib_weight, *after)


def forward_kernel(split, chips, n_dec, n_after, chunk, place, *refs):
    refs = list(refs)
    mine, sib = refs[:2]
    shares = refs[2 : 2 + 2 * chips]
    refs = refs[2 + 2 * chips :]
    if n_dec:
        dec, dec_shares = refs[0], refs[1 : 1 + 2 * chips]
        refs = refs[1 + 2 * chips :]
    gain, *weights = refs[: 3 if split else 4]
    refs = refs[(3 if split else 4) + n_after :]
    if split:
        resid, hidden = refs[:2]
        held, inner, gate, up, arrived = refs[2:]
        down = ()
    else:
        keep, give, resid = refs[:3]
        refs = refs[3:]
        if n_dec:
            dec_out, dec_resid = refs[:2]
            refs = refs[2:]
        held, inner, hidden, gate, up, down, arrived = refs
    copies = [
        [
            pltpu.make_async_copy(
                source.at[:, pl.ds(i * chunk, chunk)], target.at[i], arrived.at[w, i]
            )
            for i in range(target.shape[0])
        ]
        for w, (source, target) in enumerate(zip(weights, [gate, up, down]))
    ]
    for pair in zip(copies[0], copies[1]):
        for copy in pair:
            copy.start()
    for rest in copies[2:]:
        for copy in rest:
            copy.start()
    piece = mine.shape[0]
    half = shares[0].shape[1]
    core = place[0]
    for rows, at_rows, put in ((mine, core, 0), (sib, 1 - core, piece)):
        here = pl.ds(pl.multiple_of(at_rows * piece, piece), piece)
        for side in range(2):
            at = core if side == 0 else 1 - core
            cols = pl.ds(pl.multiple_of(at * half, half), half)
            added = shares[side][here, :].astype(jnp.float32)
            for k in range(1, chips):
                added += shares[2 * k + side][here, :].astype(jnp.float32)
            value = rows[:, cols].astype(jnp.float32) + added
            held[put : put + piece, cols] = value.astype(jnp.bfloat16)
    if n_dec:
        added = dec_shares[0][...].astype(jnp.float32)
        for share in dec_shares[1:]:
            added += share[...].astype(jnp.float32)
        held[2 * piece :, :] = (dec[...].astype(jnp.float32) + added).astype(jnp.bfloat16)
    for put in range(0, held.shape[0], piece):
        here = slice(put, min(put + piece, held.shape[0]))
        inner[here, :] = normed(held[here, :].astype(jnp.float32), gain[...])
    resid[...] = held[:piece, :]
    if n_dec:
        dec_resid[...] = held[2 * piece :, :]

    for i in range(gate.shape[0]):
        at = slice(i * chunk, (i + 1) * chunk)
        copies[0][i].wait()
        gated = jnp.dot(inner[...], gate[i], preferred_element_type=jnp.float32)
        copies[1][i].wait()
        raised = jnp.dot(inner[...], up[i], preferred_element_type=jnp.float32)
        hidden[:, at] = (gated / (1.0 + jnp.exp(-gated)) * raised).astype(jnp.bfloat16)
    for i in range(0 if split else down.shape[0]):
        at = slice(i * chunk, (i + 1) * chunk)
        copies[2][i].wait()
        part = jnp.dot(hidden[...], down[i], preferred_element_type=jnp.float32)
        part = part.astype(jnp.bfloat16)
        keep[:, at] = part[:piece]
        give[:, at] = part[piece : 2 * piece]
        if n_dec:
            dec_out[:, at] = part[2 * piece :]


def lower_kernel(chunk, hidden, weight, *refs):
    keep, give, down, arrived = refs[-4:]
    piece = keep.shape[0]
    copies = [
        pltpu.make_async_copy(weight.at[:, pl.ds(i * chunk, chunk)], down.at[i], arrived.at[i])
        for i in range(down.shape[0])
    ]
    for copy in copies:
        copy.start()
    for i, copy in enumerate(copies):
        at = slice(i * chunk, (i + 1) * chunk)
        copy.wait()
        part = jnp.dot(hidden[...], down[i], preferred_element_type=jnp.float32)
        part = part.astype(jnp.bfloat16)
        keep[:, at] = part[:piece]
        give[:, at] = part[piece:]


def lower(hidden, weight, after):
    rows, units = hidden.shape
    width = weight.shape[1]
    chunk = 256
    return pl.pallas_call(
        functools.partial(lower_kernel, chunk),
        out_shape=[jax.ShapeDtypeStruct((rows // 2, width), jnp.bfloat16)] * 2,
        in_specs=[VMEM_WHOLE] + [IN_PLACE] * (1 + len(after)),
        out_specs=[VMEM_WHOLE] * 2,
        scratch_shapes=[
            pltpu.VMEM((width // chunk, units, chunk), jnp.bfloat16),
            pltpu.SemaphoreType.DMA((width // chunk,)),
        ],
        compiler_params=params(24),
        cost_estimate=cost(2 * rows * width * units, 2 * width * units),
        name="lower",
    )(hidden, weight, *after)


def feed_forward(
    place, mine, sib, shares, gain, gate, up, down=None, dec=None, dec_shares=None, after=()
):
    piece, width = mine.shape
    chips = len(shares) // 2
    units = gate.shape[1]
    chunk = 256
    n_dec = 0 if dec is None else dec.shape[0]
    rows = 2 * piece + n_dec
    args = [mine, sib, *shares]
    if n_dec:
        args += [dec, *dec_shares]
    n_whole = len(args) + 1
    split = down is None
    args += [gain, gate, up] + [down] * (not split)
    if split:
        shapes = [(piece, width), (rows, units)]
    else:
        shapes = [(n, width) for n in [piece] * 3 + [n_dec] * 2 * bool(n_dec)]
    n_weights = 2 if split else 3
    return pl.pallas_call(
        functools.partial(forward_kernel, split, chips, n_dec, len(after), chunk),
        out_shape=[jax.ShapeDtypeStruct(shape, jnp.bfloat16) for shape in shapes],
        in_specs=[SMEM_WHOLE] + [VMEM_WHOLE] * n_whole + [IN_PLACE] * (n_weights + len(after)),
        out_specs=[VMEM_WHOLE] * len(shapes),
        scratch_shapes=[
            pltpu.VMEM((rows, width), jnp.bfloat16),
            pltpu.VMEM((rows, width), jnp.bfloat16),
        ]
        + [pltpu.VMEM((rows, units), jnp.bfloat16)] * (not split)
        + [pltpu.VMEM((units // chunk, width, chunk), jnp.bfloat16)] * 2
        + [pltpu.VMEM((width // chunk, units, chunk), jnp.bfloat16)] * (not split)
        + [pltpu.SemaphoreType.DMA((n_weights, max(units, width) // chunk))],
        compiler_params=params(40),
        cost_estimate=cost(6 * rows * width * units, 6 * width * units, rows * units),
        name="feed_forward",
    )(place, *args, *after)


def angle_tables(places):
    halfway = HD // 2
    powers = jnp.arange(halfway, dtype=jnp.float32) * (2.0 / HD)
    inverse = THETA ** (-powers)
    angles = places.astype(jnp.float32)[:, None] * inverse[None, :]
    cosine, sine = jnp.cos(angles), jnp.sin(angles)
    return jnp.concatenate([cosine, cosine], axis=-1), jnp.concatenate([-sine, sine], axis=-1)


def add(*values):
    total = values[0].astype(jnp.float32)
    for value in values[1:]:
        total = total + value.astype(jnp.float32)
    return total.astype(jnp.bfloat16)


def on_device(
    prefill_rows,
    decode_rows,
    deal_order,
    prefill_offset,
    cache_length,
    prefill_cache,
    decode_cache,
    qkv_weight,
    out_weight,
    attention_gain,
    forward_gain,
    gate_weight,
    up_weight,
    down_weight,
):
    tensor_count = lax.axis_size("tensor")
    dp_count = lax.axis_size("dp")
    chips = tensor_count // 2
    tensor_place = lax.axis_index("tensor")
    group_place = lax.axis_index("dp")
    chip, core = tensor_place // 2, tensor_place % 2
    piece, width = prefill_rows.shape
    per_device = decode_rows.shape[0]
    requests = deal_order.shape[0]
    slots = cache_length.shape[0]
    padded = -(-slots // 16) * 16
    heads = qkv_weight.shape[1]
    tokens = piece * tensor_count

    def place_of(k):
        spots = [core, (chip + k) % chips, prefill_offset[0]]
        return jnp.stack(spots + [(chip + j) % chips for j in range(chips)]).astype(jnp.int32)

    places = [place_of(k) for k in range(chips)]
    weight = in_hbm(qkv_weight.reshape(width, -1))
    gate_weight, up_weight, down_weight = map(in_hbm, (gate_weight, up_weight, down_weight))
    prefill_cache, decode_cache = in_hbm(prefill_cache), in_hbm(decode_cache)

    mines = [prefill_rows] + [from_chip(prefill_rows, k) for k in range(1, chips)]
    sibs = [swap_cores(prefill_rows)]

    low = max(dp_count // 4, 1)
    pool = [decode_rows] + [swap_groups(decode_rows, i) for i in range(1, low)]
    pool = near = jnp.concatenate(pool, axis=0)
    pool = [pool] + [swap_groups(pool, i * low) for i in range(1, dp_count // low)]
    pool = jnp.concatenate(pool, axis=0)
    index = jnp.arange(dp_count * per_device, dtype=jnp.int32)
    origin = jnp.bitwise_xor(group_place, index // per_device)
    request = (origin * tensor_count + tensor_place) * per_device + index % per_device
    slot_of = jnp.sum(
        jnp.where(
            request[:, None] == jnp.arange(requests, dtype=jnp.int32)[None, :],
            deal_order[None, :],
            0,
        ),
        axis=1,
    )
    in_group = slot_of - group_place * slots
    chooser = (jnp.arange(padded, dtype=jnp.int32)[:, None] == in_group[None, :]) & (
        in_group[None, :] < slots
    )
    dealt = jnp.dot(
        chooser.astype(jnp.bfloat16), pool, preferred_element_type=jnp.float32
    ).astype(jnp.bfloat16)

    gain = attention_gain.reshape(1, width)
    tables = angle_tables(prefill_offset[0] + jnp.arange(tokens, dtype=jnp.int32))
    dec_tables = angle_tables(jnp.pad(cache_length, (0, padded - slots)))
    queries, entries, everything = [], [], None
    for k in range(chips):
        query, entry, everything = project(
            places[k],
            in_hbm(mines[k]),
            in_hbm(sibs[k]),
            gain,
            weight,
            tables,
            heads,
            everything,
            [query] if k else [near],
        )
        if k == 0:
            *mines[1:], query = lax.optimization_barrier((*mines[1:], query))
            sibs += [swap_cores(rows) for rows in mines[1:]]
        queries.append(query)
        entries.append(entry)
    dealt_parts = [dealt, *from_rest(dealt)]

    out_share = out_weight
    sib_weight, queries[-1] = lax.optimization_barrier((out_weight, queries[-1]))
    sib_weight = in_vmem(swap_cores(sib_weight))
    out_weight = in_vmem(out_weight)

    def finish(attended, place, before):
        attended, *before = lax.optimization_barrier((attended, *before))
        sib = swap_cores(attended)
        return out_project(place, attended, sib, out_weight, sib_weight), before

    parts = []
    dec_shares = []
    for k in range(chips):
        after = dec_shares[:1] if k else dealt_parts[:1]
        attended = fill_attend(places[k], queries[k], prefill_cache, entries, heads, after)
        if k == 0:
            part, dealt_parts[1:] = finish(attended, places[k], dealt_parts[1:])
        else:
            part, dec_shares[1:] = finish(attended, places[k], dec_shares[1:])
        parts.append(part)
        if k == 0:
            lengths, parts[0] = lax.optimization_barrier((cache_length, parts[0]))
            dec_part, dealt, dec_entries = step_attend(
                lengths,
                dealt_parts,
                gain,
                dec_tables,
                weight,
                decode_cache,
                in_hbm(out_share),
                heads,
            )
            dec_shares = [dec_part, *from_rest(dec_part)]

    def shares_of(own, others):
        pairs = []
        for value in [own, *others]:
            pairs += [value, swap_cores(value)]
        return pairs

    gain = forward_gain.reshape(1, width)
    order = [*range(1, chips), 0]

    def fetch(b):
        return [from_chip(parts[(b - j) % chips], j) for j in range(1, chips)]

    theirs = fetch(order[0])
    arrived = []
    for n, b in enumerate(order):
        got = feed_forward(
            places[b],
            mines[b],
            sibs[b],
            shares_of(parts[b], theirs),
            gain,
            gate_weight,
            up_weight,
            down_weight if n + 1 < chips else None,
            dealt if n == 0 else None,
            dec_shares if n == 0 else None,
        )
        if n + 1 < chips:
            keep, give = got[:2]
            *theirs, keep = lax.optimization_barrier((*fetch(order[n + 1]), keep))
            both = add(keep, swap_cores(give))
            arrived.append(from_chip(both, chips - b))
        if n == 0:
            dec_sum, dec_resid = got[3:]
            dec_others = from_rest(dec_sum)
    resid, hidden = got
    dec_sum, hidden = lax.optimization_barrier((dec_sum, hidden))
    final = add(dec_resid, dec_sum, *dec_others)
    picker = in_group[:, None] == jnp.arange(padded, dtype=jnp.int32)[None, :]
    picker = picker & (in_group[:, None] < slots)
    routed = jnp.dot(
        picker.astype(jnp.bfloat16), final, preferred_element_type=jnp.float32
    ).astype(jnp.bfloat16)
    keep, give = lower(hidden, down_weight, [routed])
    low = max(dp_count // 4, 1)
    pairs = routed.reshape(dp_count // low, low * per_device, width)
    rows = add(
        pairs[0], *[swap_groups(pairs[i], i * low) for i in range(1, dp_count // low)]
    )
    *arrived, rows, give = lax.optimization_barrier((*arrived, rows, give))
    pairs = rows.reshape(low, per_device, width)
    routed = add(pairs[0], *[swap_groups(pairs[i], i) for i in range(1, low)])

    prefill_out = add(resid, keep, swap_cores(give), *arrived)
    return (prefill_out, routed, everything, dec_entries)


def solution(mesh):
    placed = (
        P(("dp", "tensor"), None),
        P(("dp", "tensor"), None),
        P(),
        P("dp"),
        P("dp"),
        P(None, "dp", None, "tensor"),
        P(None, "dp", None, "tensor"),
        P(None, "tensor", None),
        P("tensor", None),
        P(),
        P(),
        P(None, "tensor"),
        P(None, "tensor"),
        P("tensor", None),
    )
    return jax.shard_map(
        on_device,
        mesh=mesh,
        in_specs=placed,
        out_specs=(
            P(("dp", "tensor"), None),
            P(("dp", "tensor"), None),
            P(None, "dp", "tensor"),
            P(None, "dp", "tensor"),
        ),
        check_vma=False,
    )
```

```python
import functools
import math

import jax
import jax.numpy as jnp
from jax import lax
from jax.experimental import pallas as pl
from jax.experimental.pallas import tpu as pltpu
from jax.sharding import PartitionSpec as P

HD = 128
EPSILON = 1e-06
THETA = 1000000.0
NEGATIVE = -1e30
MIB = 1 << 20


def swap_cores(value):
    count = lax.axis_size("tensor")
    return lax.ppermute(value, "tensor", [(i, i ^ 1) for i in range(count)])


def from_chip(value, step):
    count = lax.axis_size("tensor")
    chips = count // 2
    return lax.ppermute(
        value, "tensor", [(i, (i // 2 - step) % chips * 2 + i % 2) for i in range(count)]
    )


def from_other(value, step):
    count = lax.axis_size("tensor")
    return lax.ppermute(
        value, "tensor", [(i, (i // 2 - step) % (count // 2) * 2 + 1 - i % 2) for i in range(count)]
    )


def from_rest(value):
    chips = lax.axis_size("tensor") // 2
    return [from_chip(value, k) for k in range(1, chips)] + [from_other(value, k) for k in range(chips)]


def swap_groups(value, mask):
    count = lax.axis_size("dp")
    return lax.ppermute(value, "dp", [(i, i ^ mask) for i in range(count)])


def whole(shape):
    return pl.BlockSpec(shape, lambda *_: (0,) * len(shape))


def params(mib):
    return pltpu.CompilerParams(vmem_limit_bytes=mib * MIB)


def cost(flops, moved, exps=0):
    return pl.CostEstimate(flops=int(flops), bytes_accessed=int(moved), transcendentals=int(exps))


def normed(values, gain):
    spread = jnp.mean(values * values, axis=-1, keepdims=True)
    return (values * lax.rsqrt(spread + EPSILON) * gain).astype(jnp.bfloat16)


def turn(vectors, cosine, sine):
    return vectors * cosine + pltpu.roll(vectors, HD // 2, 1) * sine


def in_vmem(value):
    return pltpu.with_memory_space_constraint(value, pltpu.VMEM)


def in_hbm(value):
    return pltpu.with_memory_space_constraint(value, pltpu.HBM)


VMEM_WHOLE = pl.BlockSpec(memory_space=pltpu.VMEM)
SMEM_WHOLE = pl.BlockSpec(memory_space=pltpu.SMEM)
IN_PLACE = pl.BlockSpec(memory_space=pl.ANY)


def project_kernel(groups, heads, place, mine, sib, weight, gain, cosine, sine, *refs):
    query, entries, everything, inner, rows_held, weight_held, row_sems, weight_sem, out_sem = refs[-9:]
    piece = mine.shape[0]
    core = place[0]
    scale = gain[...]
    depth = (groups + 2) * HD
    row_copies = [
        pltpu.make_async_copy(ref, rows_held.at[i], row_sems.at[i])
        for i, ref in enumerate((mine, sib))
    ]
    weight_copy = pltpu.make_async_copy(weight, weight_held, weight_sem)
    for copy in row_copies + [weight_copy]:
        copy.start()
    for i, at in enumerate((core, 1 - core)):
        row_copies[i].wait()
        start = pl.multiple_of(at * piece, piece)
        inner[pl.ds(start, piece), :] = normed(rows_held[i].astype(jnp.float32), scale)
    here = pl.ds(pl.multiple_of(place[1] * 2 * piece, 2 * piece), 2 * piece)
    cos, sin = cosine[here, :], sine[here, :]
    weight_copy.wait()
    product = jnp.dot(inner[...], weight_held[...], preferred_element_type=jnp.float32)
    for j in range(heads):
        mixed = product[:, j * depth : (j + 1) * depth]
        for g in range(groups):
            at = (j * groups + g) * HD
            part = mixed[:, g * HD : (g + 1) * HD]
            query[:, at : at + HD] = turn(part, cos, sin).astype(jnp.bfloat16)
        at = slice(j * HD, (j + 1) * HD)
        key = mixed[:, groups * HD : (groups + 1) * HD]
        entries[0, :, at] = turn(key, cos, sin).astype(jnp.bfloat16)
        entries[1, :, at] = mixed[:, (groups + 1) * HD :].astype(jnp.bfloat16)
    keep = pltpu.make_async_copy(entries, everything.at[:, here, :], out_sem)
    keep.start()
    keep.wait()


def project(place, mine, sib, gain, weight, tables, heads, everything, after=()):
    piece, width = mine.shape
    depth = weight.shape[1] // heads
    groups = depth // HD - 2
    block = 2 * piece
    args = [mine, sib, weight, gain, *tables]
    extra = list(after)
    aliases = {}
    if everything is not None:
        extra.append(everything)
        aliases = {len(args) + len(extra): 2}
    return pl.pallas_call(
        functools.partial(project_kernel, groups, heads),
        out_shape=[
            jax.ShapeDtypeStruct((block, heads * groups * HD), jnp.bfloat16),
            jax.ShapeDtypeStruct((2, block, heads * HD), jnp.bfloat16),
            jax.ShapeDtypeStruct((2, tables[0].shape[0], heads * HD), jnp.bfloat16),
        ],
        in_specs=[SMEM_WHOLE] + [IN_PLACE] * 3 + [VMEM_WHOLE] * 3 + [IN_PLACE] * len(extra),
        out_specs=[VMEM_WHOLE, VMEM_WHOLE, IN_PLACE],
        scratch_shapes=[
            pltpu.VMEM((block, width), jnp.bfloat16),
            pltpu.VMEM((2, piece, width), jnp.bfloat16),
            pltpu.VMEM(weight.shape, jnp.bfloat16),
            pltpu.SemaphoreType.DMA((2,)),
            pltpu.SemaphoreType.DMA(()),
            pltpu.SemaphoreType.DMA(()),
        ],
        input_output_aliases=aliases,
        compiler_params=params(20),
        cost_estimate=cost(2 * block * weight.size, 2 * (weight.size + 2 * block * width)),
        name="project",
    )(place, *args, *extra)


def fill_kernel(groups, chips, place, query, cache_key, cache_value, *refs):
    new_keys, new_values, out = refs[:chips], refs[chips : 2 * chips], refs[-1]
    scaling = math.log2(math.e) / math.sqrt(HD)
    count = query.shape[0]
    stored = cache_key.shape[2]
    old_seen = lax.broadcasted_iota(jnp.int32, (1, stored), 1) < place[2]
    ahead = lax.broadcasted_iota(jnp.int32, (count, count), 1) - lax.broadcasted_iota(
        jnp.int32, (count, count), 0
    )
    across = (((1,), (1,)), ((), ()))
    for g in range(groups):
        rows = query[:, g * HD : (g + 1) * HD]
        scores = lax.dot_general(rows, cache_key[0, 0], across, preferred_element_type=jnp.float32)
        scores = [jnp.where(old_seen, scores * scaling, NEGATIVE)]
        for k in range(chips):
            fresh = lax.dot_general(
                rows, new_keys[k][0], across, preferred_element_type=jnp.float32
            )
            gap = (place[1] - place[3 + k]) * count
            scores.append(jnp.where(ahead <= gap, fresh * scaling, NEGATIVE))
        top = jnp.max(scores[0], axis=-1, keepdims=True)
        for part in scores[1:]:
            top = jnp.maximum(top, jnp.max(part, axis=-1, keepdims=True))
        mix, total = 0.0, 0.0
        for part, values in zip(scores, [cache_value[0, 0], *[v[0] for v in new_values]]):
            weights = jnp.exp2(part - top)
            total += jnp.sum(weights, axis=-1, keepdims=True)
            mix += jnp.dot(weights.astype(jnp.bfloat16), values, preferred_element_type=jnp.float32)
        out[:, g * HD : (g + 1) * HD] = (mix / total).astype(jnp.bfloat16)


def fill_attend(place, query, cache, entries, heads, after=()):
    count = query.shape[0]
    groups = query.shape[1] // heads // HD
    stored = cache.shape[2]
    chips = len(entries)
    pairs = count * groups * heads * (stored + chips * count)
    return pl.pallas_call(
        functools.partial(fill_kernel, groups, chips),
        out_shape=jax.ShapeDtypeStruct(query.shape, jnp.bfloat16),
        grid_spec=pltpu.PrefetchScalarGridSpec(
            num_scalar_prefetch=1,
            grid=(heads,),
            in_specs=[
                pl.BlockSpec((count, groups * HD), lambda j, s: (0, j)),
                pl.BlockSpec((1, 1, stored, HD), lambda j, s: (0, 0, 0, j)),
                pl.BlockSpec((1, 1, stored, HD), lambda j, s: (1, 0, 0, j)),
            ]
            + [pl.BlockSpec((1, count, HD), lambda j, s: (0, 0, j))] * chips
            + [pl.BlockSpec((1, count, HD), lambda j, s: (1, 0, j))] * chips
            + [IN_PLACE] * len(after),
            out_specs=pl.BlockSpec((count, groups * HD), lambda j, s: (0, j)),
        ),
        compiler_params=params(12),
        cost_estimate=cost(8 * pairs * HD, 2 * cache.size, pairs),
        name="fill_attend",
    )(place, query, cache, cache, *entries, *entries, *after)


def step_kernel(heads, pieces, lengths, gain, cosine, sine, *refs):
    dealt_parts, refs = refs[:pieces], refs[pieces:]
    qkv, cache, weight, out, dealt, entries = refs[:6]
    held, scores, shares, qkv_held, weight_held, arrived, qkv_sem, weight_sem = refs[6:]
    scaling = 1.0 / math.sqrt(HD)
    slots, stored, width = cache.shape[1:]
    depth = qkv.shape[1] // heads
    groups = depth // HD - 2
    lanes = 8
    qkv_copy = pltpu.make_async_copy(qkv, qkv_held, qkv_sem)
    copies = [
        [pltpu.make_async_copy(cache.at[w, s], held.at[w, s], arrived.at[w, s]) for s in range(slots)]
        for w in range(2)
    ]
    weight_copy = pltpu.make_async_copy(weight, weight_held, weight_sem)
    for copy in [qkv_copy] + copies[0] + copies[1] + [weight_copy]:
        copy.start()
    rows = dealt_parts[0][...].astype(jnp.float32)
    for part in dealt_parts[1:]:
        rows += part[...].astype(jnp.float32)
    dealt[...] = rows.astype(jnp.bfloat16)
    inner = normed(rows, gain[...])
    cos, sin = cosine[...], sine[...]
    queries, new_keys, new_values = [], [], []
    qkv_copy.wait()
    product = jnp.dot(inner, qkv_held[...], preferred_element_type=jnp.float32)
    for j in range(heads):
        mixed = product[:, j * depth : (j + 1) * depth]
        for g in range(groups):
            part = turn(mixed[:, g * HD : (g + 1) * HD], cos, sin)
            queries.append(part.astype(jnp.bfloat16).astype(jnp.float32))
        at = slice(j * HD, (j + 1) * HD)
        key = turn(mixed[:, groups * HD : (groups + 1) * HD], cos, sin).astype(jnp.bfloat16)
        value = mixed[:, (groups + 1) * HD :].astype(jnp.bfloat16)
        entries[0, :, at] = key[:slots]
        entries[1, :, at] = value[:slots]
        new_keys.append(key.astype(jnp.float32))
        new_values.append(value.astype(jnp.float32))
    new_keys = jnp.concatenate(new_keys, axis=1)
    new_values = jnp.concatenate(new_values, axis=1)
    across = (((1,), (1,)), ((), ()))
    places = lax.broadcasted_iota(jnp.int32, (1, stored), 1)
    blank = jnp.zeros((1, HD), jnp.float32)
    own_scores = []
    for s in range(slots):
        rows = []
        for j in range(heads):
            for g in range(groups):
                part = queries[j * groups + g][s : s + 1]
                rows.append(
                    jnp.concatenate([part if i == j else blank for i in range(heads)], axis=1)
                )
        rows.append(jnp.zeros((lanes - heads * groups, width), jnp.float32))
        rows = jnp.concatenate(rows, axis=0)
        own_scores.append(jnp.sum(rows * new_keys[s : s + 1], axis=-1, keepdims=True))
        copies[0][s].wait()
        old = lax.dot_general(
            rows.astype(jnp.bfloat16), held[0, s], across, preferred_element_type=jnp.float32
        )
        scores[s * lanes : (s + 1) * lanes, :] = jnp.where(
            places < lengths[s], old * scaling, NEGATIVE
        )
    old = scores[...]
    own = jnp.concatenate(own_scores, axis=0) * scaling
    top = jnp.maximum(jnp.max(old, axis=-1, keepdims=True), own)
    old = jnp.exp(old - top)
    own = jnp.exp(own - top)
    total = jnp.sum(old, axis=-1, keepdims=True) + own
    shares[...] = old / total
    own = (own / total).astype(jnp.bfloat16).astype(jnp.float32)
    attended = []
    for s in range(slots):
        copies[1][s].wait()
        here = slice(s * lanes, (s + 1) * lanes)
        mix = jnp.dot(
            shares[here, :].astype(jnp.bfloat16), held[1, s], preferred_element_type=jnp.float32
        )
        mix += own[here] * new_values[s : s + 1]
        parts = []
        for j in range(heads):
            for g in range(groups):
                row = j * groups + g
                parts.append(mix[row : row + 1, j * HD : (j + 1) * HD])
        attended.append(jnp.concatenate(parts, axis=1))
    if out.shape[0] > slots:
        attended.append(jnp.zeros((out.shape[0] - slots, groups * width), jnp.float32))
    attended = jnp.concatenate(attended, axis=0).astype(jnp.bfloat16)
    weight_copy.wait()
    part = jnp.dot(attended, weight_held[...], preferred_element_type=jnp.float32)
    out[...] = part.astype(jnp.bfloat16)


def step_attend(lengths, dealt_parts, gain, tables, qkv, cache, weight, heads):
    slots, stored, width = cache.shape[1:]
    padded, model = dealt_parts[0].shape
    rows = slots * 8
    pieces = len(dealt_parts)
    return pl.pallas_call(
        functools.partial(step_kernel, heads, pieces),
        out_shape=[
            jax.ShapeDtypeStruct((padded, model), jnp.bfloat16),
            jax.ShapeDtypeStruct((padded, model), jnp.bfloat16),
            jax.ShapeDtypeStruct((2, slots, width), jnp.bfloat16),
        ],
        in_specs=[SMEM_WHOLE] + [VMEM_WHOLE] * (3 + pieces) + [IN_PLACE] * 3,
        out_specs=[VMEM_WHOLE] * 3,
        scratch_shapes=[
            pltpu.VMEM(cache.shape, jnp.bfloat16),
            pltpu.VMEM((rows, stored), jnp.float32),
            pltpu.VMEM((rows, stored), jnp.float32),
            pltpu.VMEM(qkv.shape, jnp.bfloat16),
            pltpu.VMEM(weight.shape, jnp.bfloat16),
            pltpu.SemaphoreType.DMA((2, slots)),
            pltpu.SemaphoreType.DMA(()),
            pltpu.SemaphoreType.DMA(()),
        ],
        compiler_params=params(18),
        cost_estimate=cost(16 * cache.size, 3 * cache.size, rows * stored),
        name="step_attend",
    )(lengths, gain, *tables, *dealt_parts, qkv, cache, weight)


def out_kernel(place, mine, sib, weight, sib_weight, *refs):
    out = refs[-1]
    half = out.shape[1]
    cols = pl.ds(pl.multiple_of(place[0] * half, half), half)
    part = jnp.dot(mine[...], weight[:, cols], preferred_element_type=jnp.float32)
    part += jnp.dot(sib[...], sib_weight[:, cols], preferred_element_type=jnp.float32)
    out[...] = part.astype(jnp.bfloat16)


def out_project(place, mine, sib, weight, sib_weight, after=()):
    rows, depth = mine.shape
    half = weight.shape[1] // 2
    return pl.pallas_call(
        out_kernel,
        out_shape=jax.ShapeDtypeStruct((rows, half), jnp.bfloat16),
        in_specs=[SMEM_WHOLE] + [VMEM_WHOLE] * 4 + [IN_PLACE] * len(after),
        out_specs=VMEM_WHOLE,
        compiler_params=params(8),
        cost_estimate=cost(4 * rows * depth * half, 4 * depth * half + 6 * rows * half),
        name="out_project",
    )(place, mine, sib, weight, sib_weight, *after)


def forward_kernel(split, chips, n_dec, n_after, chunk, place, *refs):
    refs = list(refs)
    mine, sib = refs[:2]
    shares = refs[2 : 2 + 2 * chips]
    refs = refs[2 + 2 * chips :]
    if n_dec:
        dec, dec_shares = refs[0], refs[1 : 1 + 2 * chips]
        refs = refs[1 + 2 * chips :]
    gain, *weights = refs[: 3 if split else 4]
    refs = refs[(3 if split else 4) + n_after :]
    if split:
        resid, hidden = refs[:2]
        held, inner, gate, up, arrived = refs[2:]
        down = ()
    else:
        keep, give, resid = refs[:3]
        refs = refs[3:]
        if n_dec:
            dec_out, dec_resid = refs[:2]
            refs = refs[2:]
        held, inner, hidden, gate, up, down, arrived = refs
    copies = [
        [
            pltpu.make_async_copy(
                source.at[:, pl.ds(i * chunk, chunk)], target.at[i], arrived.at[w, i]
            )
            for i in range(target.shape[0])
        ]
        for w, (source, target) in enumerate(zip(weights, [gate, up, down]))
    ]
    for pair in zip(copies[0], copies[1]):
        for copy in pair:
            copy.start()
    for rest in copies[2:]:
        for copy in rest:
            copy.start()
    piece = mine.shape[0]
    half = shares[0].shape[1]
    core = place[0]
    for rows, at_rows, put in ((mine, core, 0), (sib, 1 - core, piece)):
        here = pl.ds(pl.multiple_of(at_rows * piece, piece), piece)
        for side in range(2):
            at = core if side == 0 else 1 - core
            cols = pl.ds(pl.multiple_of(at * half, half), half)
            added = shares[side][here, :].astype(jnp.float32)
            for k in range(1, chips):
                added += shares[2 * k + side][here, :].astype(jnp.float32)
            value = rows[:, cols].astype(jnp.float32) + added
            held[put : put + piece, cols] = value.astype(jnp.bfloat16)
    if n_dec:
        added = dec_shares[0][...].astype(jnp.float32)
        for share in dec_shares[1:]:
            added += share[...].astype(jnp.float32)
        held[2 * piece :, :] = (dec[...].astype(jnp.float32) + added).astype(jnp.bfloat16)
    for put in range(0, held.shape[0], piece):
        here = slice(put, min(put + piece, held.shape[0]))
        inner[here, :] = normed(held[here, :].astype(jnp.float32), gain[...])
    resid[...] = held[:piece, :]
    if n_dec:
        dec_resid[...] = held[2 * piece :, :]

    for i in range(gate.shape[0]):
        at = slice(i * chunk, (i + 1) * chunk)
        copies[0][i].wait()
        gated = jnp.dot(inner[...], gate[i], preferred_element_type=jnp.float32)
        copies[1][i].wait()
        raised = jnp.dot(inner[...], up[i], preferred_element_type=jnp.float32)
        hidden[:, at] = (gated / (1.0 + jnp.exp(-gated)) * raised).astype(jnp.bfloat16)
    for i in range(0 if split else down.shape[0]):
        at = slice(i * chunk, (i + 1) * chunk)
        copies[2][i].wait()
        part = jnp.dot(hidden[...], down[i], preferred_element_type=jnp.float32)
        part = part.astype(jnp.bfloat16)
        keep[:, at] = part[:piece]
        give[:, at] = part[piece : 2 * piece]
        if n_dec:
            dec_out[:, at] = part[2 * piece :]


def lower_kernel(chunk, hidden, weight, *refs):
    keep, give, down, arrived = refs[-4:]
    piece = keep.shape[0]
    copies = [
        pltpu.make_async_copy(weight.at[:, pl.ds(i * chunk, chunk)], down.at[i], arrived.at[i])
        for i in range(down.shape[0])
    ]
    for copy in copies:
        copy.start()
    for i, copy in enumerate(copies):
        at = slice(i * chunk, (i + 1) * chunk)
        copy.wait()
        part = jnp.dot(hidden[...], down[i], preferred_element_type=jnp.float32)
        part = part.astype(jnp.bfloat16)
        keep[:, at] = part[:piece]
        give[:, at] = part[piece:]


def lower(hidden, weight, after):
    rows, units = hidden.shape
    width = weight.shape[1]
    chunk = 1024
    return pl.pallas_call(
        functools.partial(lower_kernel, chunk),
        out_shape=[jax.ShapeDtypeStruct((rows // 2, width), jnp.bfloat16)] * 2,
        in_specs=[VMEM_WHOLE] + [IN_PLACE] * (1 + len(after)),
        out_specs=[VMEM_WHOLE] * 2,
        scratch_shapes=[
            pltpu.VMEM((width // chunk, units, chunk), jnp.bfloat16),
            pltpu.SemaphoreType.DMA((width // chunk,)),
        ],
        compiler_params=params(24),
        cost_estimate=cost(2 * rows * width * units, 2 * width * units),
        name="lower",
    )(hidden, weight, *after)


def feed_forward(
    place, mine, sib, shares, gain, gate, up, down=None, dec=None, dec_shares=None, after=()
):
    piece, width = mine.shape
    chips = len(shares) // 2
    units = gate.shape[1]
    chunk = 1024
    n_dec = 0 if dec is None else dec.shape[0]
    rows = 2 * piece + n_dec
    args = [mine, sib, *shares]
    if n_dec:
        args += [dec, *dec_shares]
    n_whole = len(args) + 1
    split = down is None
    args += [gain, gate, up] + [down] * (not split)
    if split:
        shapes = [(piece, width), (rows, units)]
    else:
        shapes = [(n, width) for n in [piece] * 3 + [n_dec] * 2 * bool(n_dec)]
    n_weights = 2 if split else 3
    return pl.pallas_call(
        functools.partial(forward_kernel, split, chips, n_dec, len(after), chunk),
        out_shape=[jax.ShapeDtypeStruct(shape, jnp.bfloat16) for shape in shapes],
        in_specs=[SMEM_WHOLE] + [VMEM_WHOLE] * n_whole + [IN_PLACE] * (n_weights + len(after)),
        out_specs=[VMEM_WHOLE] * len(shapes),
        scratch_shapes=[
            pltpu.VMEM((rows, width), jnp.bfloat16),
            pltpu.VMEM((rows, width), jnp.bfloat16),
        ]
        + [pltpu.VMEM((rows, units), jnp.bfloat16)] * (not split)
        + [pltpu.VMEM((units // chunk, width, chunk), jnp.bfloat16)] * 2
        + [pltpu.VMEM((width // chunk, units, chunk), jnp.bfloat16)] * (not split)
        + [pltpu.SemaphoreType.DMA((n_weights, max(units, width) // chunk))],
        compiler_params=params(40),
        cost_estimate=cost(6 * rows * width * units, 6 * width * units, rows * units),
        name="feed_forward",
    )(place, *args, *after)


def angle_tables(places):
    halfway = HD // 2
    powers = jnp.arange(halfway, dtype=jnp.float32) * (2.0 / HD)
    inverse = THETA ** (-powers)
    angles = places.astype(jnp.float32)[:, None] * inverse[None, :]
    cosine, sine = jnp.cos(angles), jnp.sin(angles)
    return jnp.concatenate([cosine, cosine], axis=-1), jnp.concatenate([-sine, sine], axis=-1)


def add(*values):
    total = values[0].astype(jnp.float32)
    for value in values[1:]:
        total = total + value.astype(jnp.float32)
    return total.astype(jnp.bfloat16)


def on_device(
    prefill_rows,
    decode_rows,
    deal_order,
    prefill_offset,
    cache_length,
    prefill_cache,
    decode_cache,
    qkv_weight,
    out_weight,
    attention_gain,
    forward_gain,
    gate_weight,
    up_weight,
    down_weight,
):
    tensor_count = lax.axis_size("tensor")
    dp_count = lax.axis_size("dp")
    chips = tensor_count // 2
    tensor_place = lax.axis_index("tensor")
    group_place = lax.axis_index("dp")
    chip, core = tensor_place // 2, tensor_place % 2
    piece, width = prefill_rows.shape
    per_device = decode_rows.shape[0]
    requests = deal_order.shape[0]
    slots = cache_length.shape[0]
    padded = -(-slots // 16) * 16
    heads = qkv_weight.shape[1]
    tokens = piece * tensor_count

    def place_of(k):
        spots = [core, (chip + k) % chips, prefill_offset[0]]
        return jnp.stack(spots + [(chip + j) % chips for j in range(chips)]).astype(jnp.int32)

    places = [place_of(k) for k in range(chips)]
    weight = in_hbm(qkv_weight.reshape(width, -1))
    gate_weight, up_weight, down_weight = map(in_hbm, (gate_weight, up_weight, down_weight))
    prefill_cache, decode_cache = in_hbm(prefill_cache), in_hbm(decode_cache)

    mines = [prefill_rows] + [from_chip(prefill_rows, k) for k in range(1, chips)]
    sibs = [swap_cores(prefill_rows)]

    low = max(dp_count // 4, 1)
    pool = [decode_rows] + [swap_groups(decode_rows, i) for i in range(1, low)]
    pool = near = jnp.concatenate(pool, axis=0)
    pool = [pool] + [swap_groups(pool, i * low) for i in range(1, dp_count // low)]
    index = jnp.arange(dp_count * per_device, dtype=jnp.int32)
    origin = jnp.bitwise_xor(group_place, index // per_device)
    request = (origin * tensor_count + tensor_place) * per_device + index % per_device
    slot_of = jnp.sum(
        jnp.where(
            request[:, None] == jnp.arange(requests, dtype=jnp.int32)[None, :],
            deal_order[None, :],
            0,
        ),
        axis=1,
    )
    in_group = slot_of - group_place * slots
    chooser = (jnp.arange(padded, dtype=jnp.int32)[:, None] == in_group[None, :]) & (
        in_group[None, :] < slots
    )
    gain = attention_gain.reshape(1, width)
    tables = angle_tables(prefill_offset[0] + jnp.arange(tokens, dtype=jnp.int32))
    dec_tables = angle_tables(jnp.pad(cache_length, (0, padded - slots)))
    queries, entries, everything = [], [], None
    for k in range(chips):
        query, entry, everything = project(
            places[k],
            in_hbm(mines[k]),
            in_hbm(sibs[k]),
            gain,
            weight,
            tables,
            heads,
            everything,
            [query] if k else [near],
        )
        if k == 0:
            first, *pool = pool
            mines[1:], pool, query = lax.optimization_barrier((mines[1:], pool, query))
            pool = jnp.concatenate([first, *pool], axis=0)
            sibs += [swap_cores(rows) for rows in mines[1:]]
        queries.append(query)
        entries.append(entry)
    dealt = jnp.dot(
        chooser.astype(jnp.bfloat16), pool, preferred_element_type=jnp.float32
    ).astype(jnp.bfloat16)
    dealt_parts = [dealt, *from_rest(dealt)]

    out_share = out_weight
    sib_weight, queries[-1] = lax.optimization_barrier((out_weight, queries[-1]))
    sib_weight = in_vmem(swap_cores(sib_weight))
    out_weight = in_vmem(out_weight)

    def finish(attended, place, before):
        attended, *before = lax.optimization_barrier((attended, *before))
        sib = swap_cores(attended)
        return out_project(place, attended, sib, out_weight, sib_weight), before

    parts = []
    dec_shares = []
    for k in range(chips):
        after = dec_shares[:1] if k else dealt_parts[:1]
        attended = fill_attend(places[k], queries[k], prefill_cache, entries, heads, after)
        if k == 0:
            part, dealt_parts[1:] = finish(attended, places[k], dealt_parts[1:])
        else:
            part, dec_shares[1:] = finish(attended, places[k], dec_shares[1:])
        parts.append(part)
        if k == 0:
            lengths, parts[0] = lax.optimization_barrier((cache_length, parts[0]))
            dec_part, dealt, dec_entries = step_attend(
                lengths,
                dealt_parts,
                gain,
                dec_tables,
                weight,
                decode_cache,
                in_hbm(out_share),
                heads,
            )
            dec_shares = [dec_part, *from_rest(dec_part)]

    def shares_of(own, others):
        pairs = []
        for value in [own, *others]:
            pairs += [value, swap_cores(value)]
        return pairs

    gain = forward_gain.reshape(1, width)
    order = [*range(1, chips), 0]

    def fetch(b):
        return [from_chip(parts[(b - j) % chips], j) for j in range(1, chips)]

    theirs = fetch(order[0])
    arrived = []
    for n, b in enumerate(order):
        got = feed_forward(
            places[b],
            mines[b],
            sibs[b],
            shares_of(parts[b], theirs),
            gain,
            gate_weight,
            up_weight,
            down_weight if n + 1 < chips else None,
            dealt if n == 0 else None,
            dec_shares if n == 0 else None,
        )
        if n + 1 < chips:
            keep, give = got[:2]
            *theirs, keep = lax.optimization_barrier((*fetch(order[n + 1]), keep))
            both = add(keep, swap_cores(give))
            arrived.append(from_chip(both, chips - b))
        if n == 0:
            dec_sum, dec_resid = got[3:]
            dec_others = from_rest(dec_sum)
    resid, hidden = got
    dec_sum, hidden = lax.optimization_barrier((dec_sum, hidden))
    final = add(dec_resid, dec_sum, *dec_others)
    picker = in_group[:, None] == jnp.arange(padded, dtype=jnp.int32)[None, :]
    picker = picker & (in_group[:, None] < slots)
    routed = jnp.dot(
        picker.astype(jnp.bfloat16), final, preferred_element_type=jnp.float32
    ).astype(jnp.bfloat16)
    keep, give = lower(hidden, down_weight, [routed])
    low = max(dp_count // 4, 1)
    pairs = routed.reshape(dp_count // low, low * per_device, width)
    rows = add(
        pairs[0], *[swap_groups(pairs[i], i * low) for i in range(1, dp_count // low)]
    )
    *arrived, rows, give = lax.optimization_barrier((*arrived, rows, give))
    pairs = rows.reshape(low, per_device, width)
    routed = add(pairs[0], *[swap_groups(pairs[i], i) for i in range(1, low)])

    prefill_out = add(resid, keep, swap_cores(give), *arrived)
    return (prefill_out, routed, everything, dec_entries)


def solution(mesh):
    placed = (
        P(("dp", "tensor"), None),
        P(("dp", "tensor"), None),
        P(),
        P("dp"),
        P("dp"),
        P(None, "dp", None, "tensor"),
        P(None, "dp", None, "tensor"),
        P(None, "tensor", None),
        P("tensor", None),
        P(),
        P(),
        P(None, "tensor"),
        P(None, "tensor"),
        P("tensor", None),
    )
    return jax.shard_map(
        on_device,
        mesh=mesh,
        in_specs=placed,
        out_specs=(
            P(("dp", "tensor"), None),
            P(("dp", "tensor"), None),
            P(None, "dp", "tensor"),
            P(None, "dp", "tensor"),
        ),
        check_vma=False,
    )
```

```python
import functools
import math

import jax
import jax.numpy as jnp
from jax import lax
from jax.experimental import pallas as pl
from jax.experimental.pallas import tpu as pltpu
from jax.sharding import PartitionSpec as P

HD = 128
EPSILON = 1e-06
THETA = 1000000.0
NEGATIVE = -1e30
MIB = 1 << 20


def swap_cores(value):
    count = lax.axis_size("tensor")
    return lax.ppermute(value, "tensor", [(i, i ^ 1) for i in range(count)])


def from_chip(value, step):
    count = lax.axis_size("tensor")
    chips = count // 2
    return lax.ppermute(
        value, "tensor", [(i, (i // 2 - step) % chips * 2 + i % 2) for i in range(count)]
    )


def from_other(value, step):
    count = lax.axis_size("tensor")
    return lax.ppermute(
        value, "tensor", [(i, (i // 2 - step) % (count // 2) * 2 + 1 - i % 2) for i in range(count)]
    )


def from_rest(value):
    chips = lax.axis_size("tensor") // 2
    return [from_chip(value, k) for k in range(1, chips)] + [from_other(value, k) for k in range(chips)]


def swap_groups(value, mask):
    count = lax.axis_size("dp")
    return lax.ppermute(value, "dp", [(i, i ^ mask) for i in range(count)])


def whole(shape):
    return pl.BlockSpec(shape, lambda *_: (0,) * len(shape))


def params(mib):
    return pltpu.CompilerParams(vmem_limit_bytes=mib * MIB)


def cost(flops, moved, exps=0):
    return pl.CostEstimate(flops=int(flops), bytes_accessed=int(moved), transcendentals=int(exps))


def normed(values, gain):
    spread = jnp.mean(values * values, axis=-1, keepdims=True)
    return (values * lax.rsqrt(spread + EPSILON) * gain).astype(jnp.bfloat16)


def turn(vectors, cosine, sine):
    return vectors * cosine + pltpu.roll(vectors, HD // 2, 1) * sine


def in_vmem(value):
    return pltpu.with_memory_space_constraint(value, pltpu.VMEM)


def in_hbm(value):
    return pltpu.with_memory_space_constraint(value, pltpu.HBM)


VMEM_WHOLE = pl.BlockSpec(memory_space=pltpu.VMEM)
SMEM_WHOLE = pl.BlockSpec(memory_space=pltpu.SMEM)
IN_PLACE = pl.BlockSpec(memory_space=pl.ANY)


def project_kernel(n_dec, n_after, groups, heads, place, *refs):
    refs = list(refs)
    mine, sib, weight, gain, cosine, sine = refs[:6]
    refs = refs[6:]
    if n_dec:
        dec, dec_cos, dec_sin = refs[:3]
        refs = refs[3:]
    refs = refs[n_after:]
    query, entries, everything = refs[:3]
    if n_dec:
        dec_query, dec_entries = refs[3:5]
    inner, rows_held, weight_held, row_sems, weight_sems, out_sem = refs[-6:]
    piece = mine.shape[0]
    core = place[0]
    scale = gain[...]
    depth = (groups + 2) * HD
    row_copies = [
        pltpu.make_async_copy(ref, rows_held.at[i], row_sems.at[i])
        for i, ref in enumerate((mine, sib))
    ]
    weight_copies = [
        pltpu.make_async_copy(
            weight.at[:, pl.ds(j * depth, depth)], weight_held.at[j], weight_sems.at[j]
        )
        for j in range(heads)
    ]
    for copy in row_copies + weight_copies:
        copy.start()
    for i, at in enumerate((core, 1 - core)):
        row_copies[i].wait()
        start = pl.multiple_of(at * piece, piece)
        inner[pl.ds(start, piece), :] = normed(rows_held[i].astype(jnp.float32), scale)
    if n_dec:
        inner[2 * piece :, :] = normed(dec[...].astype(jnp.float32), scale)
    here = pl.ds(pl.multiple_of(place[1] * 2 * piece, 2 * piece), 2 * piece)
    for j in range(heads):
        weight_copies[j].wait()
        mixed = jnp.dot(inner[...], weight_held[j], preferred_element_type=jnp.float32)

        def put(rows, cos, sin, query_out, entry_out):
            for g in range(groups):
                part = rows[:, g * HD : (g + 1) * HD]
                at = (j * groups + g) * HD
                turned = turn(part, cos, sin).astype(jnp.bfloat16)
                query_out[:, at : at + HD] = turned.astype(query_out.dtype)
            key = turn(rows[:, groups * HD : (groups + 1) * HD], cos, sin).astype(jnp.bfloat16)
            value = rows[:, (groups + 1) * HD :].astype(jnp.bfloat16)
            size = entry_out.shape[1]
            entry_out[0, :, j * HD : (j + 1) * HD] = key[:size]
            entry_out[1, :, j * HD : (j + 1) * HD] = value[:size]

        put(mixed[: 2 * piece], cosine[here, :], sine[here, :], query, entries)
        if n_dec:
            put(mixed[2 * piece :], dec_cos[...], dec_sin[...], dec_query, dec_entries)
    keep = pltpu.make_async_copy(entries, everything.at[:, here, :], out_sem)
    keep.start()
    keep.wait()


def project(
    place, mine, sib, gain, weight, tables, heads, everything, dec=None, dec_tables=None, slots=0, after=()
):
    piece, width = mine.shape
    depth = weight.shape[1] // heads
    groups = depth // HD - 2
    block = 2 * piece
    n_dec = 0 if dec is None else dec.shape[0]
    args = [mine, sib, weight, gain, *tables]
    if n_dec:
        args += [dec, *dec_tables]
    n_operands = len(args)
    after = list(after)
    aliases = {}
    if everything is not None:
        after.append(everything)
        aliases = {n_operands + len(after): 2}
    wide = heads * groups * HD
    out_shape = [
        jax.ShapeDtypeStruct((block, wide), jnp.bfloat16),
        jax.ShapeDtypeStruct((2, block, heads * HD), jnp.bfloat16),
        jax.ShapeDtypeStruct((2, tables[0].shape[0], heads * HD), jnp.bfloat16),
    ]
    if n_dec:
        out_shape += [
            jax.ShapeDtypeStruct((n_dec, wide), jnp.float32),
            jax.ShapeDtypeStruct((2, slots, heads * HD), jnp.bfloat16),
        ]
    rows = block + n_dec
    return pl.pallas_call(
        functools.partial(project_kernel, n_dec, len(after), groups, heads),
        out_shape=out_shape,
        in_specs=[SMEM_WHOLE]
        + [IN_PLACE] * 3
        + [VMEM_WHOLE] * (len(args) - 3)
        + [IN_PLACE] * len(after),
        out_specs=[VMEM_WHOLE] * 2 + [IN_PLACE] + [VMEM_WHOLE] * (len(out_shape) - 3),
        scratch_shapes=[
            pltpu.VMEM((rows, width), jnp.bfloat16),
            pltpu.VMEM((2, piece, width), jnp.bfloat16),
            pltpu.VMEM((heads, width, depth), jnp.bfloat16),
            pltpu.SemaphoreType.DMA((2,)),
            pltpu.SemaphoreType.DMA((heads,)),
            pltpu.SemaphoreType.DMA(()),
        ],
        input_output_aliases=aliases,
        compiler_params=params(20),
        cost_estimate=cost(2 * rows * weight.size, 2 * (weight.size + 2 * rows * width)),
        name="project",
    )(place, *args, *after)


def fill_kernel(groups, chips, place, query, cache_key, cache_value, *refs):
    new_keys, new_values, out = refs[:chips], refs[chips : 2 * chips], refs[-1]
    scaling = math.log2(math.e) / math.sqrt(HD)
    count = query.shape[0]
    stored = cache_key.shape[2]
    old_seen = lax.broadcasted_iota(jnp.int32, (1, stored), 1) < place[2]
    ahead = lax.broadcasted_iota(jnp.int32, (count, count), 1) - lax.broadcasted_iota(
        jnp.int32, (count, count), 0
    )
    across = (((1,), (1,)), ((), ()))
    for g in range(groups):
        rows = query[:, g * HD : (g + 1) * HD]
        scores = lax.dot_general(rows, cache_key[0, 0], across, preferred_element_type=jnp.float32)
        scores = [jnp.where(old_seen, scores * scaling, NEGATIVE)]
        for k in range(chips):
            fresh = lax.dot_general(
                rows, new_keys[k][0], across, preferred_element_type=jnp.float32
            )
            gap = (place[1] - place[3 + k]) * count
            scores.append(jnp.where(ahead <= gap, fresh * scaling, NEGATIVE))
        top = jnp.max(scores[0], axis=-1, keepdims=True)
        for part in scores[1:]:
            top = jnp.maximum(top, jnp.max(part, axis=-1, keepdims=True))
        mix, total = 0.0, 0.0
        for part, values in zip(scores, [cache_value[0, 0], *[v[0] for v in new_values]]):
            weights = jnp.exp2(part - top)
            total += jnp.sum(weights, axis=-1, keepdims=True)
            mix += jnp.dot(weights.astype(jnp.bfloat16), values, preferred_element_type=jnp.float32)
        out[:, g * HD : (g + 1) * HD] = (mix / total).astype(jnp.bfloat16)


def fill_attend(place, query, cache, entries, heads, after=()):
    count = query.shape[0]
    groups = query.shape[1] // heads // HD
    stored = cache.shape[2]
    chips = len(entries)
    pairs = count * groups * heads * (stored + chips * count)
    return pl.pallas_call(
        functools.partial(fill_kernel, groups, chips),
        out_shape=jax.ShapeDtypeStruct(query.shape, jnp.bfloat16),
        grid_spec=pltpu.PrefetchScalarGridSpec(
            num_scalar_prefetch=1,
            grid=(heads,),
            in_specs=[
                pl.BlockSpec((count, groups * HD), lambda j, s: (0, j)),
                pl.BlockSpec((1, 1, stored, HD), lambda j, s: (0, 0, 0, j)),
                pl.BlockSpec((1, 1, stored, HD), lambda j, s: (1, 0, 0, j)),
            ]
            + [pl.BlockSpec((1, count, HD), lambda j, s: (0, 0, j))] * chips
            + [pl.BlockSpec((1, count, HD), lambda j, s: (1, 0, j))] * chips
            + [IN_PLACE] * len(after),
            out_specs=pl.BlockSpec((count, groups * HD), lambda j, s: (0, j)),
        ),
        compiler_params=params(12),
        cost_estimate=cost(8 * pairs * HD, 2 * cache.size, pairs),
        name="fill_attend",
    )(place, query, cache, cache, *entries, *entries, *after)


def step_kernel(
    heads, lengths, query, entries, cache, weight, out, held, scores, shares, weight_held, arrived, weight_sem
):
    scaling = 1.0 / math.sqrt(HD)
    slots, stored, width = cache.shape[1:]
    groups = query.shape[1] // width
    lanes = 8
    copies = [
        [pltpu.make_async_copy(cache.at[w, s], held.at[w, s], arrived.at[w, s]) for s in range(slots)]
        for w in range(2)
    ]
    weight_copy = pltpu.make_async_copy(weight, weight_held, weight_sem)
    for copy in copies[0] + copies[1] + [weight_copy]:
        copy.start()
    across = (((1,), (1,)), ((), ()))
    places = lax.broadcasted_iota(jnp.int32, (1, stored), 1)
    blank = jnp.zeros((1, HD), jnp.float32)
    new_keys = entries[0].astype(jnp.float32)
    new_values = entries[1].astype(jnp.float32)
    own_scores = []
    for s in range(slots):
        rows = []
        for j in range(heads):
            for g in range(groups):
                at = (j * groups + g) * HD
                part = query[s : s + 1, at : at + HD]
                rows.append(
                    jnp.concatenate([part if i == j else blank for i in range(heads)], axis=1)
                )
        rows.append(jnp.zeros((lanes - heads * groups, width), jnp.float32))
        rows = jnp.concatenate(rows, axis=0)
        own_scores.append(jnp.sum(rows * new_keys[s : s + 1], axis=-1, keepdims=True))
        copies[0][s].wait()
        old = lax.dot_general(
            rows.astype(jnp.bfloat16), held[0, s], across, preferred_element_type=jnp.float32
        )
        scores[s * lanes : (s + 1) * lanes, :] = jnp.where(
            places < lengths[s], old * scaling, NEGATIVE
        )
    old = scores[...]
    own = jnp.concatenate(own_scores, axis=0) * scaling
    top = jnp.maximum(jnp.max(old, axis=-1, keepdims=True), own)
    old = jnp.exp(old - top)
    own = jnp.exp(own - top)
    total = jnp.sum(old, axis=-1, keepdims=True) + own
    shares[...] = old / total
    own = (own / total).astype(jnp.bfloat16).astype(jnp.float32)
    attended = []
    for s in range(slots):
        copies[1][s].wait()
        here = slice(s * lanes, (s + 1) * lanes)
        mix = jnp.dot(
            shares[here, :].astype(jnp.bfloat16), held[1, s], preferred_element_type=jnp.float32
        )
        mix += own[here] * new_values[s : s + 1]
        parts = []
        for j in range(heads):
            for g in range(groups):
                row = j * groups + g
                parts.append(mix[row : row + 1, j * HD : (j + 1) * HD])
        attended.append(jnp.concatenate(parts, axis=1))
    if out.shape[0] > slots:
        attended.append(jnp.zeros((out.shape[0] - slots, query.shape[1]), jnp.float32))
    attended = jnp.concatenate(attended, axis=0).astype(jnp.bfloat16)
    weight_copy.wait()
    part = jnp.dot(attended, weight_held[...], preferred_element_type=jnp.float32)
    out[...] = part.astype(jnp.bfloat16)


def step_attend(lengths, query, entries, cache, weight, heads):
    slots, stored = cache.shape[1:3]
    padded = query.shape[0]
    rows = slots * 8
    return pl.pallas_call(
        functools.partial(step_kernel, heads),
        out_shape=jax.ShapeDtypeStruct((padded, weight.shape[1]), jnp.bfloat16),
        in_specs=[SMEM_WHOLE, VMEM_WHOLE, VMEM_WHOLE, IN_PLACE, IN_PLACE],
        out_specs=VMEM_WHOLE,
        scratch_shapes=[
            pltpu.VMEM(cache.shape, jnp.bfloat16),
            pltpu.VMEM((rows, stored), jnp.float32),
            pltpu.VMEM((rows, stored), jnp.float32),
            pltpu.VMEM(weight.shape, jnp.bfloat16),
            pltpu.SemaphoreType.DMA((2, slots)),
            pltpu.SemaphoreType.DMA(()),
        ],
        compiler_params=params(20),
        cost_estimate=cost(16 * cache.size, 2 * cache.size, rows * stored),
        name="step_attend",
    )(lengths, query, entries, cache, weight)


def out_kernel(place, mine, sib, weight, sib_weight, *refs):
    out = refs[-1]
    half = out.shape[1]
    cols = pl.ds(pl.multiple_of(place[0] * half, half), half)
    part = jnp.dot(mine[...], weight[:, cols], preferred_element_type=jnp.float32)
    part += jnp.dot(sib[...], sib_weight[:, cols], preferred_element_type=jnp.float32)
    out[...] = part.astype(jnp.bfloat16)


def out_project(place, mine, sib, weight, sib_weight, after=()):
    rows, depth = mine.shape
    half = weight.shape[1] // 2
    return pl.pallas_call(
        out_kernel,
        out_shape=jax.ShapeDtypeStruct((rows, half), jnp.bfloat16),
        in_specs=[SMEM_WHOLE] + [VMEM_WHOLE] * 4 + [IN_PLACE] * len(after),
        out_specs=VMEM_WHOLE,
        compiler_params=params(8),
        cost_estimate=cost(4 * rows * depth * half, 4 * depth * half + 6 * rows * half),
        name="out_project",
    )(place, mine, sib, weight, sib_weight, *after)


def forward_kernel(split, chips, n_dec, n_after, chunk, place, *refs):
    refs = list(refs)
    mine, sib = refs[:2]
    shares = refs[2 : 2 + 2 * chips]
    refs = refs[2 + 2 * chips :]
    if n_dec:
        dec, dec_shares = refs[0], refs[1 : 1 + 2 * chips]
        refs = refs[1 + 2 * chips :]
    gain, *weights = refs[: 3 if split else 4]
    refs = refs[(3 if split else 4) + n_after :]
    if split:
        resid, hidden = refs[:2]
        held, inner, gate, up, arrived = refs[2:]
        down = ()
    else:
        keep, give, resid = refs[:3]
        refs = refs[3:]
        if n_dec:
            dec_out, dec_resid = refs[:2]
            refs = refs[2:]
        held, inner, hidden, gate, up, down, arrived = refs
    copies = [
        [
            pltpu.make_async_copy(
                source.at[:, pl.ds(i * chunk, chunk)], target.at[i], arrived.at[w, i]
            )
            for i in range(target.shape[0])
        ]
        for w, (source, target) in enumerate(zip(weights, [gate, up, down]))
    ]
    for pair in zip(copies[0], copies[1]):
        for copy in pair:
            copy.start()
    for rest in copies[2:]:
        for copy in rest:
            copy.start()
    piece = mine.shape[0]
    half = shares[0].shape[1]
    core = place[0]
    for rows, at_rows, put in ((mine, core, 0), (sib, 1 - core, piece)):
        here = pl.ds(pl.multiple_of(at_rows * piece, piece), piece)
        for side in range(2):
            at = core if side == 0 else 1 - core
            cols = pl.ds(pl.multiple_of(at * half, half), half)
            added = shares[side][here, :].astype(jnp.float32)
            for k in range(1, chips):
                added += shares[2 * k + side][here, :].astype(jnp.float32)
            value = rows[:, cols].astype(jnp.float32) + added
            held[put : put + piece, cols] = value.astype(jnp.bfloat16)
    if n_dec:
        added = dec_shares[0][...].astype(jnp.float32)
        for share in dec_shares[1:]:
            added += share[...].astype(jnp.float32)
        held[2 * piece :, :] = (dec[...].astype(jnp.float32) + added).astype(jnp.bfloat16)
    for put in range(0, held.shape[0], piece):
        here = slice(put, min(put + piece, held.shape[0]))
        inner[here, :] = normed(held[here, :].astype(jnp.float32), gain[...])
    resid[...] = held[:piece, :]
    if n_dec:
        dec_resid[...] = held[2 * piece :, :]

    for i in range(gate.shape[0]):
        at = slice(i * chunk, (i + 1) * chunk)
        copies[0][i].wait()
        gated = jnp.dot(inner[...], gate[i], preferred_element_type=jnp.float32)
        copies[1][i].wait()
        raised = jnp.dot(inner[...], up[i], preferred_element_type=jnp.float32)
        hidden[:, at] = (gated / (1.0 + jnp.exp(-gated)) * raised).astype(jnp.bfloat16)
    for i in range(0 if split else down.shape[0]):
        at = slice(i * chunk, (i + 1) * chunk)
        copies[2][i].wait()
        part = jnp.dot(hidden[...], down[i], preferred_element_type=jnp.float32)
        part = part.astype(jnp.bfloat16)
        keep[:, at] = part[:piece]
        give[:, at] = part[piece : 2 * piece]
        if n_dec:
            dec_out[:, at] = part[2 * piece :]


def lower_kernel(chunk, hidden, weight, *refs):
    keep, give, down, arrived = refs[-4:]
    piece = keep.shape[0]
    copies = [
        pltpu.make_async_copy(weight.at[:, pl.ds(i * chunk, chunk)], down.at[i], arrived.at[i])
        for i in range(down.shape[0])
    ]
    for copy in copies:
        copy.start()
    for i, copy in enumerate(copies):
        at = slice(i * chunk, (i + 1) * chunk)
        copy.wait()
        part = jnp.dot(hidden[...], down[i], preferred_element_type=jnp.float32)
        part = part.astype(jnp.bfloat16)
        keep[:, at] = part[:piece]
        give[:, at] = part[piece:]


def lower(hidden, weight, after):
    rows, units = hidden.shape
    width = weight.shape[1]
    chunk = width // 4
    return pl.pallas_call(
        functools.partial(lower_kernel, chunk),
        out_shape=[jax.ShapeDtypeStruct((rows // 2, width), jnp.bfloat16)] * 2,
        in_specs=[VMEM_WHOLE] + [IN_PLACE] * (1 + len(after)),
        out_specs=[VMEM_WHOLE] * 2,
        scratch_shapes=[
            pltpu.VMEM((4, units, chunk), jnp.bfloat16),
            pltpu.SemaphoreType.DMA((4,)),
        ],
        compiler_params=params(24),
        cost_estimate=cost(2 * rows * width * units, 2 * width * units),
        name="lower",
    )(hidden, weight, *after)


def feed_forward(
    place, mine, sib, shares, gain, gate, up, down=None, dec=None, dec_shares=None, after=()
):
    piece, width = mine.shape
    chips = len(shares) // 2
    units = gate.shape[1]
    chunks = 4
    chunk = width // chunks
    n_dec = 0 if dec is None else dec.shape[0]
    rows = 2 * piece + n_dec
    args = [mine, sib, *shares]
    if n_dec:
        args += [dec, *dec_shares]
    n_whole = len(args) + 1
    split = down is None
    args += [gain, gate, up] + [down] * (not split)
    if split:
        shapes = [(piece, width), (rows, units)]
    else:
        shapes = [(n, width) for n in [piece] * 3 + [n_dec] * 2 * bool(n_dec)]
    n_weights = 2 if split else 3
    return pl.pallas_call(
        functools.partial(forward_kernel, split, chips, n_dec, len(after), chunk),
        out_shape=[jax.ShapeDtypeStruct(shape, jnp.bfloat16) for shape in shapes],
        in_specs=[SMEM_WHOLE] + [VMEM_WHOLE] * n_whole + [IN_PLACE] * (n_weights + len(after)),
        out_specs=[VMEM_WHOLE] * len(shapes),
        scratch_shapes=[
            pltpu.VMEM((rows, width), jnp.bfloat16),
            pltpu.VMEM((rows, width), jnp.bfloat16),
        ]
        + [pltpu.VMEM((rows, units), jnp.bfloat16)] * (not split)
        + [pltpu.VMEM((units // chunk, width, chunk), jnp.bfloat16)] * 2
        + [pltpu.VMEM((chunks, units, chunk), jnp.bfloat16)] * (not split)
        + [pltpu.SemaphoreType.DMA((n_weights, chunks))],
        compiler_params=params(40),
        cost_estimate=cost(6 * rows * width * units, 6 * width * units, rows * units),
        name="feed_forward",
    )(place, *args, *after)


def angle_tables(places):
    halfway = HD // 2
    powers = jnp.arange(halfway, dtype=jnp.float32) * (2.0 / HD)
    inverse = THETA ** (-powers)
    angles = places.astype(jnp.float32)[:, None] * inverse[None, :]
    cosine, sine = jnp.cos(angles), jnp.sin(angles)
    return jnp.concatenate([cosine, cosine], axis=-1), jnp.concatenate([-sine, sine], axis=-1)


def add(*values):
    total = values[0].astype(jnp.float32)
    for value in values[1:]:
        total = total + value.astype(jnp.float32)
    return total.astype(jnp.bfloat16)


def on_device(
    prefill_rows,
    decode_rows,
    deal_order,
    prefill_offset,
    cache_length,
    prefill_cache,
    decode_cache,
    qkv_weight,
    out_weight,
    attention_gain,
    forward_gain,
    gate_weight,
    up_weight,
    down_weight,
):
    tensor_count = lax.axis_size("tensor")
    dp_count = lax.axis_size("dp")
    chips = tensor_count // 2
    tensor_place = lax.axis_index("tensor")
    group_place = lax.axis_index("dp")
    chip, core = tensor_place // 2, tensor_place % 2
    piece, width = prefill_rows.shape
    per_device = decode_rows.shape[0]
    requests = deal_order.shape[0]
    slots = cache_length.shape[0]
    padded = -(-slots // 16) * 16
    heads = qkv_weight.shape[1]
    tokens = piece * tensor_count

    def place_of(k):
        spots = [core, (chip + k) % chips, prefill_offset[0]]
        return jnp.stack(spots + [(chip + j) % chips for j in range(chips)]).astype(jnp.int32)

    places = [place_of(k) for k in range(chips)]
    weight = in_hbm(qkv_weight.reshape(width, -1))
    gate_weight, up_weight, down_weight = map(in_hbm, (gate_weight, up_weight, down_weight))
    prefill_cache, decode_cache = in_hbm(prefill_cache), in_hbm(decode_cache)

    mines = [prefill_rows] + [from_chip(prefill_rows, k) for k in range(1, chips)]
    sibs = [swap_cores(prefill_rows)]

    low = max(dp_count // 4, 1)
    pool = [decode_rows] + [swap_groups(decode_rows, i) for i in range(1, low)]
    near = jnp.concatenate(pool, axis=0)
    pool = [near] + [swap_groups(near, i * low) for i in range(1, dp_count // low)]
    index = jnp.arange(dp_count * per_device, dtype=jnp.int32)
    origin = jnp.bitwise_xor(group_place, index // per_device)
    request = (origin * tensor_count + tensor_place) * per_device + index % per_device
    slot_of = jnp.sum(
        jnp.where(
            request[:, None] == jnp.arange(requests, dtype=jnp.int32)[None, :],
            deal_order[None, :],
            0,
        ),
        axis=1,
    )
    in_group = slot_of - group_place * slots
    chooser = (jnp.arange(padded, dtype=jnp.int32)[:, None] == in_group[None, :]) & (
        in_group[None, :] < slots
    )
    gain = attention_gain.reshape(1, width)
    tables = angle_tables(prefill_offset[0] + jnp.arange(tokens, dtype=jnp.int32))
    dec_tables = angle_tables(jnp.pad(cache_length, (0, padded - slots)))
    queries, entries, everything = [None] * chips, [None] * chips, None
    for k in range(chips):
        last = k == chips - 1
        if k == 1:
            far = pool[1:]
            mines[1:], far, queries[0] = lax.optimization_barrier((mines[1:], far, queries[0]))
            sibs += [swap_cores(rows) for rows in mines[1:]]
            pool = jnp.concatenate([near, *far], axis=0)
            dealt = jnp.dot(
                chooser.astype(jnp.bfloat16), pool, preferred_element_type=jnp.float32
            ).astype(jnp.bfloat16)
            dealt = add(dealt, *from_rest(dealt))
        got = project(
            places[k],
            in_hbm(mines[k]),
            in_hbm(sibs[k]),
            gain,
            weight,
            tables,
            heads,
            everything,
            dealt if last else None,
            dec_tables if last else None,
            slots,
            [queries[k - 1]] if k else [near],
        )
        queries[k], entries[k], everything = got[:3]
        if last:
            dec_query, dec_entries = got[3:]

    out_share = out_weight
    sib_weight, queries[-1] = lax.optimization_barrier((out_weight, queries[-1]))
    sib_weight = in_vmem(swap_cores(sib_weight))
    out_weight = in_vmem(out_weight)

    def finish(attended, place, before):
        attended, *before = lax.optimization_barrier((attended, *before))
        sib = swap_cores(attended)
        return out_project(place, attended, sib, out_weight, sib_weight), before

    parts = []
    dec_shares = []
    for k in range(chips):
        attended = fill_attend(
            places[k], queries[k], prefill_cache, entries, heads, dec_shares[:1]
        )
        part, dec_shares[1:] = finish(attended, places[k], dec_shares[1:])
        parts.append(part)
        if k == 0:
            lengths, parts[0] = lax.optimization_barrier((cache_length, parts[0]))
            dec_part = step_attend(
                lengths, dec_query, dec_entries, decode_cache, in_hbm(out_share), heads
            )
            dec_shares = [dec_part, *from_rest(dec_part)]

    def shares_of(own, others):
        pairs = []
        for value in [own, *others]:
            pairs += [value, swap_cores(value)]
        return pairs

    gain = forward_gain.reshape(1, width)
    order = [*range(1, chips), 0]

    def fetch(b):
        return [from_chip(parts[(b - j) % chips], j) for j in range(1, chips)]

    theirs = fetch(order[0])
    arrived = []
    for n, b in enumerate(order):
        got = feed_forward(
            places[b],
            mines[b],
            sibs[b],
            shares_of(parts[b], theirs),
            gain,
            gate_weight,
            up_weight,
            down_weight if n + 1 < chips else None,
            dealt if n == 0 else None,
            dec_shares if n == 0 else None,
        )
        if n + 1 < chips:
            keep, give = got[:2]
            *theirs, keep = lax.optimization_barrier((*fetch(order[n + 1]), keep))
            both = add(keep, swap_cores(give))
            arrived.append(from_chip(both, chips - b))
        if n == 0:
            dec_sum, dec_resid = got[3:]
            dec_others = from_rest(dec_sum)
    resid, hidden = got
    dec_sum, hidden = lax.optimization_barrier((dec_sum, hidden))
    final = add(dec_resid, dec_sum, *dec_others)
    picker = in_group[:, None] == jnp.arange(padded, dtype=jnp.int32)[None, :]
    picker = picker & (in_group[:, None] < slots)
    routed = jnp.dot(
        picker.astype(jnp.bfloat16), final, preferred_element_type=jnp.float32
    ).astype(jnp.bfloat16)
    keep, give = lower(hidden, down_weight, [routed])
    low = max(dp_count // 4, 1)
    pairs = routed.reshape(dp_count // low, low * per_device, width)
    rows = add(
        pairs[0], *[swap_groups(pairs[i], i * low) for i in range(1, dp_count // low)]
    )
    *arrived, rows, give = lax.optimization_barrier((*arrived, rows, give))
    pairs = rows.reshape(low, per_device, width)
    routed = add(pairs[0], *[swap_groups(pairs[i], i) for i in range(1, low)])

    prefill_out = add(resid, keep, swap_cores(give), *arrived)
    return (prefill_out, routed, everything, dec_entries)


def solution(mesh):
    placed = (
        P(("dp", "tensor"), None),
        P(("dp", "tensor"), None),
        P(),
        P("dp"),
        P("dp"),
        P(None, "dp", None, "tensor"),
        P(None, "dp", None, "tensor"),
        P(None, "tensor", None),
        P("tensor", None),
        P(),
        P(),
        P(None, "tensor"),
        P(None, "tensor"),
        P("tensor", None),
    )
    return jax.shard_map(
        on_device,
        mesh=mesh,
        in_specs=placed,
        out_specs=(
            P(("dp", "tensor"), None),
            P(("dp", "tensor"), None),
            P(None, "dp", "tensor"),
            P(None, "dp", "tensor"),
        ),
        check_vma=False,
    )
```

```python
import functools
import math

import jax
import jax.numpy as jnp
from jax import lax
from jax.experimental import pallas as pl
from jax.experimental.pallas import tpu as pltpu
from jax.sharding import PartitionSpec as P

HD = 128
EPSILON = 1e-06
THETA = 1000000.0
NEGATIVE = -1e30
MIB = 1 << 20


def swap_cores(value):
    count = lax.axis_size("tensor")
    return lax.ppermute(value, "tensor", [(i, i ^ 1) for i in range(count)])


def from_chip(value, step):
    count = lax.axis_size("tensor")
    chips = count // 2
    return lax.ppermute(
        value, "tensor", [(i, (i // 2 - step) % chips * 2 + i % 2) for i in range(count)]
    )


def from_other(value, step):
    count = lax.axis_size("tensor")
    return lax.ppermute(
        value, "tensor", [(i, (i // 2 - step) % (count // 2) * 2 + 1 - i % 2) for i in range(count)]
    )


def from_rest(value):
    chips = lax.axis_size("tensor") // 2
    return [from_chip(value, k) for k in range(1, chips)] + [from_other(value, k) for k in range(chips)]


def swap_groups(value, mask):
    count = lax.axis_size("dp")
    return lax.ppermute(value, "dp", [(i, i ^ mask) for i in range(count)])


def whole(shape):
    return pl.BlockSpec(shape, lambda *_: (0,) * len(shape))


def params(mib):
    return pltpu.CompilerParams(vmem_limit_bytes=mib * MIB)


def cost(flops, moved, exps=0):
    return pl.CostEstimate(flops=int(flops), bytes_accessed=int(moved), transcendentals=int(exps))


def normed(values, gain):
    spread = jnp.mean(values * values, axis=-1, keepdims=True)
    return (values * lax.rsqrt(spread + EPSILON) * gain).astype(jnp.bfloat16)


def turn(vectors, cosine, sine):
    return vectors * cosine + pltpu.roll(vectors, HD // 2, 1) * sine


def in_vmem(value):
    return pltpu.with_memory_space_constraint(value, pltpu.VMEM)


def in_hbm(value):
    return pltpu.with_memory_space_constraint(value, pltpu.HBM)


def stays_in_vmem(shape):
    return pltpu.VMEM(shape, jnp.bfloat16)


VMEM_WHOLE = pl.BlockSpec(memory_space=pltpu.VMEM)
SMEM_WHOLE = pl.BlockSpec(memory_space=pltpu.SMEM)
IN_PLACE = pl.BlockSpec(memory_space=pl.ANY)


def project_kernel(n_dec, n_after, groups, heads, place, *refs):
    refs = list(refs)
    mine, sib, weight, gain, cosine, sine = refs[:6]
    refs = refs[6:]
    if n_dec:
        dec, dec_cos, dec_sin = refs[:3]
        refs = refs[3:]
    refs = refs[n_after:]
    query, entries, everything = refs[:3]
    if n_dec:
        dec_query, dec_entries = refs[3:5]
    inner, rows_held, weight_held, row_sems, weight_sems, out_sem = refs[-6:]
    piece = mine.shape[0]
    core = place[0]
    scale = gain[...]
    depth = (groups + 2) * HD
    row_copies = [
        pltpu.make_async_copy(ref, rows_held.at[i], row_sems.at[i])
        for i, ref in enumerate((mine, sib))
    ]
    weight_copies = [
        pltpu.make_async_copy(
            weight.at[:, pl.ds(j * depth, depth)], weight_held.at[j], weight_sems.at[j]
        )
        for j in range(heads)
    ]
    for copy in row_copies + weight_copies:
        copy.start()
    for i, at in enumerate((core, 1 - core)):
        row_copies[i].wait()
        start = pl.multiple_of(at * piece, piece)
        inner[pl.ds(start, piece), :] = normed(rows_held[i].astype(jnp.float32), scale)
    if n_dec:
        inner[2 * piece :, :] = normed(dec[...].astype(jnp.float32), scale)
    here = pl.ds(pl.multiple_of(place[1] * 2 * piece, 2 * piece), 2 * piece)
    for j in range(heads):
        weight_copies[j].wait()
        mixed = jnp.dot(inner[...], weight_held[j], preferred_element_type=jnp.float32)

        def put(rows, cos, sin, query_out, entry_out):
            for g in range(groups):
                part = rows[:, g * HD : (g + 1) * HD]
                at = (j * groups + g) * HD
                turned = turn(part, cos, sin).astype(jnp.bfloat16)
                query_out[:, at : at + HD] = turned.astype(query_out.dtype)
            key = turn(rows[:, groups * HD : (groups + 1) * HD], cos, sin).astype(jnp.bfloat16)
            value = rows[:, (groups + 1) * HD :].astype(jnp.bfloat16)
            size = entry_out.shape[1]
            entry_out[0, :, j * HD : (j + 1) * HD] = key[:size]
            entry_out[1, :, j * HD : (j + 1) * HD] = value[:size]

        put(mixed[: 2 * piece], cosine[here, :], sine[here, :], query, entries)
        if n_dec:
            put(mixed[2 * piece :], dec_cos[...], dec_sin[...], dec_query, dec_entries)
    keep = pltpu.make_async_copy(entries, everything.at[:, here, :], out_sem)
    keep.start()
    keep.wait()


def project(
    place, mine, sib, gain, weight, tables, heads, everything, dec=None, dec_tables=None, slots=0, after=()
):
    piece, width = mine.shape
    depth = weight.shape[1] // heads
    groups = depth // HD - 2
    block = 2 * piece
    n_dec = 0 if dec is None else dec.shape[0]
    args = [mine, sib, weight, gain, *tables]
    if n_dec:
        args += [dec, *dec_tables]
    n_operands = len(args)
    after = list(after)
    aliases = {}
    if everything is not None:
        after.append(everything)
        aliases = {n_operands + len(after): 2}
    wide = heads * groups * HD
    out_shape = [
        jax.ShapeDtypeStruct((block, wide), jnp.bfloat16),
        jax.ShapeDtypeStruct((2, block, heads * HD), jnp.bfloat16),
        jax.ShapeDtypeStruct((2, tables[0].shape[0], heads * HD), jnp.bfloat16),
    ]
    if n_dec:
        out_shape += [
            jax.ShapeDtypeStruct((n_dec, wide), jnp.float32),
            jax.ShapeDtypeStruct((2, slots, heads * HD), jnp.bfloat16),
        ]
    rows = block + n_dec
    return pl.pallas_call(
        functools.partial(project_kernel, n_dec, len(after), groups, heads),
        out_shape=out_shape,
        in_specs=[SMEM_WHOLE]
        + [IN_PLACE] * 3
        + [VMEM_WHOLE] * (len(args) - 3)
        + [IN_PLACE] * len(after),
        out_specs=[VMEM_WHOLE] * 2 + [IN_PLACE] + [VMEM_WHOLE] * (len(out_shape) - 3),
        scratch_shapes=[
            pltpu.VMEM((rows, width), jnp.bfloat16),
            pltpu.VMEM((2, piece, width), jnp.bfloat16),
            pltpu.VMEM((heads, width, depth), jnp.bfloat16),
            pltpu.SemaphoreType.DMA((2,)),
            pltpu.SemaphoreType.DMA((heads,)),
            pltpu.SemaphoreType.DMA(()),
        ],
        input_output_aliases=aliases,
        compiler_params=params(20),
        cost_estimate=cost(2 * rows * weight.size, 2 * (weight.size + 2 * rows * width)),
        name="project",
    )(place, *args, *after)


def fill_kernel(groups, chips, place, query, cache_key, cache_value, *refs):
    new_keys, new_values, out = refs[:chips], refs[chips : 2 * chips], refs[-1]
    scaling = math.log2(math.e) / math.sqrt(HD)
    count = query.shape[0]
    stored = cache_key.shape[2]
    old_seen = lax.broadcasted_iota(jnp.int32, (1, stored), 1) < place[2]
    ahead = lax.broadcasted_iota(jnp.int32, (count, count), 1) - lax.broadcasted_iota(
        jnp.int32, (count, count), 0
    )
    across = (((1,), (1,)), ((), ()))
    for g in range(groups):
        rows = query[:, g * HD : (g + 1) * HD]
        scores = lax.dot_general(rows, cache_key[0, 0], across, preferred_element_type=jnp.float32)
        scores = [jnp.where(old_seen, scores * scaling, NEGATIVE)]
        for k in range(chips):
            fresh = lax.dot_general(
                rows, new_keys[k][0], across, preferred_element_type=jnp.float32
            )
            gap = (place[1] - place[3 + k]) * count
            scores.append(jnp.where(ahead <= gap, fresh * scaling, NEGATIVE))
        top = jnp.max(scores[0], axis=-1, keepdims=True)
        for part in scores[1:]:
            top = jnp.maximum(top, jnp.max(part, axis=-1, keepdims=True))
        mix, total = 0.0, 0.0
        for part, values in zip(scores, [cache_value[0, 0], *[v[0] for v in new_values]]):
            weights = jnp.exp2(part - top)
            total += jnp.sum(weights, axis=-1, keepdims=True)
            mix += jnp.dot(weights.astype(jnp.bfloat16), values, preferred_element_type=jnp.float32)
        out[:, g * HD : (g + 1) * HD] = (mix / total).astype(jnp.bfloat16)


def fill_attend(place, query, cache, entries, heads, after=()):
    count = query.shape[0]
    groups = query.shape[1] // heads // HD
    stored = cache.shape[2]
    chips = len(entries)
    pairs = count * groups * heads * (stored + chips * count)
    return pl.pallas_call(
        functools.partial(fill_kernel, groups, chips),
        out_shape=jax.ShapeDtypeStruct(query.shape, jnp.bfloat16),
        grid_spec=pltpu.PrefetchScalarGridSpec(
            num_scalar_prefetch=1,
            grid=(heads,),
            in_specs=[
                pl.BlockSpec((count, groups * HD), lambda j, s: (0, j)),
                pl.BlockSpec((1, 1, stored, HD), lambda j, s: (0, 0, 0, j)),
                pl.BlockSpec((1, 1, stored, HD), lambda j, s: (1, 0, 0, j)),
            ]
            + [pl.BlockSpec((1, count, HD), lambda j, s: (0, 0, j))] * chips
            + [pl.BlockSpec((1, count, HD), lambda j, s: (1, 0, j))] * chips
            + [IN_PLACE] * len(after),
            out_specs=pl.BlockSpec((count, groups * HD), lambda j, s: (0, j)),
        ),
        compiler_params=params(12),
        cost_estimate=cost(8 * pairs * HD, 2 * cache.size, pairs),
        name="fill_attend",
    )(place, query, cache, cache, *entries, *entries, *after)


def step_kernel(
    heads, lengths, query, entries, cache, weight, out, held, scores, shares, weight_held, arrived, weight_sem
):
    scaling = 1.0 / math.sqrt(HD)
    slots, stored, width = cache.shape[1:]
    groups = query.shape[1] // width
    lanes = 8
    copies = [
        [pltpu.make_async_copy(cache.at[w, s], held.at[w, s], arrived.at[w, s]) for s in range(slots)]
        for w in range(2)
    ]
    weight_copy = pltpu.make_async_copy(weight, weight_held, weight_sem)
    for copy in copies[0] + copies[1] + [weight_copy]:
        copy.start()
    across = (((1,), (1,)), ((), ()))
    places = lax.broadcasted_iota(jnp.int32, (1, stored), 1)
    blank = jnp.zeros((1, HD), jnp.float32)
    new_keys = entries[0].astype(jnp.float32)
    new_values = entries[1].astype(jnp.float32)
    own_scores = []
    for s in range(slots):
        rows = []
        for j in range(heads):
            for g in range(groups):
                at = (j * groups + g) * HD
                part = query[s : s + 1, at : at + HD]
                rows.append(
                    jnp.concatenate([part if i == j else blank for i in range(heads)], axis=1)
                )
        rows.append(jnp.zeros((lanes - heads * groups, width), jnp.float32))
        rows = jnp.concatenate(rows, axis=0)
        own_scores.append(jnp.sum(rows * new_keys[s : s + 1], axis=-1, keepdims=True))
        copies[0][s].wait()
        old = lax.dot_general(
            rows.astype(jnp.bfloat16), held[0, s], across, preferred_element_type=jnp.float32
        )
        scores[s * lanes : (s + 1) * lanes, :] = jnp.where(
            places < lengths[s], old * scaling, NEGATIVE
        )
    old = scores[...]
    own = jnp.concatenate(own_scores, axis=0) * scaling
    top = jnp.maximum(jnp.max(old, axis=-1, keepdims=True), own)
    old = jnp.exp(old - top)
    own = jnp.exp(own - top)
    total = jnp.sum(old, axis=-1, keepdims=True) + own
    shares[...] = old / total
    own = (own / total).astype(jnp.bfloat16).astype(jnp.float32)
    attended = []
    for s in range(slots):
        copies[1][s].wait()
        here = slice(s * lanes, (s + 1) * lanes)
        mix = jnp.dot(
            shares[here, :].astype(jnp.bfloat16), held[1, s], preferred_element_type=jnp.float32
        )
        mix += own[here] * new_values[s : s + 1]
        parts = []
        for j in range(heads):
            for g in range(groups):
                row = j * groups + g
                parts.append(mix[row : row + 1, j * HD : (j + 1) * HD])
        attended.append(jnp.concatenate(parts, axis=1))
    if out.shape[0] > slots:
        attended.append(jnp.zeros((out.shape[0] - slots, query.shape[1]), jnp.float32))
    attended = jnp.concatenate(attended, axis=0).astype(jnp.bfloat16)
    weight_copy.wait()
    part = jnp.dot(attended, weight_held[...], preferred_element_type=jnp.float32)
    out[...] = part.astype(jnp.bfloat16)


def step_attend(lengths, query, entries, cache, weight, heads):
    slots, stored = cache.shape[1:3]
    padded = query.shape[0]
    rows = slots * 8
    return pl.pallas_call(
        functools.partial(step_kernel, heads),
        out_shape=jax.ShapeDtypeStruct((padded, weight.shape[1]), jnp.bfloat16),
        in_specs=[SMEM_WHOLE, VMEM_WHOLE, VMEM_WHOLE, IN_PLACE, IN_PLACE],
        out_specs=VMEM_WHOLE,
        scratch_shapes=[
            pltpu.VMEM(cache.shape, jnp.bfloat16),
            pltpu.VMEM((rows, stored), jnp.float32),
            pltpu.VMEM((rows, stored), jnp.float32),
            pltpu.VMEM(weight.shape, jnp.bfloat16),
            pltpu.SemaphoreType.DMA((2, slots)),
            pltpu.SemaphoreType.DMA(()),
        ],
        compiler_params=params(20),
        cost_estimate=cost(16 * cache.size, 2 * cache.size, rows * stored),
        name="step_attend",
    )(lengths, query, entries, cache, weight)


def out_kernel(place, mine, sib, weight, sib_weight, *refs):
    out = refs[-1]
    half = out.shape[1]
    cols = pl.ds(pl.multiple_of(place[0] * half, half), half)
    part = jnp.dot(mine[...], weight[:, cols], preferred_element_type=jnp.float32)
    part += jnp.dot(sib[...], sib_weight[:, cols], preferred_element_type=jnp.float32)
    out[...] = part.astype(jnp.bfloat16)


def out_project(place, mine, sib, weight, sib_weight, after=()):
    rows, depth = mine.shape
    half = weight.shape[1] // 2
    return pl.pallas_call(
        out_kernel,
        out_shape=jax.ShapeDtypeStruct((rows, half), jnp.bfloat16),
        in_specs=[SMEM_WHOLE] + [VMEM_WHOLE] * 4 + [IN_PLACE] * len(after),
        out_specs=VMEM_WHOLE,
        compiler_params=params(8),
        cost_estimate=cost(4 * rows * depth * half, 4 * depth * half + 6 * rows * half),
        name="out_project",
    )(place, mine, sib, weight, sib_weight, *after)


def forward_kernel(loads, chips, n_dec, n_weights, n_after, chunk, place, *refs):
    refs = list(refs)
    mine, sib = refs[:2]
    shares = refs[2 : 2 + 2 * chips]
    refs = refs[2 + 2 * chips :]
    if n_dec:
        dec, dec_shares = refs[0], refs[1 : 1 + 2 * chips]
        refs = refs[1 + 2 * chips :]
    split = n_weights == 2
    gain, *weights = refs[: 1 + n_weights]
    refs = refs[1 + n_weights + n_after :]
    if split:
        resid, hidden = refs[:2]
        held, inner = refs[2:]
    else:
        keep, give, resid = refs[:3]
        refs = refs[3:]
        if n_dec:
            dec_out, dec_resid = refs[:2]
            refs = refs[2:]
        if loads:
            weights, refs = list(zip(weights, refs[:3])), refs[3:]
        held, inner, hidden = refs[:3]
    copies = []
    if loads:
        arrived = refs[3]
        copies = [
            [
                pltpu.make_async_copy(
                    source.at[:, pl.ds(i * chunk, chunk)], target.at[i], arrived.at[w, i]
                )
                for i in range(target.shape[0])
            ]
            for w, (source, target) in enumerate(weights)
        ]
        weights = [target for _, target in weights]
        for pair in zip(copies[0], copies[1]):
            for copy in pair:
                copy.start()
        for copy in copies[2]:
            copy.start()

    def ready(w, i):
        if loads:
            copies[w][i].wait()
        return weights[w][i]

    piece = mine.shape[0]
    half = shares[0].shape[1]
    core = place[0]
    for rows, at_rows, put in ((mine, core, 0), (sib, 1 - core, piece)):
        here = pl.ds(pl.multiple_of(at_rows * piece, piece), piece)
        for side in range(2):
            at = core if side == 0 else 1 - core
            cols = pl.ds(pl.multiple_of(at * half, half), half)
            added = shares[side][here, :].astype(jnp.float32)
            for k in range(1, chips):
                added += shares[2 * k + side][here, :].astype(jnp.float32)
            value = rows[:, cols].astype(jnp.float32) + added
            held[put : put + piece, cols] = value.astype(jnp.bfloat16)
    if n_dec:
        added = dec_shares[0][...].astype(jnp.float32)
        for share in dec_shares[1:]:
            added += share[...].astype(jnp.float32)
        held[2 * piece :, :] = (dec[...].astype(jnp.float32) + added).astype(jnp.bfloat16)
    for put in range(0, held.shape[0], piece):
        here = slice(put, min(put + piece, held.shape[0]))
        inner[here, :] = normed(held[here, :].astype(jnp.float32), gain[...])
    resid[...] = held[:piece, :]
    if n_dec:
        dec_resid[...] = held[2 * piece :, :]

    for i in range(weights[0].shape[0]):
        at = slice(i * chunk, (i + 1) * chunk)
        gated = jnp.dot(inner[...], ready(0, i), preferred_element_type=jnp.float32)
        raised = jnp.dot(inner[...], ready(1, i), preferred_element_type=jnp.float32)
        hidden[:, at] = (gated / (1.0 + jnp.exp(-gated)) * raised).astype(jnp.bfloat16)
    for i in range(0 if split else weights[2].shape[0]):
        at = slice(i * chunk, (i + 1) * chunk)
        part = jnp.dot(hidden[...], ready(2, i), preferred_element_type=jnp.float32)
        part = part.astype(jnp.bfloat16)
        keep[:, at] = part[:piece]
        give[:, at] = part[piece : 2 * piece]
        if n_dec:
            dec_out[:, at] = part[2 * piece :]


def lower_kernel(hidden, down, *refs):
    keep, give = refs[-2:]
    piece = keep.shape[0]
    chunk = down.shape[2]
    for i in range(down.shape[0]):
        at = slice(i * chunk, (i + 1) * chunk)
        part = jnp.dot(hidden[...], down[i], preferred_element_type=jnp.float32)
        part = part.astype(jnp.bfloat16)
        keep[:, at] = part[:piece]
        give[:, at] = part[piece:]


def lower(hidden, down, after):
    rows, units = hidden.shape
    width = down.shape[0] * down.shape[2]
    return pl.pallas_call(
        lower_kernel,
        out_shape=[jax.ShapeDtypeStruct((rows // 2, width), jnp.bfloat16)] * 2,
        in_specs=[VMEM_WHOLE] * 2 + [IN_PLACE] * len(after),
        out_specs=[VMEM_WHOLE] * 2,
        compiler_params=params(8),
        cost_estimate=cost(2 * rows * width * units, 2 * width * units),
        name="lower",
    )(hidden, down, *after)


def feed_forward(place, mine, sib, shares, gain, weights, loads, dec=None, dec_shares=None, after=()):
    piece, width = mine.shape
    chips = len(shares) // 2
    n_dec = 0 if dec is None else dec.shape[0]
    rows = 2 * piece + n_dec
    args = [mine, sib, *shares]
    if n_dec:
        args += [dec, *dec_shares]
    args += [gain]
    split = len(weights) == 2
    chunk = width // 4 if loads else weights[0].shape[2]
    units = weights[0].shape[1] if loads else weights[0].shape[0] * chunk
    if split:
        shapes = [(piece, width), (rows, units)]
    else:
        shapes = [(n, width) for n in [piece] * 3 + [n_dec] * 2 * bool(n_dec)]
    out_shape = [jax.ShapeDtypeStruct(shape, jnp.bfloat16) for shape in shapes]
    scratch = [pltpu.VMEM((rows, width), jnp.bfloat16)] * 2
    if not split:
        scratch.append(pltpu.VMEM((rows, units), jnp.bfloat16))
    if loads:
        out_shape += [stays_in_vmem((units // chunk, width, chunk))] * 2
        out_shape += [stays_in_vmem((width // chunk, units, chunk))]
        scratch.append(pltpu.SemaphoreType.DMA((3, max(units, width) // chunk)))
    return pl.pallas_call(
        functools.partial(forward_kernel, loads, chips, n_dec, len(weights), len(after), chunk),
        out_shape=out_shape,
        in_specs=[SMEM_WHOLE]
        + [VMEM_WHOLE] * len(args)
        + [IN_PLACE if loads else VMEM_WHOLE] * len(weights)
        + [IN_PLACE] * len(after),
        out_specs=[VMEM_WHOLE] * len(out_shape),
        scratch_shapes=scratch,
        compiler_params=params(14),
        cost_estimate=cost(6 * rows * width * units, 6 * width * units, rows * units),
        name="feed_forward",
    )(place, *args, *weights, *after)


def angle_tables(places):
    halfway = HD // 2
    powers = jnp.arange(halfway, dtype=jnp.float32) * (2.0 / HD)
    inverse = THETA ** (-powers)
    angles = places.astype(jnp.float32)[:, None] * inverse[None, :]
    cosine, sine = jnp.cos(angles), jnp.sin(angles)
    return jnp.concatenate([cosine, cosine], axis=-1), jnp.concatenate([-sine, sine], axis=-1)


def add(*values):
    total = values[0].astype(jnp.float32)
    for value in values[1:]:
        total = total + value.astype(jnp.float32)
    return total.astype(jnp.bfloat16)


def on_device(
    prefill_rows,
    decode_rows,
    deal_order,
    prefill_offset,
    cache_length,
    prefill_cache,
    decode_cache,
    qkv_weight,
    out_weight,
    attention_gain,
    forward_gain,
    gate_weight,
    up_weight,
    down_weight,
):
    tensor_count = lax.axis_size("tensor")
    dp_count = lax.axis_size("dp")
    chips = tensor_count // 2
    tensor_place = lax.axis_index("tensor")
    group_place = lax.axis_index("dp")
    chip, core = tensor_place // 2, tensor_place % 2
    piece, width = prefill_rows.shape
    per_device = decode_rows.shape[0]
    requests = deal_order.shape[0]
    slots = cache_length.shape[0]
    padded = -(-slots // 16) * 16
    heads = qkv_weight.shape[1]
    tokens = piece * tensor_count

    def place_of(k):
        spots = [core, (chip + k) % chips, prefill_offset[0]]
        return jnp.stack(spots + [(chip + j) % chips for j in range(chips)]).astype(jnp.int32)

    places = [place_of(k) for k in range(chips)]
    weight = in_hbm(qkv_weight.reshape(width, -1))
    gate_weight, up_weight, down_weight = map(in_hbm, (gate_weight, up_weight, down_weight))
    prefill_cache, decode_cache = in_hbm(prefill_cache), in_hbm(decode_cache)

    mines = [prefill_rows] + [from_chip(prefill_rows, k) for k in range(1, chips)]
    sibs = [swap_cores(rows) for rows in mines]

    low = max(dp_count // 4, 1)
    pool = [decode_rows] + [swap_groups(decode_rows, i) for i in range(1, low)]
    pool = jnp.concatenate(pool, axis=0)
    pool = [pool] + [swap_groups(pool, i * low) for i in range(1, dp_count // low)]
    pool = jnp.concatenate(pool, axis=0)
    index = jnp.arange(dp_count * per_device, dtype=jnp.int32)
    origin = jnp.bitwise_xor(group_place, index // per_device)
    request = (origin * tensor_count + tensor_place) * per_device + index % per_device
    slot_of = jnp.sum(
        jnp.where(
            request[:, None] == jnp.arange(requests, dtype=jnp.int32)[None, :],
            deal_order[None, :],
            0,
        ),
        axis=1,
    )
    in_group = slot_of - group_place * slots
    chooser = (jnp.arange(padded, dtype=jnp.int32)[:, None] == in_group[None, :]) & (
        in_group[None, :] < slots
    )
    dealt = jnp.dot(
        chooser.astype(jnp.bfloat16), pool, preferred_element_type=jnp.float32
    ).astype(jnp.bfloat16)

    gain = attention_gain.reshape(1, width)
    tables = angle_tables(prefill_offset[0] + jnp.arange(tokens, dtype=jnp.int32))
    dec_tables = angle_tables(jnp.pad(cache_length, (0, padded - slots)))
    queries, entries, everything = [None] * chips, [None] * chips, None
    for k in range(chips):
        last = k == chips - 1
        if last:
            others = from_rest(dealt)
            if k:
                *others, queries[k - 1] = lax.optimization_barrier((*others, queries[k - 1]))
            dealt = add(dealt, *others)
        got = project(
            places[k],
            in_hbm(mines[k]),
            in_hbm(sibs[k]),
            gain,
            weight,
            tables,
            heads,
            everything,
            dealt if last else None,
            dec_tables if last else None,
            slots,
            [queries[k - 1]] if k else [dealt],
        )
        queries[k], entries[k], everything = got[:3]
        if last:
            dec_query, dec_entries = got[3:]

    out_share = out_weight
    sib_weight, queries[-1] = lax.optimization_barrier((out_weight, queries[-1]))
    sib_weight = in_vmem(swap_cores(sib_weight))
    out_weight = in_vmem(out_weight)

    def finish(attended, place, before):
        attended, *before = lax.optimization_barrier((attended, *before))
        sib = swap_cores(attended)
        return out_project(place, attended, sib, out_weight, sib_weight), before

    parts = []
    dec_shares = []
    for k in range(chips):
        attended = fill_attend(
            places[k], queries[k], prefill_cache, entries, heads, dec_shares[:1]
        )
        part, dec_shares[1:] = finish(attended, places[k], dec_shares[1:])
        parts.append(part)
        if k == 0:
            lengths, parts[0] = lax.optimization_barrier((cache_length, parts[0]))
            dec_part = step_attend(
                lengths, dec_query, dec_entries, decode_cache, in_hbm(out_share), heads
            )
            dec_shares = [dec_part, *from_rest(dec_part)]

    def shares_of(own, others):
        pairs = []
        for value in [own, *others]:
            pairs += [value, swap_cores(value)]
        return pairs

    gain = forward_gain.reshape(1, width)
    order = [*range(1, chips), 0]

    def fetch(b):
        return [from_chip(parts[(b - j) % chips], j) for j in range(1, chips)]

    theirs = fetch(order[0])
    weights = [gate_weight, up_weight, down_weight]
    arrived, sent = [], []
    for n, b in enumerate(order):
        got = feed_forward(
            places[b],
            mines[b],
            sibs[b],
            shares_of(parts[b], theirs),
            gain,
            weights if n + 1 < chips else weights[:2],
            n == 0,
            dealt if n == 0 else None,
            dec_shares if n == 0 else None,
            sent,
        )
        if n + 1 < chips:
            keep, give = got[:2]
            *theirs, keep = lax.optimization_barrier((*fetch(order[n + 1]), keep))
            both = add(keep, swap_cores(give))
            arrived.append(from_chip(both, chips - b))
            sent = [both]
        if n == 0:
            dec_sum, dec_resid, *weights = got[3:]
            dec_others = from_rest(dec_sum)
    resid, hidden = got
    dec_sum, hidden = lax.optimization_barrier((dec_sum, hidden))
    final = add(dec_resid, dec_sum, *dec_others)
    picker = in_group[:, None] == jnp.arange(padded, dtype=jnp.int32)[None, :]
    picker = picker & (in_group[:, None] < slots)
    routed = jnp.dot(
        picker.astype(jnp.bfloat16), final, preferred_element_type=jnp.float32
    ).astype(jnp.bfloat16)
    keep, give = lower(hidden, weights[2], [routed])
    low = max(dp_count // 4, 1)
    pairs = routed.reshape(dp_count // low, low * per_device, width)
    rows = add(
        pairs[0], *[swap_groups(pairs[i], i * low) for i in range(1, dp_count // low)]
    )
    *arrived, rows, give = lax.optimization_barrier((*arrived, rows, give))
    pairs = rows.reshape(low, per_device, width)
    routed = add(pairs[0], *[swap_groups(pairs[i], i) for i in range(1, low)])

    prefill_out = add(resid, keep, swap_cores(give), *arrived)
    return (prefill_out, routed, everything, dec_entries)


def solution(mesh):
    placed = (
        P(("dp", "tensor"), None),
        P(("dp", "tensor"), None),
        P(),
        P("dp"),
        P("dp"),
        P(None, "dp", None, "tensor"),
        P(None, "dp", None, "tensor"),
        P(None, "tensor", None),
        P("tensor", None),
        P(),
        P(),
        P(None, "tensor"),
        P(None, "tensor"),
        P("tensor", None),
    )
    return jax.shard_map(
        on_device,
        mesh=mesh,
        in_specs=placed,
        out_specs=(
            P(("dp", "tensor"), None),
            P(("dp", "tensor"), None),
            P(None, "dp", "tensor"),
            P(None, "dp", "tensor"),
        ),
        check_vma=False,
    )
```

```python
import functools
import math

import jax
import jax.numpy as jnp
from jax import lax
from jax.experimental import pallas as pl
from jax.experimental.pallas import tpu as pltpu
from jax.sharding import PartitionSpec as P

HD = 128
EPSILON = 1e-06
THETA = 1000000.0
NEGATIVE = -1e30
MIB = 1 << 20


def swap_cores(value):
    count = lax.axis_size("tensor")
    return lax.ppermute(value, "tensor", [(i, i ^ 1) for i in range(count)])


def from_chip(value, step):
    count = lax.axis_size("tensor")
    chips = count // 2
    return lax.ppermute(
        value, "tensor", [(i, (i // 2 - step) % chips * 2 + i % 2) for i in range(count)]
    )


def from_other(value, step):
    count = lax.axis_size("tensor")
    return lax.ppermute(
        value, "tensor", [(i, (i // 2 - step) % (count // 2) * 2 + 1 - i % 2) for i in range(count)]
    )


def from_rest(value):
    chips = lax.axis_size("tensor") // 2
    return [from_chip(value, k) for k in range(1, chips)] + [from_other(value, k) for k in range(chips)]


def swap_groups(value, mask):
    count = lax.axis_size("dp")
    return lax.ppermute(value, "dp", [(i, i ^ mask) for i in range(count)])


def whole(shape):
    return pl.BlockSpec(shape, lambda *_: (0,) * len(shape))


def params(mib):
    return pltpu.CompilerParams(vmem_limit_bytes=mib * MIB)


def cost(flops, moved, exps=0):
    return pl.CostEstimate(flops=int(flops), bytes_accessed=int(moved), transcendentals=int(exps))


def normed(values, gain):
    spread = jnp.mean(values * values, axis=-1, keepdims=True)
    return (values * lax.rsqrt(spread + EPSILON) * gain).astype(jnp.bfloat16)


def turn(vectors, cosine, sine):
    return vectors * cosine + pltpu.roll(vectors, HD // 2, 1) * sine


def in_vmem(value):
    return pltpu.with_memory_space_constraint(value, pltpu.VMEM)


def in_hbm(value):
    return pltpu.with_memory_space_constraint(value, pltpu.HBM)


def stays_in_vmem(shape):
    return pltpu.VMEM(shape, jnp.bfloat16)


VMEM_WHOLE = pl.BlockSpec(memory_space=pltpu.VMEM)
SMEM_WHOLE = pl.BlockSpec(memory_space=pltpu.SMEM)
IN_PLACE = pl.BlockSpec(memory_space=pl.ANY)


def project_kernel(n_dec, n_after, groups, heads, place, *refs):
    refs = list(refs)
    mine, sib, weight, gain, cosine, sine = refs[:6]
    refs = refs[6:]
    if n_dec:
        dec, dec_cos, dec_sin = refs[:3]
        refs = refs[3:]
    refs = refs[n_after:]
    query, entries, everything = refs[:3]
    if n_dec:
        dec_query, dec_entries = refs[3:5]
    inner, rows_held, weight_held, row_sems, weight_sems, out_sem = refs[-6:]
    piece = mine.shape[0]
    core = place[0]
    scale = gain[...]
    depth = (groups + 2) * HD
    row_copies = [
        pltpu.make_async_copy(ref, rows_held.at[i], row_sems.at[i])
        for i, ref in enumerate((mine, sib))
    ]
    weight_copies = [
        pltpu.make_async_copy(
            weight.at[:, pl.ds(j * depth, depth)], weight_held.at[j], weight_sems.at[j]
        )
        for j in range(heads)
    ]
    for copy in row_copies + weight_copies:
        copy.start()
    for i, at in enumerate((core, 1 - core)):
        row_copies[i].wait()
        start = pl.multiple_of(at * piece, piece)
        inner[pl.ds(start, piece), :] = normed(rows_held[i].astype(jnp.float32), scale)
    if n_dec:
        inner[2 * piece :, :] = normed(dec[...].astype(jnp.float32), scale)
    here = pl.ds(pl.multiple_of(place[1] * 2 * piece, 2 * piece), 2 * piece)
    for j in range(heads):
        weight_copies[j].wait()
        mixed = jnp.dot(inner[...], weight_held[j], preferred_element_type=jnp.float32)

        def put(rows, cos, sin, query_out, entry_out):
            for g in range(groups):
                part = rows[:, g * HD : (g + 1) * HD]
                at = (j * groups + g) * HD
                turned = turn(part, cos, sin).astype(jnp.bfloat16)
                query_out[:, at : at + HD] = turned.astype(query_out.dtype)
            key = turn(rows[:, groups * HD : (groups + 1) * HD], cos, sin).astype(jnp.bfloat16)
            value = rows[:, (groups + 1) * HD :].astype(jnp.bfloat16)
            size = entry_out.shape[1]
            entry_out[0, :, j * HD : (j + 1) * HD] = key[:size]
            entry_out[1, :, j * HD : (j + 1) * HD] = value[:size]

        put(mixed[: 2 * piece], cosine[here, :], sine[here, :], query, entries)
        if n_dec:
            put(mixed[2 * piece :], dec_cos[...], dec_sin[...], dec_query, dec_entries)
    keep = pltpu.make_async_copy(entries, everything.at[:, here, :], out_sem)
    keep.start()
    keep.wait()


def project(
    place, mine, sib, gain, weight, tables, heads, everything, dec=None, dec_tables=None, slots=0, after=()
):
    piece, width = mine.shape
    depth = weight.shape[1] // heads
    groups = depth // HD - 2
    block = 2 * piece
    n_dec = 0 if dec is None else dec.shape[0]
    args = [mine, sib, weight, gain, *tables]
    if n_dec:
        args += [dec, *dec_tables]
    n_operands = len(args)
    after = list(after)
    aliases = {}
    if everything is not None:
        after.append(everything)
        aliases = {n_operands + len(after): 2}
    wide = heads * groups * HD
    out_shape = [
        jax.ShapeDtypeStruct((block, wide), jnp.bfloat16),
        jax.ShapeDtypeStruct((2, block, heads * HD), jnp.bfloat16),
        jax.ShapeDtypeStruct((2, tables[0].shape[0], heads * HD), jnp.bfloat16),
    ]
    if n_dec:
        out_shape += [
            jax.ShapeDtypeStruct((n_dec, wide), jnp.float32),
            jax.ShapeDtypeStruct((2, slots, heads * HD), jnp.bfloat16),
        ]
    rows = block + n_dec
    return pl.pallas_call(
        functools.partial(project_kernel, n_dec, len(after), groups, heads),
        out_shape=out_shape,
        in_specs=[SMEM_WHOLE]
        + [IN_PLACE] * 3
        + [VMEM_WHOLE] * (len(args) - 3)
        + [IN_PLACE] * len(after),
        out_specs=[VMEM_WHOLE] * 2 + [IN_PLACE] + [VMEM_WHOLE] * (len(out_shape) - 3),
        scratch_shapes=[
            pltpu.VMEM((rows, width), jnp.bfloat16),
            pltpu.VMEM((2, piece, width), jnp.bfloat16),
            pltpu.VMEM((heads, width, depth), jnp.bfloat16),
            pltpu.SemaphoreType.DMA((2,)),
            pltpu.SemaphoreType.DMA((heads,)),
            pltpu.SemaphoreType.DMA(()),
        ],
        input_output_aliases=aliases,
        compiler_params=params(20),
        cost_estimate=cost(2 * rows * weight.size, 2 * (weight.size + 2 * rows * width)),
        name="project",
    )(place, *args, *after)


def fill_kernel(groups, chips, chunk, place, query, cache_key, cache_value, *refs):
    new_keys, new_values = refs[:chips], refs[chips : 2 * chips]
    source, (out, target, arrived) = refs[2 * chips], refs[-3:]
    pieces = [
        source.at[:, pl.ds(i * chunk, chunk)] if chunk else source.at[i]
        for i in range(target.shape[0])
    ]
    copies = [
        pltpu.make_async_copy(piece, target.at[i], arrived.at[i]) for i, piece in enumerate(pieces)
    ]

    @pl.when(pl.program_id(0) == 0)
    def _():
        for copy in copies:
            copy.start()

    scaling = math.log2(math.e) / math.sqrt(HD)
    count = query.shape[0]
    stored = cache_key.shape[2]
    old_seen = lax.broadcasted_iota(jnp.int32, (1, stored), 1) < place[2]
    ahead = lax.broadcasted_iota(jnp.int32, (count, count), 1) - lax.broadcasted_iota(
        jnp.int32, (count, count), 0
    )
    across = (((1,), (1,)), ((), ()))
    for g in range(groups):
        rows = query[:, g * HD : (g + 1) * HD]
        scores = lax.dot_general(rows, cache_key[0, 0], across, preferred_element_type=jnp.float32)
        scores = [jnp.where(old_seen, scores * scaling, NEGATIVE)]
        for k in range(chips):
            fresh = lax.dot_general(
                rows, new_keys[k][0], across, preferred_element_type=jnp.float32
            )
            gap = (place[1] - place[3 + k]) * count
            scores.append(jnp.where(ahead <= gap, fresh * scaling, NEGATIVE))
        top = jnp.max(scores[0], axis=-1, keepdims=True)
        for part in scores[1:]:
            top = jnp.maximum(top, jnp.max(part, axis=-1, keepdims=True))
        mix, total = 0.0, 0.0
        for part, values in zip(scores, [cache_value[0, 0], *[v[0] for v in new_values]]):
            weights = jnp.exp2(part - top)
            total += jnp.sum(weights, axis=-1, keepdims=True)
            mix += jnp.dot(weights.astype(jnp.bfloat16), values, preferred_element_type=jnp.float32)
        out[:, g * HD : (g + 1) * HD] = (mix / total).astype(jnp.bfloat16)

    @pl.when(pl.program_id(0) == pl.num_programs(0) - 1)
    def _():
        for copy in copies:
            copy.wait()


def fill_attend(place, query, cache, entries, heads, source, chunk, after=()):
    count = query.shape[0]
    groups = query.shape[1] // heads // HD
    stored = cache.shape[2]
    chips = len(entries)
    pairs = count * groups * heads * (stored + chips * count)
    target = (source.shape[1] // chunk, source.shape[0], chunk) if chunk else source.shape
    return pl.pallas_call(
        functools.partial(fill_kernel, groups, chips, chunk),
        out_shape=[jax.ShapeDtypeStruct(query.shape, jnp.bfloat16), stays_in_vmem(target)],
        grid_spec=pltpu.PrefetchScalarGridSpec(
            num_scalar_prefetch=1,
            grid=(heads,),
            in_specs=[
                pl.BlockSpec((count, groups * HD), lambda j, s: (0, j)),
                pl.BlockSpec((1, 1, stored, HD), lambda j, s: (0, 0, 0, j)),
                pl.BlockSpec((1, 1, stored, HD), lambda j, s: (1, 0, 0, j)),
            ]
            + [pl.BlockSpec((1, count, HD), lambda j, s: (0, 0, j))] * chips
            + [pl.BlockSpec((1, count, HD), lambda j, s: (1, 0, j))] * chips
            + [IN_PLACE] * (1 + len(after)),
            out_specs=[pl.BlockSpec((count, groups * HD), lambda j, s: (0, j)), IN_PLACE],
            scratch_shapes=[pltpu.SemaphoreType.DMA((target[0],))],
        ),
        compiler_params=params(12),
        cost_estimate=cost(8 * pairs * HD, 2 * cache.size, pairs),
        name="fill_attend",
    )(place, query, cache, cache, *entries, *entries, source, *after)


def step_kernel(heads, lengths, query, entries, held, weight, out, scores, shares, weight_held, weight_sem):
    scaling = 1.0 / math.sqrt(HD)
    slots, stored, width = held.shape[1:]
    groups = query.shape[1] // width
    lanes = 8
    weight_copy = pltpu.make_async_copy(weight, weight_held, weight_sem)
    weight_copy.start()
    across = (((1,), (1,)), ((), ()))
    places = lax.broadcasted_iota(jnp.int32, (1, stored), 1)
    blank = jnp.zeros((1, HD), jnp.float32)
    new_keys = entries[0].astype(jnp.float32)
    new_values = entries[1].astype(jnp.float32)
    own_scores = []
    for s in range(slots):
        rows = []
        for j in range(heads):
            for g in range(groups):
                at = (j * groups + g) * HD
                part = query[s : s + 1, at : at + HD]
                rows.append(
                    jnp.concatenate([part if i == j else blank for i in range(heads)], axis=1)
                )
        rows.append(jnp.zeros((lanes - heads * groups, width), jnp.float32))
        rows = jnp.concatenate(rows, axis=0)
        own_scores.append(jnp.sum(rows * new_keys[s : s + 1], axis=-1, keepdims=True))
        old = lax.dot_general(
            rows.astype(jnp.bfloat16), held[0, s], across, preferred_element_type=jnp.float32
        )
        scores[s * lanes : (s + 1) * lanes, :] = jnp.where(
            places < lengths[s], old * scaling, NEGATIVE
        )
    old = scores[...]
    own = jnp.concatenate(own_scores, axis=0) * scaling
    top = jnp.maximum(jnp.max(old, axis=-1, keepdims=True), own)
    old = jnp.exp(old - top)
    own = jnp.exp(own - top)
    total = jnp.sum(old, axis=-1, keepdims=True) + own
    shares[...] = old / total
    own = (own / total).astype(jnp.bfloat16).astype(jnp.float32)
    attended = []
    for s in range(slots):
        here = slice(s * lanes, (s + 1) * lanes)
        mix = jnp.dot(
            shares[here, :].astype(jnp.bfloat16), held[1, s], preferred_element_type=jnp.float32
        )
        mix += own[here] * new_values[s : s + 1]
        parts = []
        for j in range(heads):
            for g in range(groups):
                row = j * groups + g
                parts.append(mix[row : row + 1, j * HD : (j + 1) * HD])
        attended.append(jnp.concatenate(parts, axis=1))
    if out.shape[0] > slots:
        attended.append(jnp.zeros((out.shape[0] - slots, query.shape[1]), jnp.float32))
    attended = jnp.concatenate(attended, axis=0).astype(jnp.bfloat16)
    weight_copy.wait()
    part = jnp.dot(attended, weight_held[...], preferred_element_type=jnp.float32)
    out[...] = part.astype(jnp.bfloat16)


def step_attend(lengths, query, entries, cache, weight, heads):
    slots, stored = cache.shape[1:3]
    padded = query.shape[0]
    rows = slots * 8
    return pl.pallas_call(
        functools.partial(step_kernel, heads),
        out_shape=jax.ShapeDtypeStruct((padded, weight.shape[1]), jnp.bfloat16),
        in_specs=[SMEM_WHOLE] + [VMEM_WHOLE] * 3 + [IN_PLACE],
        out_specs=VMEM_WHOLE,
        scratch_shapes=[
            pltpu.VMEM((rows, stored), jnp.float32),
            pltpu.VMEM((rows, stored), jnp.float32),
            pltpu.VMEM(weight.shape, jnp.bfloat16),
            pltpu.SemaphoreType.DMA(()),
        ],
        compiler_params=params(12),
        cost_estimate=cost(16 * cache.size, 2 * cache.size, rows * stored),
        name="step_attend",
    )(lengths, query, entries, cache, weight)


def out_kernel(place, mine, sib, weight, sib_weight, *refs):
    out = refs[-1]
    half = out.shape[1]
    cols = pl.ds(pl.multiple_of(place[0] * half, half), half)
    part = jnp.dot(mine[...], weight[:, cols], preferred_element_type=jnp.float32)
    part += jnp.dot(sib[...], sib_weight[:, cols], preferred_element_type=jnp.float32)
    out[...] = part.astype(jnp.bfloat16)


def out_project(place, mine, sib, weight, sib_weight, after=()):
    rows, depth = mine.shape
    half = weight.shape[1] // 2
    return pl.pallas_call(
        out_kernel,
        out_shape=jax.ShapeDtypeStruct((rows, half), jnp.bfloat16),
        in_specs=[SMEM_WHOLE] + [VMEM_WHOLE] * 4 + [IN_PLACE] * len(after),
        out_specs=VMEM_WHOLE,
        compiler_params=params(8),
        cost_estimate=cost(4 * rows * depth * half, 4 * depth * half + 6 * rows * half),
        name="out_project",
    )(place, mine, sib, weight, sib_weight, *after)


def forward_kernel(loads, chips, n_dec, n_weights, n_after, chunk, place, *refs):
    refs = list(refs)
    mine, sib = refs[:2]
    shares = refs[2 : 2 + 2 * chips]
    refs = refs[2 + 2 * chips :]
    if n_dec:
        dec, dec_shares = refs[0], refs[1 : 1 + 2 * chips]
        refs = refs[1 + 2 * chips :]
    split = n_weights == 2
    gain, *weights = refs[: 1 + n_weights]
    refs = refs[1 + n_weights + n_after :]
    if split:
        resid, hidden = refs[:2]
        held, inner = refs[2:]
    else:
        keep, give, resid = refs[:3]
        refs = refs[3:]
        if n_dec:
            dec_out, dec_resid = refs[:2]
            refs = refs[2:]
        if loads:
            sources, weights[1:], refs = weights[1:], refs[:2], refs[2:]
        held, inner, hidden = refs[:3]
    copies = {}
    if loads:
        arrived = refs[3]
        for w, source in enumerate(sources, 1):
            for i in range(weights[w].shape[0]):
                copies[w, i] = pltpu.make_async_copy(
                    source.at[:, pl.ds(i * chunk, chunk)], weights[w].at[i], arrived.at[w - 1, i]
                )
                copies[w, i].start()

    def ready(w, i):
        if (w, i) in copies:
            copies[w, i].wait()
        return weights[w][i]

    piece = mine.shape[0]
    half = shares[0].shape[1]
    core = place[0]
    for rows, at_rows, put in ((mine, core, 0), (sib, 1 - core, piece)):
        here = pl.ds(pl.multiple_of(at_rows * piece, piece), piece)
        for side in range(2):
            at = core if side == 0 else 1 - core
            cols = pl.ds(pl.multiple_of(at * half, half), half)
            added = shares[side][here, :].astype(jnp.float32)
            for k in range(1, chips):
                added += shares[2 * k + side][here, :].astype(jnp.float32)
            value = rows[:, cols].astype(jnp.float32) + added
            held[put : put + piece, cols] = value.astype(jnp.bfloat16)
    if n_dec:
        added = dec_shares[0][...].astype(jnp.float32)
        for share in dec_shares[1:]:
            added += share[...].astype(jnp.float32)
        held[2 * piece :, :] = (dec[...].astype(jnp.float32) + added).astype(jnp.bfloat16)
    for put in range(0, held.shape[0], piece):
        here = slice(put, min(put + piece, held.shape[0]))
        inner[here, :] = normed(held[here, :].astype(jnp.float32), gain[...])
    resid[...] = held[:piece, :]
    if n_dec:
        dec_resid[...] = held[2 * piece :, :]

    for i in range(weights[0].shape[0]):
        at = slice(i * chunk, (i + 1) * chunk)
        gated = jnp.dot(inner[...], ready(0, i), preferred_element_type=jnp.float32)
        raised = jnp.dot(inner[...], ready(1, i), preferred_element_type=jnp.float32)
        hidden[:, at] = (gated / (1.0 + jnp.exp(-gated)) * raised).astype(jnp.bfloat16)
    for i in range(0 if split else weights[2].shape[0]):
        at = slice(i * chunk, (i + 1) * chunk)
        part = jnp.dot(hidden[...], ready(2, i), preferred_element_type=jnp.float32)
        part = part.astype(jnp.bfloat16)
        keep[:, at] = part[:piece]
        give[:, at] = part[piece : 2 * piece]
        if n_dec:
            dec_out[:, at] = part[2 * piece :]


def lower_kernel(hidden, down, *refs):
    keep, give = refs[-2:]
    piece = keep.shape[0]
    chunk = down.shape[2]
    for i in range(down.shape[0]):
        at = slice(i * chunk, (i + 1) * chunk)
        part = jnp.dot(hidden[...], down[i], preferred_element_type=jnp.float32)
        part = part.astype(jnp.bfloat16)
        keep[:, at] = part[:piece]
        give[:, at] = part[piece:]


def lower(hidden, down, after):
    rows, units = hidden.shape
    width = down.shape[0] * down.shape[2]
    return pl.pallas_call(
        lower_kernel,
        out_shape=[jax.ShapeDtypeStruct((rows // 2, width), jnp.bfloat16)] * 2,
        in_specs=[VMEM_WHOLE] * 2 + [IN_PLACE] * len(after),
        out_specs=[VMEM_WHOLE] * 2,
        compiler_params=params(8),
        cost_estimate=cost(2 * rows * width * units, 2 * width * units),
        name="lower",
    )(hidden, down, *after)


def feed_forward(place, mine, sib, shares, gain, weights, loads, dec=None, dec_shares=None, after=()):
    piece, width = mine.shape
    chips = len(shares) // 2
    n_dec = 0 if dec is None else dec.shape[0]
    rows = 2 * piece + n_dec
    args = [mine, sib, *shares]
    if n_dec:
        args += [dec, *dec_shares]
    args += [gain]
    split = len(weights) == 2
    chunk = weights[0].shape[2]
    units = weights[0].shape[0] * chunk
    if split:
        shapes = [(piece, width), (rows, units)]
    else:
        shapes = [(n, width) for n in [piece] * 3 + [n_dec] * 2 * bool(n_dec)]
    out_shape = [jax.ShapeDtypeStruct(shape, jnp.bfloat16) for shape in shapes]
    scratch = [pltpu.VMEM((rows, width), jnp.bfloat16)] * 2
    if not split:
        scratch.append(pltpu.VMEM((rows, units), jnp.bfloat16))
    if loads:
        out_shape += [stays_in_vmem((units // chunk, width, chunk))]
        out_shape += [stays_in_vmem((width // chunk, units, chunk))]
        scratch.append(pltpu.SemaphoreType.DMA((2, max(units, width) // chunk)))
    return pl.pallas_call(
        functools.partial(forward_kernel, loads, chips, n_dec, len(weights), len(after), chunk),
        out_shape=out_shape,
        in_specs=[SMEM_WHOLE]
        + [VMEM_WHOLE] * (len(args) + 1)
        + [IN_PLACE if loads else VMEM_WHOLE] * (len(weights) - 1)
        + [IN_PLACE] * len(after),
        out_specs=[VMEM_WHOLE] * len(out_shape),
        scratch_shapes=scratch,
        compiler_params=params(9),
        cost_estimate=cost(6 * rows * width * units, 6 * width * units, rows * units),
        name="feed_forward",
    )(place, *args, *weights, *after)


def angle_tables(places):
    halfway = HD // 2
    powers = jnp.arange(halfway, dtype=jnp.float32) * (2.0 / HD)
    inverse = THETA ** (-powers)
    angles = places.astype(jnp.float32)[:, None] * inverse[None, :]
    cosine, sine = jnp.cos(angles), jnp.sin(angles)
    return jnp.concatenate([cosine, cosine], axis=-1), jnp.concatenate([-sine, sine], axis=-1)


def add(*values):
    total = values[0].astype(jnp.float32)
    for value in values[1:]:
        total = total + value.astype(jnp.float32)
    return total.astype(jnp.bfloat16)


def on_device(
    prefill_rows,
    decode_rows,
    deal_order,
    prefill_offset,
    cache_length,
    prefill_cache,
    decode_cache,
    qkv_weight,
    out_weight,
    attention_gain,
    forward_gain,
    gate_weight,
    up_weight,
    down_weight,
):
    tensor_count = lax.axis_size("tensor")
    dp_count = lax.axis_size("dp")
    chips = tensor_count // 2
    tensor_place = lax.axis_index("tensor")
    group_place = lax.axis_index("dp")
    chip, core = tensor_place // 2, tensor_place % 2
    piece, width = prefill_rows.shape
    per_device = decode_rows.shape[0]
    requests = deal_order.shape[0]
    slots = cache_length.shape[0]
    padded = -(-slots // 16) * 16
    heads = qkv_weight.shape[1]
    tokens = piece * tensor_count

    def place_of(k):
        spots = [core, (chip + k) % chips, prefill_offset[0]]
        return jnp.stack(spots + [(chip + j) % chips for j in range(chips)]).astype(jnp.int32)

    places = [place_of(k) for k in range(chips)]
    weight = in_hbm(qkv_weight.reshape(width, -1))
    gate_weight, up_weight, down_weight = map(in_hbm, (gate_weight, up_weight, down_weight))
    prefill_cache, decode_cache = in_hbm(prefill_cache), in_hbm(decode_cache)

    mines = [prefill_rows] + [from_chip(prefill_rows, k) for k in range(1, chips)]
    sibs = [swap_cores(rows) for rows in mines]

    low = max(dp_count // 4, 1)
    pool = [decode_rows] + [swap_groups(decode_rows, i) for i in range(1, low)]
    pool = jnp.concatenate(pool, axis=0)
    pool = [pool] + [swap_groups(pool, i * low) for i in range(1, dp_count // low)]
    pool = jnp.concatenate(pool, axis=0)
    index = jnp.arange(dp_count * per_device, dtype=jnp.int32)
    origin = jnp.bitwise_xor(group_place, index // per_device)
    request = (origin * tensor_count + tensor_place) * per_device + index % per_device
    slot_of = jnp.sum(
        jnp.where(
            request[:, None] == jnp.arange(requests, dtype=jnp.int32)[None, :],
            deal_order[None, :],
            0,
        ),
        axis=1,
    )
    in_group = slot_of - group_place * slots
    chooser = (jnp.arange(padded, dtype=jnp.int32)[:, None] == in_group[None, :]) & (
        in_group[None, :] < slots
    )
    dealt = jnp.dot(
        chooser.astype(jnp.bfloat16), pool, preferred_element_type=jnp.float32
    ).astype(jnp.bfloat16)

    gain = attention_gain.reshape(1, width)
    tables = angle_tables(prefill_offset[0] + jnp.arange(tokens, dtype=jnp.int32))
    dec_tables = angle_tables(jnp.pad(cache_length, (0, padded - slots)))
    queries, entries, everything = [None] * chips, [None] * chips, None
    for k in range(chips):
        last = k == chips - 1
        if last:
            others = from_rest(dealt)
            if k:
                *others, queries[k - 1] = lax.optimization_barrier((*others, queries[k - 1]))
            dealt = add(dealt, *others)
        got = project(
            places[k],
            in_hbm(mines[k]),
            in_hbm(sibs[k]),
            gain,
            weight,
            tables,
            heads,
            everything,
            dealt if last else None,
            dec_tables if last else None,
            slots,
            [queries[k - 1]] if k else [dealt],
        )
        queries[k], entries[k], everything = got[:3]
        if last:
            dec_query, dec_entries = got[3:]

    out_share = in_hbm(out_weight)
    sib_weight, queries[-1] = lax.optimization_barrier((out_weight, queries[-1]))
    sib_weight = in_vmem(swap_cores(sib_weight))
    out_weight = in_vmem(out_weight)

    def finish(attended, place, before):
        attended, *before = lax.optimization_barrier((attended, *before))
        sib = swap_cores(attended)
        return out_project(place, attended, sib, out_weight, sib_weight), before

    parts = []
    dec_shares = []
    for k in range(chips):
        wanted = decode_cache if k == 0 else gate_weight if k == 1 else out_share
        attended, fetched = fill_attend(
            places[k],
            queries[k],
            prefill_cache,
            entries,
            heads,
            wanted,
            width // 4 if k else 0,
            dec_shares[:1],
        )
        if k == 1:
            held_gate = fetched
        part, dec_shares[1:] = finish(attended, places[k], dec_shares[1:])
        parts.append(part)
        if k == 0:
            lengths, parts[0] = lax.optimization_barrier((cache_length, parts[0]))
            dec_part = step_attend(
                lengths, dec_query, dec_entries, fetched, out_share, heads
            )
            dec_shares = [dec_part, *from_rest(dec_part)]

    def shares_of(own, others):
        pairs = []
        for value in [own, *others]:
            pairs += [value, swap_cores(value)]
        return pairs

    gain = forward_gain.reshape(1, width)
    order = [*range(1, chips), 0]

    def fetch(b):
        return [from_chip(parts[(b - j) % chips], j) for j in range(1, chips)]

    theirs = fetch(order[0])
    weights = [held_gate, up_weight, down_weight]
    arrived, sent = [], []
    for n, b in enumerate(order):
        got = feed_forward(
            places[b],
            mines[b],
            sibs[b],
            shares_of(parts[b], theirs),
            gain,
            weights if n + 1 < chips else weights[:2],
            n == 0,
            dealt if n == 0 else None,
            dec_shares if n == 0 else None,
            sent,
        )
        if n + 1 < chips:
            keep, give = got[:2]
            *theirs, keep = lax.optimization_barrier((*fetch(order[n + 1]), keep))
            both = add(keep, swap_cores(give))
            arrived.append(from_chip(both, chips - b))
            sent = [both]
        if n == 0:
            dec_sum, dec_resid, *weights[1:] = got[3:]
            dec_others = from_rest(dec_sum)
    resid, hidden = got
    dec_sum, hidden = lax.optimization_barrier((dec_sum, hidden))
    final = add(dec_resid, dec_sum, *dec_others)
    picker = in_group[:, None] == jnp.arange(padded, dtype=jnp.int32)[None, :]
    picker = picker & (in_group[:, None] < slots)
    routed = jnp.dot(
        picker.astype(jnp.bfloat16), final, preferred_element_type=jnp.float32
    ).astype(jnp.bfloat16)
    keep, give = lower(hidden, weights[2], [routed])
    low = max(dp_count // 4, 1)
    pairs = routed.reshape(dp_count // low, low * per_device, width)
    rows = add(
        pairs[0], *[swap_groups(pairs[i], i * low) for i in range(1, dp_count // low)]
    )
    *arrived, rows, give = lax.optimization_barrier((*arrived, rows, give))
    pairs = rows.reshape(low, per_device, width)
    routed = add(pairs[0], *[swap_groups(pairs[i], i) for i in range(1, low)])

    prefill_out = add(resid, keep, swap_cores(give), *arrived)
    return (prefill_out, routed, everything, dec_entries)


def solution(mesh):
    placed = (
        P(("dp", "tensor"), None),
        P(("dp", "tensor"), None),
        P(),
        P("dp"),
        P("dp"),
        P(None, "dp", None, "tensor"),
        P(None, "dp", None, "tensor"),
        P(None, "tensor", None),
        P("tensor", None),
        P(),
        P(),
        P(None, "tensor"),
        P(None, "tensor"),
        P("tensor", None),
    )
    return jax.shard_map(
        on_device,
        mesh=mesh,
        in_specs=placed,
        out_specs=(
            P(("dp", "tensor"), None),
            P(("dp", "tensor"), None),
            P(None, "dp", "tensor"),
            P(None, "dp", "tensor"),
        ),
        check_vma=False,
    )
```

```python
import functools
import math

import jax
import jax.numpy as jnp
from jax import lax
from jax.experimental import pallas as pl
from jax.experimental.pallas import tpu as pltpu
from jax.sharding import PartitionSpec as P

HD = 128
EPSILON = 1e-06
THETA = 1000000.0
NEGATIVE = -1e30
MIB = 1 << 20


def swap_cores(value):
    count = lax.axis_size("tensor")
    return lax.ppermute(value, "tensor", [(i, i ^ 1) for i in range(count)])


def from_chip(value, step):
    count = lax.axis_size("tensor")
    chips = count // 2
    return lax.ppermute(
        value, "tensor", [(i, (i // 2 - step) % chips * 2 + i % 2) for i in range(count)]
    )


def from_other(value, step):
    count = lax.axis_size("tensor")
    return lax.ppermute(
        value, "tensor", [(i, (i // 2 - step) % (count // 2) * 2 + 1 - i % 2) for i in range(count)]
    )


def from_rest(value):
    chips = lax.axis_size("tensor") // 2
    return [from_chip(value, k) for k in range(1, chips)] + [from_other(value, k) for k in range(chips)]


def swap_groups(value, mask):
    count = lax.axis_size("dp")
    return lax.ppermute(value, "dp", [(i, i ^ mask) for i in range(count)])


def whole(shape):
    return pl.BlockSpec(shape, lambda *_: (0,) * len(shape))


def params(mib):
    return pltpu.CompilerParams(vmem_limit_bytes=mib * MIB)


def cost(flops, moved, exps=0):
    return pl.CostEstimate(flops=int(flops), bytes_accessed=int(moved), transcendentals=int(exps))


def normed(values, gain):
    spread = jnp.mean(values * values, axis=-1, keepdims=True)
    return (values * lax.rsqrt(spread + EPSILON) * gain).astype(jnp.bfloat16)


def turn(vectors, cosine, sine):
    return vectors * cosine + pltpu.roll(vectors, HD // 2, 1) * sine


def in_vmem(value):
    return pltpu.with_memory_space_constraint(value, pltpu.VMEM)


def in_hbm(value):
    return pltpu.with_memory_space_constraint(value, pltpu.HBM)


def stays_in_vmem(shape):
    return pltpu.VMEM(shape, jnp.bfloat16)


VMEM_WHOLE = pl.BlockSpec(memory_space=pltpu.VMEM)
SMEM_WHOLE = pl.BlockSpec(memory_space=pltpu.SMEM)
IN_PLACE = pl.BlockSpec(memory_space=pl.ANY)


def project_kernel(n_dec, n_after, groups, heads, place, *refs):
    refs = list(refs)
    mine, sib, weight, gain, cosine, sine = refs[:6]
    refs = refs[6:]
    if n_dec:
        dec, dec_cos, dec_sin = refs[:3]
        refs = refs[3:]
    refs = refs[n_after:]
    query, entries, everything = refs[:3]
    if n_dec:
        dec_query, dec_entries = refs[3:5]
    inner, rows_held, weight_held, row_sems, weight_sems, out_sem = refs[-6:]
    piece = mine.shape[0]
    core = place[0]
    scale = gain[...]
    depth = (groups + 2) * HD
    row_copies = [
        pltpu.make_async_copy(ref, rows_held.at[i], row_sems.at[i])
        for i, ref in enumerate((mine, sib))
    ]
    weight_copies = [
        pltpu.make_async_copy(
            weight.at[:, pl.ds(j * depth, depth)], weight_held.at[j], weight_sems.at[j]
        )
        for j in range(heads)
    ]
    for copy in row_copies + weight_copies:
        copy.start()
    for i, at in enumerate((core, 1 - core)):
        row_copies[i].wait()
        start = pl.multiple_of(at * piece, piece)
        inner[pl.ds(start, piece), :] = normed(rows_held[i].astype(jnp.float32), scale)
    if n_dec:
        inner[2 * piece :, :] = normed(dec[...].astype(jnp.float32), scale)
    here = pl.ds(pl.multiple_of(place[1] * 2 * piece, 2 * piece), 2 * piece)
    for j in range(heads):
        weight_copies[j].wait()
        mixed = jnp.dot(inner[...], weight_held[j], preferred_element_type=jnp.float32)

        def put(rows, cos, sin, query_out, entry_out):
            for g in range(groups):
                part = rows[:, g * HD : (g + 1) * HD]
                at = (j * groups + g) * HD
                turned = turn(part, cos, sin).astype(jnp.bfloat16)
                query_out[:, at : at + HD] = turned.astype(query_out.dtype)
            key = turn(rows[:, groups * HD : (groups + 1) * HD], cos, sin).astype(jnp.bfloat16)
            value = rows[:, (groups + 1) * HD :].astype(jnp.bfloat16)
            size = entry_out.shape[1]
            entry_out[0, :, j * HD : (j + 1) * HD] = key[:size]
            entry_out[1, :, j * HD : (j + 1) * HD] = value[:size]

        put(mixed[: 2 * piece], cosine[here, :], sine[here, :], query, entries)
        if n_dec:
            put(mixed[2 * piece :], dec_cos[...], dec_sin[...], dec_query, dec_entries)
    keep = pltpu.make_async_copy(entries, everything.at[:, here, :], out_sem)
    keep.start()
    keep.wait()


def project(
    place, mine, sib, gain, weight, tables, heads, everything, dec=None, dec_tables=None, slots=0, after=()
):
    piece, width = mine.shape
    depth = weight.shape[1] // heads
    groups = depth // HD - 2
    block = 2 * piece
    n_dec = 0 if dec is None else dec.shape[0]
    args = [mine, sib, weight, gain, *tables]
    if n_dec:
        args += [dec, *dec_tables]
    n_operands = len(args)
    after = list(after)
    aliases = {}
    if everything is not None:
        after.append(everything)
        aliases = {n_operands + len(after): 2}
    wide = heads * groups * HD
    out_shape = [
        jax.ShapeDtypeStruct((block, wide), jnp.bfloat16),
        jax.ShapeDtypeStruct((2, block, heads * HD), jnp.bfloat16),
        jax.ShapeDtypeStruct((2, tables[0].shape[0], heads * HD), jnp.bfloat16),
    ]
    if n_dec:
        out_shape += [
            jax.ShapeDtypeStruct((n_dec, wide), jnp.float32),
            jax.ShapeDtypeStruct((2, slots, heads * HD), jnp.bfloat16),
        ]
    rows = block + n_dec
    return pl.pallas_call(
        functools.partial(project_kernel, n_dec, len(after), groups, heads),
        out_shape=out_shape,
        in_specs=[SMEM_WHOLE]
        + [IN_PLACE] * 3
        + [VMEM_WHOLE] * (len(args) - 3)
        + [IN_PLACE] * len(after),
        out_specs=[VMEM_WHOLE] * 2 + [IN_PLACE] + [VMEM_WHOLE] * (len(out_shape) - 3),
        scratch_shapes=[
            pltpu.VMEM((rows, width), jnp.bfloat16),
            pltpu.VMEM((2, piece, width), jnp.bfloat16),
            pltpu.VMEM((heads, width, depth), jnp.bfloat16),
            pltpu.SemaphoreType.DMA((2,)),
            pltpu.SemaphoreType.DMA((heads,)),
            pltpu.SemaphoreType.DMA(()),
        ],
        input_output_aliases=aliases,
        compiler_params=params(20),
        cost_estimate=cost(2 * rows * weight.size, 2 * (weight.size + 2 * rows * width)),
        name="project",
    )(place, *args, *after)


def fill_kernel(groups, chips, chunk, place, query, cache_key, cache_value, *refs):
    new_keys, new_values = refs[:chips], refs[chips : 2 * chips]
    source, (out, target, arrived) = refs[2 * chips], refs[-3:]
    pieces = [
        source.at[:, pl.ds(i * chunk, chunk)] if chunk else source.at[i]
        for i in range(target.shape[0])
    ]
    copies = [
        pltpu.make_async_copy(piece, target.at[i], arrived.at[i]) for i, piece in enumerate(pieces)
    ]

    @pl.when(pl.program_id(0) == 0)
    def _():
        for copy in copies:
            copy.start()

    scaling = math.log2(math.e) / math.sqrt(HD)
    count = query.shape[0]
    stored = cache_key.shape[2]
    old_seen = lax.broadcasted_iota(jnp.int32, (1, stored), 1) < place[2]
    ahead = lax.broadcasted_iota(jnp.int32, (count, count), 1) - lax.broadcasted_iota(
        jnp.int32, (count, count), 0
    )
    across = (((1,), (1,)), ((), ()))
    for g in range(groups):
        rows = query[:, g * HD : (g + 1) * HD]
        scores = lax.dot_general(rows, cache_key[0, 0], across, preferred_element_type=jnp.float32)
        scores = [jnp.where(old_seen, scores * scaling, NEGATIVE)]
        for k in range(chips):
            fresh = lax.dot_general(
                rows, new_keys[k][0], across, preferred_element_type=jnp.float32
            )
            gap = (place[1] - place[3 + k]) * count
            scores.append(jnp.where(ahead <= gap, fresh * scaling, NEGATIVE))
        top = jnp.max(scores[0], axis=-1, keepdims=True)
        for part in scores[1:]:
            top = jnp.maximum(top, jnp.max(part, axis=-1, keepdims=True))
        mix, total = 0.0, 0.0
        for part, values in zip(scores, [cache_value[0, 0], *[v[0] for v in new_values]]):
            weights = jnp.exp2(part - top)
            total += jnp.sum(weights, axis=-1, keepdims=True)
            mix += jnp.dot(weights.astype(jnp.bfloat16), values, preferred_element_type=jnp.float32)
        out[:, g * HD : (g + 1) * HD] = (mix / total).astype(jnp.bfloat16)

    @pl.when(pl.program_id(0) == pl.num_programs(0) - 1)
    def _():
        for copy in copies:
            copy.wait()


def fill_attend(place, query, cache, entries, heads, source, chunk, after=()):
    count = query.shape[0]
    groups = query.shape[1] // heads // HD
    stored = cache.shape[2]
    chips = len(entries)
    pairs = count * groups * heads * (stored + chips * count)
    target = (source.shape[1] // chunk, source.shape[0], chunk) if chunk else source.shape
    return pl.pallas_call(
        functools.partial(fill_kernel, groups, chips, chunk),
        out_shape=[jax.ShapeDtypeStruct(query.shape, jnp.bfloat16), stays_in_vmem(target)],
        grid_spec=pltpu.PrefetchScalarGridSpec(
            num_scalar_prefetch=1,
            grid=(heads,),
            in_specs=[
                pl.BlockSpec((count, groups * HD), lambda j, s: (0, j)),
                pl.BlockSpec((1, 1, stored, HD), lambda j, s: (0, 0, 0, j)),
                pl.BlockSpec((1, 1, stored, HD), lambda j, s: (1, 0, 0, j)),
            ]
            + [pl.BlockSpec((1, count, HD), lambda j, s: (0, 0, j))] * chips
            + [pl.BlockSpec((1, count, HD), lambda j, s: (1, 0, j))] * chips
            + [IN_PLACE] * (1 + len(after)),
            out_specs=[pl.BlockSpec((count, groups * HD), lambda j, s: (0, j)), IN_PLACE],
            scratch_shapes=[pltpu.SemaphoreType.DMA((target[0],))],
        ),
        compiler_params=params(12),
        cost_estimate=cost(8 * pairs * HD, 2 * cache.size, pairs),
        name="fill_attend",
    )(place, query, cache, cache, *entries, *entries, source, *after)


def step_kernel(heads, lengths, query, entries, held, weight, out, scores, shares, weight_held, weight_sem):
    scaling = 1.0 / math.sqrt(HD)
    slots, stored, width = held.shape[1:]
    groups = query.shape[1] // width
    lanes = 8
    weight_copy = pltpu.make_async_copy(weight, weight_held, weight_sem)
    weight_copy.start()
    across = (((1,), (1,)), ((), ()))
    places = lax.broadcasted_iota(jnp.int32, (1, stored), 1)
    blank = jnp.zeros((1, HD), jnp.float32)
    new_keys = entries[0].astype(jnp.float32)
    new_values = entries[1].astype(jnp.float32)
    own_scores = []
    for s in range(slots):
        rows = []
        for j in range(heads):
            for g in range(groups):
                at = (j * groups + g) * HD
                part = query[s : s + 1, at : at + HD]
                rows.append(
                    jnp.concatenate([part if i == j else blank for i in range(heads)], axis=1)
                )
        rows.append(jnp.zeros((lanes - heads * groups, width), jnp.float32))
        rows = jnp.concatenate(rows, axis=0)
        own_scores.append(jnp.sum(rows * new_keys[s : s + 1], axis=-1, keepdims=True))
        old = lax.dot_general(
            rows.astype(jnp.bfloat16), held[0, s], across, preferred_element_type=jnp.float32
        )
        scores[s * lanes : (s + 1) * lanes, :] = jnp.where(
            places < lengths[s], old * scaling, NEGATIVE
        )
    old = scores[...]
    own = jnp.concatenate(own_scores, axis=0) * scaling
    top = jnp.maximum(jnp.max(old, axis=-1, keepdims=True), own)
    old = jnp.exp(old - top)
    own = jnp.exp(own - top)
    total = jnp.sum(old, axis=-1, keepdims=True) + own
    shares[...] = old / total
    own = (own / total).astype(jnp.bfloat16).astype(jnp.float32)
    attended = []
    for s in range(slots):
        here = slice(s * lanes, (s + 1) * lanes)
        mix = jnp.dot(
            shares[here, :].astype(jnp.bfloat16), held[1, s], preferred_element_type=jnp.float32
        )
        mix += own[here] * new_values[s : s + 1]
        parts = []
        for j in range(heads):
            for g in range(groups):
                row = j * groups + g
                parts.append(mix[row : row + 1, j * HD : (j + 1) * HD])
        attended.append(jnp.concatenate(parts, axis=1))
    if out.shape[0] > slots:
        attended.append(jnp.zeros((out.shape[0] - slots, query.shape[1]), jnp.float32))
    attended = jnp.concatenate(attended, axis=0).astype(jnp.bfloat16)
    weight_copy.wait()
    part = jnp.dot(attended, weight_held[...], preferred_element_type=jnp.float32)
    out[...] = part.astype(jnp.bfloat16)


def step_attend(lengths, query, entries, cache, weight, heads):
    slots, stored = cache.shape[1:3]
    padded = query.shape[0]
    rows = slots * 8
    return pl.pallas_call(
        functools.partial(step_kernel, heads),
        out_shape=jax.ShapeDtypeStruct((padded, weight.shape[1]), jnp.bfloat16),
        in_specs=[SMEM_WHOLE] + [VMEM_WHOLE] * 3 + [IN_PLACE],
        out_specs=VMEM_WHOLE,
        scratch_shapes=[
            pltpu.VMEM((rows, stored), jnp.float32),
            pltpu.VMEM((rows, stored), jnp.float32),
            pltpu.VMEM(weight.shape, jnp.bfloat16),
            pltpu.SemaphoreType.DMA(()),
        ],
        compiler_params=params(12),
        cost_estimate=cost(16 * cache.size, 2 * cache.size, rows * stored),
        name="step_attend",
    )(lengths, query, entries, cache, weight)


def out_kernel(place, mine, sib, weight, sib_weight, *refs):
    out = refs[-1]
    half = out.shape[1]
    cols = pl.ds(pl.multiple_of(place[0] * half, half), half)
    part = jnp.dot(mine[...], weight[:, cols], preferred_element_type=jnp.float32)
    part += jnp.dot(sib[...], sib_weight[:, cols], preferred_element_type=jnp.float32)
    out[...] = part.astype(jnp.bfloat16)


def out_project(place, mine, sib, weight, sib_weight, after=()):
    rows, depth = mine.shape
    half = weight.shape[1] // 2
    return pl.pallas_call(
        out_kernel,
        out_shape=jax.ShapeDtypeStruct((rows, half), jnp.bfloat16),
        in_specs=[SMEM_WHOLE] + [VMEM_WHOLE] * 4 + [IN_PLACE] * len(after),
        out_specs=VMEM_WHOLE,
        compiler_params=params(8),
        cost_estimate=cost(4 * rows * depth * half, 4 * depth * half + 6 * rows * half),
        name="out_project",
    )(place, mine, sib, weight, sib_weight, *after)


def forward_kernel(loads, chips, n_dec, n_weights, n_after, chunk, place, *refs):
    refs = list(refs)
    mine, sib = refs[:2]
    shares = refs[2 : 2 + 2 * chips]
    refs = refs[2 + 2 * chips :]
    if n_dec:
        dec, dec_shares = refs[0], refs[1 : 1 + 2 * chips]
        refs = refs[1 + 2 * chips :]
    split = n_weights == 2
    gain, *weights = refs[: 1 + n_weights]
    refs = refs[1 + n_weights + n_after :]
    if split:
        resid, hidden = refs[:2]
        held, inner = refs[2:]
    else:
        keep, give, resid = refs[:3]
        refs = refs[3:]
        if n_dec:
            dec_out, dec_resid = refs[:2]
            refs = refs[2:]
        if loads:
            sources, weights[1:], refs = weights[1:], refs[:2], refs[2:]
        held, inner, hidden = refs[:3]
    copies = {}
    if loads:
        arrived = refs[3]
        for w, source in enumerate(sources, 1):
            for i in range(weights[w].shape[0]):
                copies[w, i] = pltpu.make_async_copy(
                    source.at[:, pl.ds(i * chunk, chunk)], weights[w].at[i], arrived.at[w - 1, i]
                )
                copies[w, i].start()

    def ready(w, i):
        if (w, i) in copies:
            copies[w, i].wait()
        return weights[w][i]

    piece = mine.shape[0]
    half = shares[0].shape[1]
    core = place[0]
    for rows, at_rows, put in ((mine, core, 0), (sib, 1 - core, piece)):
        here = pl.ds(pl.multiple_of(at_rows * piece, piece), piece)
        for side in range(2):
            at = core if side == 0 else 1 - core
            cols = pl.ds(pl.multiple_of(at * half, half), half)
            added = shares[side][here, :].astype(jnp.float32)
            for k in range(1, chips):
                added += shares[2 * k + side][here, :].astype(jnp.float32)
            value = rows[:, cols].astype(jnp.float32) + added
            held[put : put + piece, cols] = value.astype(jnp.bfloat16)
    if n_dec:
        added = dec_shares[0][...].astype(jnp.float32)
        for share in dec_shares[1:]:
            added += share[...].astype(jnp.float32)
        held[2 * piece :, :] = (dec[...].astype(jnp.float32) + added).astype(jnp.bfloat16)
    for put in range(0, held.shape[0], piece):
        here = slice(put, min(put + piece, held.shape[0]))
        inner[here, :] = normed(held[here, :].astype(jnp.float32), gain[...])
    resid[...] = held[:piece, :]
    if n_dec:
        dec_resid[...] = held[2 * piece :, :]

    for i in range(weights[0].shape[0]):
        at = slice(i * chunk, (i + 1) * chunk)
        gated = jnp.dot(inner[...], ready(0, i), preferred_element_type=jnp.float32)
        raised = jnp.dot(inner[...], ready(1, i), preferred_element_type=jnp.float32)
        hidden[:, at] = (gated / (1.0 + jnp.exp(-gated)) * raised).astype(jnp.bfloat16)
    for i in range(0 if split else weights[2].shape[0]):
        at = slice(i * chunk, (i + 1) * chunk)
        part = jnp.dot(hidden[...], ready(2, i), preferred_element_type=jnp.float32)
        part = part.astype(jnp.bfloat16)
        keep[:, at] = part[:piece]
        give[:, at] = part[piece : 2 * piece]
        if n_dec:
            dec_out[:, at] = part[2 * piece :]


def lower_kernel(hidden, down, *refs):
    keep, give = refs[-2:]
    piece = keep.shape[0]
    chunk = down.shape[2]
    for i in range(down.shape[0]):
        at = slice(i * chunk, (i + 1) * chunk)
        part = jnp.dot(hidden[...], down[i], preferred_element_type=jnp.float32)
        part = part.astype(jnp.bfloat16)
        keep[:, at] = part[:piece]
        give[:, at] = part[piece:]


def lower(hidden, down, after):
    rows, units = hidden.shape
    width = down.shape[0] * down.shape[2]
    return pl.pallas_call(
        lower_kernel,
        out_shape=[jax.ShapeDtypeStruct((rows // 2, width), jnp.bfloat16)] * 2,
        in_specs=[VMEM_WHOLE] * 2 + [IN_PLACE] * len(after),
        out_specs=[VMEM_WHOLE] * 2,
        compiler_params=params(8),
        cost_estimate=cost(2 * rows * width * units, 2 * width * units),
        name="lower",
    )(hidden, down, *after)


def feed_forward(place, mine, sib, shares, gain, weights, loads, dec=None, dec_shares=None, after=()):
    piece, width = mine.shape
    chips = len(shares) // 2
    n_dec = 0 if dec is None else dec.shape[0]
    rows = 2 * piece + n_dec
    args = [mine, sib, *shares]
    if n_dec:
        args += [dec, *dec_shares]
    args += [gain]
    split = len(weights) == 2
    chunk = weights[0].shape[2]
    units = weights[0].shape[0] * chunk
    if split:
        shapes = [(piece, width), (rows, units)]
    else:
        shapes = [(n, width) for n in [piece] * 3 + [n_dec] * 2 * bool(n_dec)]
    out_shape = [jax.ShapeDtypeStruct(shape, jnp.bfloat16) for shape in shapes]
    scratch = [pltpu.VMEM((rows, width), jnp.bfloat16)] * 2
    if not split:
        scratch.append(pltpu.VMEM((rows, units), jnp.bfloat16))
    if loads:
        out_shape += [stays_in_vmem((units // chunk, width, chunk))]
        out_shape += [stays_in_vmem((width // chunk, units, chunk))]
        scratch.append(pltpu.SemaphoreType.DMA((2, max(units, width) // chunk)))
    return pl.pallas_call(
        functools.partial(forward_kernel, loads, chips, n_dec, len(weights), len(after), chunk),
        out_shape=out_shape,
        in_specs=[SMEM_WHOLE]
        + [VMEM_WHOLE] * (len(args) + 1)
        + [IN_PLACE if loads else VMEM_WHOLE] * (len(weights) - 1)
        + [IN_PLACE] * len(after),
        out_specs=[VMEM_WHOLE] * len(out_shape),
        scratch_shapes=scratch,
        compiler_params=params(9),
        cost_estimate=cost(6 * rows * width * units, 6 * width * units, rows * units),
        name="feed_forward",
    )(place, *args, *weights, *after)


def angle_tables(places):
    halfway = HD // 2
    powers = jnp.arange(halfway, dtype=jnp.float32) * (2.0 / HD)
    inverse = THETA ** (-powers)
    angles = places.astype(jnp.float32)[:, None] * inverse[None, :]
    cosine, sine = jnp.cos(angles), jnp.sin(angles)
    return jnp.concatenate([cosine, cosine], axis=-1), jnp.concatenate([-sine, sine], axis=-1)


def add(*values):
    total = values[0].astype(jnp.float32)
    for value in values[1:]:
        total = total + value.astype(jnp.float32)
    return total.astype(jnp.bfloat16)


def on_device(
    prefill_rows,
    decode_rows,
    deal_order,
    prefill_offset,
    cache_length,
    prefill_cache,
    decode_cache,
    qkv_weight,
    out_weight,
    attention_gain,
    forward_gain,
    gate_weight,
    up_weight,
    down_weight,
):
    tensor_count = lax.axis_size("tensor")
    dp_count = lax.axis_size("dp")
    chips = tensor_count // 2
    tensor_place = lax.axis_index("tensor")
    group_place = lax.axis_index("dp")
    chip, core = tensor_place // 2, tensor_place % 2
    piece, width = prefill_rows.shape
    per_device = decode_rows.shape[0]
    requests = deal_order.shape[0]
    slots = cache_length.shape[0]
    padded = -(-slots // 16) * 16
    heads = qkv_weight.shape[1]
    tokens = piece * tensor_count

    def place_of(k):
        spots = [core, (chip + k) % chips, prefill_offset[0]]
        return jnp.stack(spots + [(chip + j) % chips for j in range(chips)]).astype(jnp.int32)

    places = [place_of(k) for k in range(chips)]
    weight = in_hbm(qkv_weight.reshape(width, -1))
    gate_weight, up_weight, down_weight = map(in_hbm, (gate_weight, up_weight, down_weight))
    prefill_cache, decode_cache = in_hbm(prefill_cache), in_hbm(decode_cache)

    mines = [prefill_rows] + [from_chip(prefill_rows, k) for k in range(1, chips)]
    sibs = [swap_cores(rows) for rows in mines]

    low = max(dp_count // 4, 1)
    pool = [decode_rows] + [swap_groups(decode_rows, i) for i in range(1, low)]
    pool = jnp.concatenate(pool, axis=0)
    pool = [pool] + [swap_groups(pool, i * low) for i in range(1, dp_count // low)]
    pool = jnp.concatenate(pool, axis=0)
    index = jnp.arange(dp_count * per_device, dtype=jnp.int32)
    origin = jnp.bitwise_xor(group_place, index // per_device)
    request = (origin * tensor_count + tensor_place) * per_device + index % per_device
    slot_of = jnp.sum(
        jnp.where(
            request[:, None] == jnp.arange(requests, dtype=jnp.int32)[None, :],
            deal_order[None, :],
            0,
        ),
        axis=1,
    )
    in_group = slot_of - group_place * slots
    chooser = (jnp.arange(padded, dtype=jnp.int32)[:, None] == in_group[None, :]) & (
        in_group[None, :] < slots
    )
    dealt = jnp.dot(
        chooser.astype(jnp.bfloat16), pool, preferred_element_type=jnp.float32
    ).astype(jnp.bfloat16)

    gain = attention_gain.reshape(1, width)
    tables = angle_tables(prefill_offset[0] + jnp.arange(tokens, dtype=jnp.int32))
    dec_tables = angle_tables(jnp.pad(cache_length, (0, padded - slots)))
    queries, entries, everything = [None] * chips, [None] * chips, None
    for k in range(chips):
        last = k == chips - 1
        if last:
            others = from_rest(dealt)
            if k:
                *others, queries[k - 1] = lax.optimization_barrier((*others, queries[k - 1]))
            dealt = add(dealt, *others)
        got = project(
            places[k],
            in_hbm(mines[k]),
            in_hbm(sibs[k]),
            gain,
            weight,
            tables,
            heads,
            everything,
            dealt if last else None,
            dec_tables if last else None,
            slots,
            [queries[k - 1]] if k else [dealt],
        )
        queries[k], entries[k], everything = got[:3]
        if last:
            dec_query, dec_entries = got[3:]

    out_share = in_hbm(out_weight)
    sib_weight, queries[-1] = lax.optimization_barrier((out_weight, queries[-1]))
    sib_weight = in_vmem(swap_cores(sib_weight))
    out_weight = in_vmem(out_weight)

    def finish(attended, place):
        return out_project(place, attended, swap_cores(attended), out_weight, sib_weight)

    parts = []
    dec_shares = []
    for k in range(chips):
        wanted = decode_cache if k == 0 else gate_weight if k == 1 else out_share
        attended, fetched = fill_attend(
            places[k],
            queries[k],
            prefill_cache,
            entries,
            heads,
            wanted,
            width // 4 if k else 0,
            dec_shares[:1],
        )
        if k == 1:
            held_gate = fetched
        parts.append(finish(attended, places[k]))
        if k == 0:
            lengths, parts[0] = lax.optimization_barrier((cache_length, parts[0]))
            dec_part = step_attend(
                lengths, dec_query, dec_entries, fetched, out_share, heads
            )
            dec_shares = [dec_part, *from_rest(dec_part)]

    def shares_of(own, others):
        pairs = []
        for value in [own, *others]:
            pairs += [value, swap_cores(value)]
        return pairs

    gain = forward_gain.reshape(1, width)
    order = [*range(1, chips), 0]

    def fetch(b):
        return [from_chip(parts[(b - j) % chips], j) for j in range(1, chips)]

    theirs, dec_shares[1:] = lax.optimization_barrier((fetch(order[0]), dec_shares[1:]))
    weights = [held_gate, up_weight, down_weight]
    arrived, sent = [], []
    for n, b in enumerate(order):
        got = feed_forward(
            places[b],
            mines[b],
            sibs[b],
            shares_of(parts[b], theirs),
            gain,
            weights if n + 1 < chips else weights[:2],
            n == 0,
            dealt if n == 0 else None,
            dec_shares if n == 0 else None,
            sent,
        )
        if n + 1 < chips:
            keep, give = got[:2]
            *theirs, keep = lax.optimization_barrier((*fetch(order[n + 1]), keep))
            both = add(keep, swap_cores(give))
            arrived.append(from_chip(both, chips - b))
            sent = [both]
        if n == 0:
            dec_sum, dec_resid, *weights[1:] = got[3:]
            dec_others = from_rest(dec_sum)
    resid, hidden = got
    dec_sum, hidden = lax.optimization_barrier((dec_sum, hidden))
    final = add(dec_resid, dec_sum, *dec_others)
    picker = in_group[:, None] == jnp.arange(padded, dtype=jnp.int32)[None, :]
    picker = picker & (in_group[:, None] < slots)
    routed = jnp.dot(
        picker.astype(jnp.bfloat16), final, preferred_element_type=jnp.float32
    ).astype(jnp.bfloat16)
    keep, give = lower(hidden, weights[2], [routed])
    low = max(dp_count // 4, 1)
    pairs = routed.reshape(dp_count // low, low * per_device, width)
    rows = add(
        pairs[0], *[swap_groups(pairs[i], i * low) for i in range(1, dp_count // low)]
    )
    *arrived, rows, give = lax.optimization_barrier((*arrived, rows, give))
    pairs = rows.reshape(low, per_device, width)
    others = [swap_groups(pairs[i], i) for i in range(1, low)]
    prefill_out = add(resid, keep, swap_cores(give), *arrived)
    others, prefill_out = lax.optimization_barrier((others, prefill_out))
    routed = add(pairs[0], *others)
    return (prefill_out, routed, everything, dec_entries)


def solution(mesh):
    placed = (
        P(("dp", "tensor"), None),
        P(("dp", "tensor"), None),
        P(),
        P("dp"),
        P("dp"),
        P(None, "dp", None, "tensor"),
        P(None, "dp", None, "tensor"),
        P(None, "tensor", None),
        P("tensor", None),
        P(),
        P(),
        P(None, "tensor"),
        P(None, "tensor"),
        P("tensor", None),
    )
    return jax.shard_map(
        on_device,
        mesh=mesh,
        in_specs=placed,
        out_specs=(
            P(("dp", "tensor"), None),
            P(("dp", "tensor"), None),
            P(None, "dp", "tensor"),
            P(None, "dp", "tensor"),
        ),
        check_vma=False,
    )
```

```python
import functools
import math

import jax
import jax.numpy as jnp
from jax import lax
from jax.experimental import pallas as pl
from jax.experimental.pallas import tpu as pltpu
from jax.sharding import PartitionSpec as P

HD = 128
EPSILON = 1e-06
THETA = 1000000.0
NEGATIVE = -1e30
MIB = 1 << 20


def swap_cores(value):
    count = lax.axis_size("tensor")
    return lax.ppermute(value, "tensor", [(i, i ^ 1) for i in range(count)])


def from_chip(value, step):
    count = lax.axis_size("tensor")
    chips = count // 2
    return lax.ppermute(
        value, "tensor", [(i, (i // 2 - step) % chips * 2 + i % 2) for i in range(count)]
    )


def from_other(value, step):
    count = lax.axis_size("tensor")
    return lax.ppermute(
        value, "tensor", [(i, (i // 2 - step) % (count // 2) * 2 + 1 - i % 2) for i in range(count)]
    )


def from_rest(value):
    chips = lax.axis_size("tensor") // 2
    return [from_chip(value, k) for k in range(1, chips)] + [from_other(value, k) for k in range(chips)]


def swap_groups(value, mask):
    count = lax.axis_size("dp")
    return lax.ppermute(value, "dp", [(i, i ^ mask) for i in range(count)])


def whole(shape):
    return pl.BlockSpec(shape, lambda *_: (0,) * len(shape))


def params(mib):
    return pltpu.CompilerParams(vmem_limit_bytes=mib * MIB)


def cost(flops, moved, exps=0):
    return pl.CostEstimate(flops=int(flops), bytes_accessed=int(moved), transcendentals=int(exps))


def normed(values, gain):
    spread = jnp.mean(values * values, axis=-1, keepdims=True)
    return (values * lax.rsqrt(spread + EPSILON) * gain).astype(jnp.bfloat16)


def turn(vectors, cosine, sine):
    return vectors * cosine + pltpu.roll(vectors, HD // 2, 1) * sine


def in_vmem(value):
    return pltpu.with_memory_space_constraint(value, pltpu.VMEM)


def in_hbm(value):
    return pltpu.with_memory_space_constraint(value, pltpu.HBM)


def stays_in_vmem(shape):
    return pltpu.VMEM(shape, jnp.bfloat16)


VMEM_WHOLE = pl.BlockSpec(memory_space=pltpu.VMEM)
SMEM_WHOLE = pl.BlockSpec(memory_space=pltpu.SMEM)
IN_PLACE = pl.BlockSpec(memory_space=pl.ANY)


def project_kernel(loads, n_dec, n_after, groups, heads, place, *refs):
    refs = list(refs)
    mine, sib, weight, gain, cosine, sine = refs[:6]
    refs = refs[6:]
    if n_dec:
        dec, dec_cos, dec_sin = refs[:3]
        refs = refs[3:]
    refs = refs[n_after:]
    query, entries, everything = refs[:3]
    if n_dec:
        dec_query, dec_entries = refs[3:5]
    inner, rows_held, row_sems, weight_sems, out_sem = refs[-5:]
    weight_held = refs[-6] if loads else weight
    piece = mine.shape[0]
    core = place[0]
    scale = gain[...]
    depth = (groups + 2) * HD
    row_copies = [
        pltpu.make_async_copy(ref, rows_held.at[i], row_sems.at[i])
        for i, ref in enumerate((mine, sib))
    ]
    weight_copies = [
        pltpu.make_async_copy(
            weight.at[:, pl.ds(j * depth, depth)], weight_held.at[j], weight_sems.at[j]
        )
        for j in range(heads if loads else 0)
    ]
    for copy in row_copies + weight_copies:
        copy.start()
    for i, at in enumerate((core, 1 - core)):
        row_copies[i].wait()
        start = pl.multiple_of(at * piece, piece)
        inner[pl.ds(start, piece), :] = normed(rows_held[i].astype(jnp.float32), scale)
    if n_dec:
        inner[2 * piece :, :] = normed(dec[...].astype(jnp.float32), scale)
    here = pl.ds(pl.multiple_of(place[1] * 2 * piece, 2 * piece), 2 * piece)
    for j in range(heads):
        if loads:
            weight_copies[j].wait()
        mixed = jnp.dot(inner[...], weight_held[j], preferred_element_type=jnp.float32)

        def put(rows, cos, sin, query_out, entry_out):
            for g in range(groups):
                part = rows[:, g * HD : (g + 1) * HD]
                at = (j * groups + g) * HD
                turned = turn(part, cos, sin).astype(jnp.bfloat16)
                query_out[:, at : at + HD] = turned.astype(query_out.dtype)
            key = turn(rows[:, groups * HD : (groups + 1) * HD], cos, sin).astype(jnp.bfloat16)
            value = rows[:, (groups + 1) * HD :].astype(jnp.bfloat16)
            size = entry_out.shape[1]
            entry_out[0, :, j * HD : (j + 1) * HD] = key[:size]
            entry_out[1, :, j * HD : (j + 1) * HD] = value[:size]

        put(mixed[: 2 * piece], cosine[here, :], sine[here, :], query, entries)
        if n_dec:
            put(mixed[2 * piece :], dec_cos[...], dec_sin[...], dec_query, dec_entries)
    keep = pltpu.make_async_copy(entries, everything.at[:, here, :], out_sem)
    keep.start()
    keep.wait()


def project(
    place, mine, sib, gain, weight, tables, heads, everything, dec=None, dec_tables=None, slots=0, after=()
):
    piece, width = mine.shape
    loads = everything is None
    depth = weight.shape[1] // heads if loads else weight.shape[2]
    groups = depth // HD - 2
    block = 2 * piece
    n_dec = 0 if dec is None else dec.shape[0]
    args = [mine, sib, weight, gain, *tables]
    if n_dec:
        args += [dec, *dec_tables]
    n_operands = len(args)
    after = list(after)
    aliases = {}
    if everything is not None:
        after.append(everything)
        aliases = {n_operands + len(after): 2}
    wide = heads * groups * HD
    out_shape = [
        jax.ShapeDtypeStruct((block, wide), jnp.bfloat16),
        jax.ShapeDtypeStruct((2, block, heads * HD), jnp.bfloat16),
        jax.ShapeDtypeStruct((2, tables[0].shape[0], heads * HD), jnp.bfloat16),
    ]
    if n_dec:
        out_shape += [
            jax.ShapeDtypeStruct((n_dec, wide), jnp.float32),
            jax.ShapeDtypeStruct((2, slots, heads * HD), jnp.bfloat16),
        ]
    if loads:
        out_shape.append(stays_in_vmem((heads, width, depth)))
    rows = block + n_dec
    return pl.pallas_call(
        functools.partial(project_kernel, loads, n_dec, len(after), groups, heads),
        out_shape=out_shape,
        in_specs=[SMEM_WHOLE]
        + [IN_PLACE] * 2
        + [IN_PLACE if loads else VMEM_WHOLE]
        + [VMEM_WHOLE] * (len(args) - 3)
        + [IN_PLACE] * len(after),
        out_specs=[VMEM_WHOLE] * 2 + [IN_PLACE] + [VMEM_WHOLE] * (len(out_shape) - 3),
        scratch_shapes=[
            pltpu.VMEM((rows, width), jnp.bfloat16),
            pltpu.VMEM((2, piece, width), jnp.bfloat16),
            pltpu.SemaphoreType.DMA((2,)),
            pltpu.SemaphoreType.DMA((heads,)),
            pltpu.SemaphoreType.DMA(()),
        ],
        input_output_aliases=aliases,
        compiler_params=params(12),
        cost_estimate=cost(2 * rows * weight.size, 2 * (weight.size + 2 * rows * width)),
        name="project",
    )(place, *args, *after)


def fill_kernel(groups, chips, chunk, place, query, cache_key, cache_value, *refs):
    new_keys, new_values = refs[:chips], refs[chips : 2 * chips]
    source, (out, target, arrived) = refs[2 * chips], refs[-3:]
    pieces = [
        source.at[:, pl.ds(i * chunk, chunk)] if chunk else source.at[i]
        for i in range(target.shape[0])
    ]
    copies = [
        pltpu.make_async_copy(piece, target.at[i], arrived.at[i]) for i, piece in enumerate(pieces)
    ]

    @pl.when(pl.program_id(0) == 0)
    def _():
        for copy in copies:
            copy.start()

    scaling = math.log2(math.e) / math.sqrt(HD)
    count = query.shape[0]
    stored = cache_key.shape[2]
    old_seen = lax.broadcasted_iota(jnp.int32, (1, stored), 1) < place[2]
    ahead = lax.broadcasted_iota(jnp.int32, (count, count), 1) - lax.broadcasted_iota(
        jnp.int32, (count, count), 0
    )
    across = (((1,), (1,)), ((), ()))
    for g in range(groups):
        rows = query[:, g * HD : (g + 1) * HD]
        scores = lax.dot_general(rows, cache_key[0, 0], across, preferred_element_type=jnp.float32)
        scores = [jnp.where(old_seen, scores * scaling, NEGATIVE)]
        for k in range(chips):
            fresh = lax.dot_general(
                rows, new_keys[k][0], across, preferred_element_type=jnp.float32
            )
            gap = (place[1] - place[3 + k]) * count
            scores.append(jnp.where(ahead <= gap, fresh * scaling, NEGATIVE))
        top = jnp.max(scores[0], axis=-1, keepdims=True)
        for part in scores[1:]:
            top = jnp.maximum(top, jnp.max(part, axis=-1, keepdims=True))
        mix, total = 0.0, 0.0
        for part, values in zip(scores, [cache_value[0, 0], *[v[0] for v in new_values]]):
            weights = jnp.exp2(part - top)
            total += jnp.sum(weights, axis=-1, keepdims=True)
            mix += jnp.dot(weights.astype(jnp.bfloat16), values, preferred_element_type=jnp.float32)
        out[:, g * HD : (g + 1) * HD] = (mix / total).astype(jnp.bfloat16)

    @pl.when(pl.program_id(0) == pl.num_programs(0) - 1)
    def _():
        for copy in copies:
            copy.wait()


def fill_attend(place, query, cache, entries, heads, source, chunk, after=()):
    count = query.shape[0]
    groups = query.shape[1] // heads // HD
    stored = cache.shape[2]
    chips = len(entries)
    pairs = count * groups * heads * (stored + chips * count)
    target = (source.shape[1] // chunk, source.shape[0], chunk) if chunk else source.shape
    return pl.pallas_call(
        functools.partial(fill_kernel, groups, chips, chunk),
        out_shape=[jax.ShapeDtypeStruct(query.shape, jnp.bfloat16), stays_in_vmem(target)],
        grid_spec=pltpu.PrefetchScalarGridSpec(
            num_scalar_prefetch=1,
            grid=(heads,),
            in_specs=[
                pl.BlockSpec((count, groups * HD), lambda j, s: (0, j)),
                pl.BlockSpec((1, 1, stored, HD), lambda j, s: (0, 0, 0, j)),
                pl.BlockSpec((1, 1, stored, HD), lambda j, s: (1, 0, 0, j)),
            ]
            + [pl.BlockSpec((1, count, HD), lambda j, s: (0, 0, j))] * chips
            + [pl.BlockSpec((1, count, HD), lambda j, s: (1, 0, j))] * chips
            + [IN_PLACE] * (1 + len(after)),
            out_specs=[pl.BlockSpec((count, groups * HD), lambda j, s: (0, j)), IN_PLACE],
            scratch_shapes=[pltpu.SemaphoreType.DMA((target[0],))],
        ),
        compiler_params=params(12),
        cost_estimate=cost(8 * pairs * HD, 2 * cache.size, pairs),
        name="fill_attend",
    )(place, query, cache, cache, *entries, *entries, source, *after)


def step_kernel(heads, lengths, query, entries, held, weight, out, scores, shares, weight_held, weight_sem):
    scaling = 1.0 / math.sqrt(HD)
    slots, stored, width = held.shape[1:]
    groups = query.shape[1] // width
    lanes = 8
    weight_copy = pltpu.make_async_copy(weight, weight_held, weight_sem)
    weight_copy.start()
    across = (((1,), (1,)), ((), ()))
    places = lax.broadcasted_iota(jnp.int32, (1, stored), 1)
    blank = jnp.zeros((1, HD), jnp.float32)
    new_keys = entries[0].astype(jnp.float32)
    new_values = entries[1].astype(jnp.float32)
    own_scores = []
    for s in range(slots):
        rows = []
        for j in range(heads):
            for g in range(groups):
                at = (j * groups + g) * HD
                part = query[s : s + 1, at : at + HD]
                rows.append(
                    jnp.concatenate([part if i == j else blank for i in range(heads)], axis=1)
                )
        rows.append(jnp.zeros((lanes - heads * groups, width), jnp.float32))
        rows = jnp.concatenate(rows, axis=0)
        own_scores.append(jnp.sum(rows * new_keys[s : s + 1], axis=-1, keepdims=True))
        old = lax.dot_general(
            rows.astype(jnp.bfloat16), held[0, s], across, preferred_element_type=jnp.float32
        )
        scores[s * lanes : (s + 1) * lanes, :] = jnp.where(
            places < lengths[s], old * scaling, NEGATIVE
        )
    old = scores[...]
    own = jnp.concatenate(own_scores, axis=0) * scaling
    top = jnp.maximum(jnp.max(old, axis=-1, keepdims=True), own)
    old = jnp.exp(old - top)
    own = jnp.exp(own - top)
    total = jnp.sum(old, axis=-1, keepdims=True) + own
    shares[...] = old / total
    own = (own / total).astype(jnp.bfloat16).astype(jnp.float32)
    attended = []
    for s in range(slots):
        here = slice(s * lanes, (s + 1) * lanes)
        mix = jnp.dot(
            shares[here, :].astype(jnp.bfloat16), held[1, s], preferred_element_type=jnp.float32
        )
        mix += own[here] * new_values[s : s + 1]
        parts = []
        for j in range(heads):
            for g in range(groups):
                row = j * groups + g
                parts.append(mix[row : row + 1, j * HD : (j + 1) * HD])
        attended.append(jnp.concatenate(parts, axis=1))
    if out.shape[0] > slots:
        attended.append(jnp.zeros((out.shape[0] - slots, query.shape[1]), jnp.float32))
    attended = jnp.concatenate(attended, axis=0).astype(jnp.bfloat16)
    weight_copy.wait()
    part = jnp.dot(attended, weight_held[...], preferred_element_type=jnp.float32)
    out[...] = part.astype(jnp.bfloat16)


def step_attend(lengths, query, entries, cache, weight, heads):
    slots, stored = cache.shape[1:3]
    padded = query.shape[0]
    rows = slots * 8
    return pl.pallas_call(
        functools.partial(step_kernel, heads),
        out_shape=jax.ShapeDtypeStruct((padded, weight.shape[1]), jnp.bfloat16),
        in_specs=[SMEM_WHOLE] + [VMEM_WHOLE] * 3 + [IN_PLACE],
        out_specs=VMEM_WHOLE,
        scratch_shapes=[
            pltpu.VMEM((rows, stored), jnp.float32),
            pltpu.VMEM((rows, stored), jnp.float32),
            pltpu.VMEM(weight.shape, jnp.bfloat16),
            pltpu.SemaphoreType.DMA(()),
        ],
        compiler_params=params(12),
        cost_estimate=cost(16 * cache.size, 2 * cache.size, rows * stored),
        name="step_attend",
    )(lengths, query, entries, cache, weight)


def out_kernel(place, mine, sib, weight, sib_weight, *refs):
    out = refs[-1]
    half = out.shape[1]
    cols = pl.ds(pl.multiple_of(place[0] * half, half), half)
    part = jnp.dot(mine[...], weight[:, cols], preferred_element_type=jnp.float32)
    part += jnp.dot(sib[...], sib_weight[:, cols], preferred_element_type=jnp.float32)
    out[...] = part.astype(jnp.bfloat16)


def out_project(place, mine, sib, weight, sib_weight, after=()):
    rows, depth = mine.shape
    half = weight.shape[1] // 2
    return pl.pallas_call(
        out_kernel,
        out_shape=jax.ShapeDtypeStruct((rows, half), jnp.bfloat16),
        in_specs=[SMEM_WHOLE] + [VMEM_WHOLE] * 4 + [IN_PLACE] * len(after),
        out_specs=VMEM_WHOLE,
        compiler_params=params(8),
        cost_estimate=cost(4 * rows * depth * half, 4 * depth * half + 6 * rows * half),
        name="out_project",
    )(place, mine, sib, weight, sib_weight, *after)


def forward_kernel(loads, chips, n_dec, n_weights, n_after, chunk, place, *refs):
    refs = list(refs)
    mine, sib = refs[:2]
    shares = refs[2 : 2 + 2 * chips]
    refs = refs[2 + 2 * chips :]
    if n_dec:
        dec, dec_shares = refs[0], refs[1 : 1 + 2 * chips]
        refs = refs[1 + 2 * chips :]
    split = n_weights == 2
    gain, *weights = refs[: 1 + n_weights]
    refs = refs[1 + n_weights + n_after :]
    if split:
        resid, hidden = refs[:2]
        held, inner = refs[2:]
    else:
        keep, give, resid = refs[:3]
        refs = refs[3:]
        if n_dec:
            dec_out, dec_resid = refs[:2]
            refs = refs[2:]
        if loads:
            sources, weights[1:], refs = weights[1:], refs[:2], refs[2:]
        held, inner, hidden = refs[:3]
    copies = {}
    if loads:
        arrived = refs[3]
        for w, source in enumerate(sources, 1):
            for i in range(weights[w].shape[0]):
                copies[w, i] = pltpu.make_async_copy(
                    source.at[:, pl.ds(i * chunk, chunk)], weights[w].at[i], arrived.at[w - 1, i]
                )
                copies[w, i].start()

    def ready(w, i):
        if (w, i) in copies:
            copies[w, i].wait()
        return weights[w][i]

    piece = mine.shape[0]
    half = shares[0].shape[1]
    core = place[0]
    for rows, at_rows, put in ((mine, core, 0), (sib, 1 - core, piece)):
        here = pl.ds(pl.multiple_of(at_rows * piece, piece), piece)
        for side in range(2):
            at = core if side == 0 else 1 - core
            cols = pl.ds(pl.multiple_of(at * half, half), half)
            added = shares[side][here, :].astype(jnp.float32)
            for k in range(1, chips):
                added += shares[2 * k + side][here, :].astype(jnp.float32)
            value = rows[:, cols].astype(jnp.float32) + added
            held[put : put + piece, cols] = value.astype(jnp.bfloat16)
    if n_dec:
        added = dec_shares[0][...].astype(jnp.float32)
        for share in dec_shares[1:]:
            added += share[...].astype(jnp.float32)
        held[2 * piece :, :] = (dec[...].astype(jnp.float32) + added).astype(jnp.bfloat16)
    for put in range(0, held.shape[0], piece):
        here = slice(put, min(put + piece, held.shape[0]))
        inner[here, :] = normed(held[here, :].astype(jnp.float32), gain[...])
    resid[...] = held[:piece, :]
    if n_dec:
        dec_resid[...] = held[2 * piece :, :]

    for i in range(weights[0].shape[0]):
        at = slice(i * chunk, (i + 1) * chunk)
        gated = jnp.dot(inner[...], ready(0, i), preferred_element_type=jnp.float32)
        raised = jnp.dot(inner[...], ready(1, i), preferred_element_type=jnp.float32)
        hidden[:, at] = (gated / (1.0 + jnp.exp(-gated)) * raised).astype(jnp.bfloat16)
    for i in range(0 if split else weights[2].shape[0]):
        at = slice(i * chunk, (i + 1) * chunk)
        part = jnp.dot(hidden[...], ready(2, i), preferred_element_type=jnp.float32)
        part = part.astype(jnp.bfloat16)
        keep[:, at] = part[:piece]
        give[:, at] = part[piece : 2 * piece]
        if n_dec:
            dec_out[:, at] = part[2 * piece :]


def lower_kernel(hidden, down, *refs):
    keep, give = refs[-2:]
    piece = keep.shape[0]
    chunk = down.shape[2]
    for i in range(down.shape[0]):
        at = slice(i * chunk, (i + 1) * chunk)
        part = jnp.dot(hidden[...], down[i], preferred_element_type=jnp.float32)
        part = part.astype(jnp.bfloat16)
        keep[:, at] = part[:piece]
        give[:, at] = part[piece:]


def lower(hidden, down, after):
    rows, units = hidden.shape
    width = down.shape[0] * down.shape[2]
    return pl.pallas_call(
        lower_kernel,
        out_shape=[jax.ShapeDtypeStruct((rows // 2, width), jnp.bfloat16)] * 2,
        in_specs=[VMEM_WHOLE] * 2 + [IN_PLACE] * len(after),
        out_specs=[VMEM_WHOLE] * 2,
        compiler_params=params(8),
        cost_estimate=cost(2 * rows * width * units, 2 * width * units),
        name="lower",
    )(hidden, down, *after)


def feed_forward(place, mine, sib, shares, gain, weights, loads, dec=None, dec_shares=None, after=()):
    piece, width = mine.shape
    chips = len(shares) // 2
    n_dec = 0 if dec is None else dec.shape[0]
    rows = 2 * piece + n_dec
    args = [mine, sib, *shares]
    if n_dec:
        args += [dec, *dec_shares]
    args += [gain]
    split = len(weights) == 2
    chunk = weights[0].shape[2]
    units = weights[0].shape[0] * chunk
    if split:
        shapes = [(piece, width), (rows, units)]
    else:
        shapes = [(n, width) for n in [piece] * 3 + [n_dec] * 2 * bool(n_dec)]
    out_shape = [jax.ShapeDtypeStruct(shape, jnp.bfloat16) for shape in shapes]
    scratch = [pltpu.VMEM((rows, width), jnp.bfloat16)] * 2
    if not split:
        scratch.append(pltpu.VMEM((rows, units), jnp.bfloat16))
    if loads:
        out_shape += [stays_in_vmem((units // chunk, width, chunk))]
        out_shape += [stays_in_vmem((width // chunk, units, chunk))]
        scratch.append(pltpu.SemaphoreType.DMA((2, max(units, width) // chunk)))
    return pl.pallas_call(
        functools.partial(forward_kernel, loads, chips, n_dec, len(weights), len(after), chunk),
        out_shape=out_shape,
        in_specs=[SMEM_WHOLE]
        + [VMEM_WHOLE] * (len(args) + 1)
        + [IN_PLACE if loads else VMEM_WHOLE] * (len(weights) - 1)
        + [IN_PLACE] * len(after),
        out_specs=[VMEM_WHOLE] * len(out_shape),
        scratch_shapes=scratch,
        compiler_params=params(9),
        cost_estimate=cost(6 * rows * width * units, 6 * width * units, rows * units),
        name="feed_forward",
    )(place, *args, *weights, *after)


def angle_tables(places):
    halfway = HD // 2
    powers = jnp.arange(halfway, dtype=jnp.float32) * (2.0 / HD)
    inverse = THETA ** (-powers)
    angles = places.astype(jnp.float32)[:, None] * inverse[None, :]
    cosine, sine = jnp.cos(angles), jnp.sin(angles)
    return jnp.concatenate([cosine, cosine], axis=-1), jnp.concatenate([-sine, sine], axis=-1)


def add(*values):
    total = values[0].astype(jnp.float32)
    for value in values[1:]:
        total = total + value.astype(jnp.float32)
    return total.astype(jnp.bfloat16)


def on_device(
    prefill_rows,
    decode_rows,
    deal_order,
    prefill_offset,
    cache_length,
    prefill_cache,
    decode_cache,
    qkv_weight,
    out_weight,
    attention_gain,
    forward_gain,
    gate_weight,
    up_weight,
    down_weight,
):
    tensor_count = lax.axis_size("tensor")
    dp_count = lax.axis_size("dp")
    chips = tensor_count // 2
    tensor_place = lax.axis_index("tensor")
    group_place = lax.axis_index("dp")
    chip, core = tensor_place // 2, tensor_place % 2
    piece, width = prefill_rows.shape
    per_device = decode_rows.shape[0]
    requests = deal_order.shape[0]
    slots = cache_length.shape[0]
    padded = -(-slots // 16) * 16
    heads = qkv_weight.shape[1]
    tokens = piece * tensor_count

    def place_of(k):
        spots = [core, (chip + k) % chips, prefill_offset[0]]
        return jnp.stack(spots + [(chip + j) % chips for j in range(chips)]).astype(jnp.int32)

    places = [place_of(k) for k in range(chips)]
    weight = in_hbm(qkv_weight.reshape(width, -1))
    gate_weight, up_weight, down_weight = map(in_hbm, (gate_weight, up_weight, down_weight))
    prefill_cache, decode_cache = in_hbm(prefill_cache), in_hbm(decode_cache)

    mines = [prefill_rows] + [from_chip(prefill_rows, k) for k in range(1, chips)]
    sibs = [swap_cores(rows) for rows in mines]

    low = max(dp_count // 4, 1)
    pool = [decode_rows] + [swap_groups(decode_rows, i) for i in range(1, low)]
    pool = jnp.concatenate(pool, axis=0)
    pool = [pool] + [swap_groups(pool, i * low) for i in range(1, dp_count // low)]
    pool = jnp.concatenate(pool, axis=0)
    index = jnp.arange(dp_count * per_device, dtype=jnp.int32)
    origin = jnp.bitwise_xor(group_place, index // per_device)
    request = (origin * tensor_count + tensor_place) * per_device + index % per_device
    slot_of = jnp.sum(
        jnp.where(
            request[:, None] == jnp.arange(requests, dtype=jnp.int32)[None, :],
            deal_order[None, :],
            0,
        ),
        axis=1,
    )
    in_group = slot_of - group_place * slots
    chooser = (jnp.arange(padded, dtype=jnp.int32)[:, None] == in_group[None, :]) & (
        in_group[None, :] < slots
    )
    dealt = jnp.dot(
        chooser.astype(jnp.bfloat16), pool, preferred_element_type=jnp.float32
    ).astype(jnp.bfloat16)

    gain = attention_gain.reshape(1, width)
    tables = angle_tables(prefill_offset[0] + jnp.arange(tokens, dtype=jnp.int32))
    dec_tables = angle_tables(jnp.pad(cache_length, (0, padded - slots)))
    queries, entries, everything = [None] * chips, [None] * chips, None
    for k in range(chips):
        last = k == chips - 1
        if last:
            others = from_rest(dealt)
            if k:
                *others, queries[k - 1] = lax.optimization_barrier((*others, queries[k - 1]))
            dealt = add(dealt, *others)
        got = project(
            places[k],
            in_hbm(mines[k]),
            in_hbm(sibs[k]),
            gain,
            weight,
            tables,
            heads,
            everything,
            dealt if last else None,
            dec_tables if last else None,
            slots,
            [queries[k - 1]] if k else [dealt],
        )
        queries[k], entries[k], everything = got[:3]
        if k == 0:
            weight = got[-1]
        if last:
            dec_query, dec_entries = got[3:5]

    out_share = in_hbm(out_weight)
    sib_weight, queries[-1] = lax.optimization_barrier((out_weight, queries[-1]))
    sib_weight = in_vmem(swap_cores(sib_weight))
    out_weight = in_vmem(out_weight)

    def finish(attended, place):
        return out_project(place, attended, swap_cores(attended), out_weight, sib_weight)

    parts = []
    dec_shares = []
    for k in range(chips):
        wanted = decode_cache if k == 0 else gate_weight if k == 1 else out_share
        attended, fetched = fill_attend(
            places[k],
            queries[k],
            prefill_cache,
            entries,
            heads,
            wanted,
            width // 4 if k else 0,
            dec_shares[:1],
        )
        if k == 1:
            held_gate = fetched
        parts.append(finish(attended, places[k]))
        if k == 0:
            lengths, parts[0] = lax.optimization_barrier((cache_length, parts[0]))
            dec_part = step_attend(
                lengths, dec_query, dec_entries, fetched, out_share, heads
            )
            dec_shares = [dec_part, *from_rest(dec_part)]

    def shares_of(own, others):
        pairs = []
        for value in [own, *others]:
            pairs += [value, swap_cores(value)]
        return pairs

    gain = forward_gain.reshape(1, width)
    order = [*range(1, chips), 0]

    def fetch(b):
        return [from_chip(parts[(b - j) % chips], j) for j in range(1, chips)]

    theirs, dec_shares[1:] = lax.optimization_barrier((fetch(order[0]), dec_shares[1:]))
    weights = [held_gate, up_weight, down_weight]
    arrived, sent = [], []
    for n, b in enumerate(order):
        got = feed_forward(
            places[b],
            mines[b],
            sibs[b],
            shares_of(parts[b], theirs),
            gain,
            weights if n + 1 < chips else weights[:2],
            n == 0,
            dealt if n == 0 else None,
            dec_shares if n == 0 else None,
            sent,
        )
        if n + 1 < chips:
            keep, give = got[:2]
            *theirs, keep = lax.optimization_barrier((*fetch(order[n + 1]), keep))
            both = add(keep, swap_cores(give))
            arrived.append(from_chip(both, chips - b))
            sent = [both]
        if n == 0:
            dec_sum, dec_resid, *weights[1:] = got[3:]
            dec_others = from_rest(dec_sum)
    resid, hidden = got
    dec_sum, hidden = lax.optimization_barrier((dec_sum, hidden))
    final = add(dec_resid, dec_sum, *dec_others)
    picker = in_group[:, None] == jnp.arange(padded, dtype=jnp.int32)[None, :]
    picker = picker & (in_group[:, None] < slots)
    routed = jnp.dot(
        picker.astype(jnp.bfloat16), final, preferred_element_type=jnp.float32
    ).astype(jnp.bfloat16)
    keep, give = lower(hidden, weights[2], [routed])
    low = max(dp_count // 4, 1)
    pairs = routed.reshape(dp_count // low, low * per_device, width)
    rows = add(
        pairs[0], *[swap_groups(pairs[i], i * low) for i in range(1, dp_count // low)]
    )
    *arrived, rows, give = lax.optimization_barrier((*arrived, rows, give))
    pairs = rows.reshape(low, per_device, width)
    others = [swap_groups(pairs[i], i) for i in range(1, low)]
    prefill_out = add(resid, keep, swap_cores(give), *arrived)
    others, prefill_out = lax.optimization_barrier((others, prefill_out))
    routed = add(pairs[0], *others)
    return (prefill_out, routed, everything, dec_entries)


def solution(mesh):
    placed = (
        P(("dp", "tensor"), None),
        P(("dp", "tensor"), None),
        P(),
        P("dp"),
        P("dp"),
        P(None, "dp", None, "tensor"),
        P(None, "dp", None, "tensor"),
        P(None, "tensor", None),
        P("tensor", None),
        P(),
        P(),
        P(None, "tensor"),
        P(None, "tensor"),
        P("tensor", None),
    )
    return jax.shard_map(
        on_device,
        mesh=mesh,
        in_specs=placed,
        out_specs=(
            P(("dp", "tensor"), None),
            P(("dp", "tensor"), None),
            P(None, "dp", "tensor"),
            P(None, "dp", "tensor"),
        ),
        check_vma=False,
    )
```

```python
import functools
import math

import jax
import jax.numpy as jnp
from jax import lax
from jax.experimental import pallas as pl
from jax.experimental.pallas import tpu as pltpu
from jax.sharding import PartitionSpec as P

HD = 128
EPSILON = 1e-06
THETA = 1000000.0
NEGATIVE = -1e30
MIB = 1 << 20


def swap_cores(value):
    count = lax.axis_size("tensor")
    return lax.ppermute(value, "tensor", [(i, i ^ 1) for i in range(count)])


def from_chip(value, step):
    count = lax.axis_size("tensor")
    chips = count // 2
    return lax.ppermute(
        value, "tensor", [(i, (i // 2 - step) % chips * 2 + i % 2) for i in range(count)]
    )


def from_other(value, step):
    count = lax.axis_size("tensor")
    return lax.ppermute(
        value, "tensor", [(i, (i // 2 - step) % (count // 2) * 2 + 1 - i % 2) for i in range(count)]
    )


def from_rest(value):
    chips = lax.axis_size("tensor") // 2
    return [from_chip(value, k) for k in range(1, chips)] + [from_other(value, k) for k in range(chips)]


def swap_groups(value, mask):
    count = lax.axis_size("dp")
    return lax.ppermute(value, "dp", [(i, i ^ mask) for i in range(count)])


def whole(shape):
    return pl.BlockSpec(shape, lambda *_: (0,) * len(shape))


def params(mib):
    return pltpu.CompilerParams(vmem_limit_bytes=mib * MIB)


def cost(flops, moved, exps=0):
    return pl.CostEstimate(flops=int(flops), bytes_accessed=int(moved), transcendentals=int(exps))


def normed(values, gain):
    spread = jnp.mean(values * values, axis=-1, keepdims=True)
    return (values * lax.rsqrt(spread + EPSILON) * gain).astype(jnp.bfloat16)


def turn(vectors, cosine, sine):
    return vectors * cosine + pltpu.roll(vectors, HD // 2, 1) * sine


def in_vmem(value):
    return pltpu.with_memory_space_constraint(value, pltpu.VMEM)


def in_hbm(value):
    return pltpu.with_memory_space_constraint(value, pltpu.HBM)


def stays_in_vmem(shape):
    return pltpu.VMEM(shape, jnp.bfloat16)


VMEM_WHOLE = pl.BlockSpec(memory_space=pltpu.VMEM)
SMEM_WHOLE = pl.BlockSpec(memory_space=pltpu.SMEM)
IN_PLACE = pl.BlockSpec(memory_space=pl.ANY)


def project_kernel(loads, n_dec, n_after, groups, heads, place, *refs):
    refs = list(refs)
    mine, sib, weight, gain, cosine, sine = refs[:6]
    refs = refs[6:]
    if n_dec:
        dec, dec_cos, dec_sin = refs[:3]
        refs = refs[3:]
    refs = refs[n_after:]
    query, entries, everything = refs[:3]
    if n_dec:
        dec_query, dec_entries = refs[3:5]
    inner, rows_held, row_sems, weight_sems, out_sem = refs[-5:]
    weight_held = refs[-6] if loads else weight
    piece = mine.shape[0]
    core = place[0]
    scale = gain[...]
    depth = (groups + 2) * HD
    row_copies = [
        pltpu.make_async_copy(ref, rows_held.at[i], row_sems.at[i])
        for i, ref in enumerate((mine, sib))
    ]
    weight_copies = [
        pltpu.make_async_copy(
            weight.at[:, pl.ds(j * depth, depth)], weight_held.at[j], weight_sems.at[j]
        )
        for j in range(heads if loads else 0)
    ]
    for copy in row_copies + weight_copies:
        copy.start()
    for i, at in enumerate((core, 1 - core)):
        row_copies[i].wait()
        start = pl.multiple_of(at * piece, piece)
        inner[pl.ds(start, piece), :] = normed(rows_held[i].astype(jnp.float32), scale)
    if n_dec:
        inner[2 * piece :, :] = normed(dec[...].astype(jnp.float32), scale)
    here = pl.ds(pl.multiple_of(place[1] * 2 * piece, 2 * piece), 2 * piece)
    for j in range(heads):
        if loads:
            weight_copies[j].wait()
        mixed = jnp.dot(inner[...], weight_held[j], preferred_element_type=jnp.float32)

        def put(rows, cos, sin, query_out, entry_out):
            for g in range(groups):
                part = rows[:, g * HD : (g + 1) * HD]
                at = (j * groups + g) * HD
                turned = turn(part, cos, sin).astype(jnp.bfloat16)
                query_out[:, at : at + HD] = turned.astype(query_out.dtype)
            key = turn(rows[:, groups * HD : (groups + 1) * HD], cos, sin).astype(jnp.bfloat16)
            value = rows[:, (groups + 1) * HD :].astype(jnp.bfloat16)
            size = entry_out.shape[1]
            entry_out[0, :, j * HD : (j + 1) * HD] = key[:size]
            entry_out[1, :, j * HD : (j + 1) * HD] = value[:size]

        put(mixed[: 2 * piece], cosine[here, :], sine[here, :], query, entries)
        if n_dec:
            put(mixed[2 * piece :], dec_cos[...], dec_sin[...], dec_query, dec_entries)
    keep = pltpu.make_async_copy(entries, everything.at[:, here, :], out_sem)
    keep.start()
    keep.wait()


def project(
    place, mine, sib, gain, weight, tables, heads, everything, dec=None, dec_tables=None, slots=0, after=()
):
    piece, width = mine.shape
    loads = everything is None
    depth = weight.shape[1] // heads if loads else weight.shape[2]
    groups = depth // HD - 2
    block = 2 * piece
    n_dec = 0 if dec is None else dec.shape[0]
    args = [mine, sib, weight, gain, *tables]
    if n_dec:
        args += [dec, *dec_tables]
    n_operands = len(args)
    after = list(after)
    aliases = {}
    if everything is not None:
        after.append(everything)
        aliases = {n_operands + len(after): 2}
    wide = heads * groups * HD
    out_shape = [
        jax.ShapeDtypeStruct((block, wide), jnp.bfloat16),
        jax.ShapeDtypeStruct((2, block, heads * HD), jnp.bfloat16),
        jax.ShapeDtypeStruct((2, tables[0].shape[0], heads * HD), jnp.bfloat16),
    ]
    if n_dec:
        out_shape += [
            jax.ShapeDtypeStruct((n_dec, wide), jnp.float32),
            jax.ShapeDtypeStruct((2, slots, heads * HD), jnp.bfloat16),
        ]
    if loads:
        out_shape.append(stays_in_vmem((heads, width, depth)))
    rows = block + n_dec
    return pl.pallas_call(
        functools.partial(project_kernel, loads, n_dec, len(after), groups, heads),
        out_shape=out_shape,
        in_specs=[SMEM_WHOLE]
        + [IN_PLACE] * 2
        + [IN_PLACE if loads else VMEM_WHOLE]
        + [VMEM_WHOLE] * (len(args) - 3)
        + [IN_PLACE] * len(after),
        out_specs=[VMEM_WHOLE] * 2 + [IN_PLACE] + [VMEM_WHOLE] * (len(out_shape) - 3),
        scratch_shapes=[
            pltpu.VMEM((rows, width), jnp.bfloat16),
            pltpu.VMEM((2, piece, width), jnp.bfloat16),
            pltpu.SemaphoreType.DMA((2,)),
            pltpu.SemaphoreType.DMA((heads,)),
            pltpu.SemaphoreType.DMA(()),
        ],
        input_output_aliases=aliases,
        compiler_params=params(12),
        cost_estimate=cost(2 * rows * weight.size, 2 * (weight.size + 2 * rows * width)),
        name="project",
    )(place, *args, *after)


def fill_kernel(groups, chips, chunk, place, query, cache_key, cache_value, *refs):
    new_keys, new_values = refs[:chips], refs[chips : 2 * chips]
    source, (out, target, arrived) = refs[2 * chips], refs[-3:]
    pieces = [
        source.at[:, pl.ds(i * chunk, chunk)] if chunk else source.at[i]
        for i in range(target.shape[0])
    ]
    copies = [
        pltpu.make_async_copy(piece, target.at[i], arrived.at[i]) for i, piece in enumerate(pieces)
    ]

    @pl.when(pl.program_id(0) == 0)
    def _():
        for copy in copies:
            copy.start()

    scaling = math.log2(math.e) / math.sqrt(HD)
    count = query.shape[0]
    stored = cache_key.shape[2]
    old_seen = lax.broadcasted_iota(jnp.int32, (1, stored), 1) < place[2]
    ahead = lax.broadcasted_iota(jnp.int32, (count, count), 1) - lax.broadcasted_iota(
        jnp.int32, (count, count), 0
    )
    across = (((1,), (1,)), ((), ()))
    for g in range(groups):
        rows = query[:, g * HD : (g + 1) * HD]
        scores = lax.dot_general(rows, cache_key[0, 0], across, preferred_element_type=jnp.float32)
        scores = [jnp.where(old_seen, scores * scaling, NEGATIVE)]
        for k in range(chips):
            fresh = lax.dot_general(
                rows, new_keys[k][0], across, preferred_element_type=jnp.float32
            )
            gap = (place[1] - place[3 + k]) * count
            scores.append(jnp.where(ahead <= gap, fresh * scaling, NEGATIVE))
        top = jnp.max(scores[0], axis=-1, keepdims=True)
        for part in scores[1:]:
            top = jnp.maximum(top, jnp.max(part, axis=-1, keepdims=True))
        mix, total = 0.0, 0.0
        for part, values in zip(scores, [cache_value[0, 0], *[v[0] for v in new_values]]):
            weights = jnp.exp2(part - top)
            total += jnp.sum(weights, axis=-1, keepdims=True)
            mix += jnp.dot(weights.astype(jnp.bfloat16), values, preferred_element_type=jnp.float32)
        out[:, g * HD : (g + 1) * HD] = (mix / total).astype(jnp.bfloat16)

    @pl.when(pl.program_id(0) == pl.num_programs(0) - 1)
    def _():
        for copy in copies:
            copy.wait()


def fill_attend(place, query, cache, entries, heads, source, chunk, after=()):
    count = query.shape[0]
    groups = query.shape[1] // heads // HD
    stored = cache.shape[2]
    chips = len(entries)
    pairs = count * groups * heads * (stored + chips * count)
    target = (source.shape[1] // chunk, source.shape[0], chunk) if chunk else source.shape
    return pl.pallas_call(
        functools.partial(fill_kernel, groups, chips, chunk),
        out_shape=[jax.ShapeDtypeStruct(query.shape, jnp.bfloat16), stays_in_vmem(target)],
        grid_spec=pltpu.PrefetchScalarGridSpec(
            num_scalar_prefetch=1,
            grid=(heads,),
            in_specs=[
                pl.BlockSpec((count, groups * HD), lambda j, s: (0, j)),
                pl.BlockSpec((1, 1, stored, HD), lambda j, s: (0, 0, 0, j)),
                pl.BlockSpec((1, 1, stored, HD), lambda j, s: (1, 0, 0, j)),
            ]
            + [pl.BlockSpec((1, count, HD), lambda j, s: (0, 0, j))] * chips
            + [pl.BlockSpec((1, count, HD), lambda j, s: (1, 0, j))] * chips
            + [IN_PLACE] * (1 + len(after)),
            out_specs=[pl.BlockSpec((count, groups * HD), lambda j, s: (0, j)), IN_PLACE],
            scratch_shapes=[pltpu.SemaphoreType.DMA((target[0],))],
        ),
        compiler_params=params(12),
        cost_estimate=cost(8 * pairs * HD, 2 * cache.size, pairs),
        name="fill_attend",
    )(place, query, cache, cache, *entries, *entries, source, *after)


def step_kernel(heads, lengths, query, entries, held, weight, out, scores, shares, weight_held, weight_sem):
    scaling = 1.0 / math.sqrt(HD)
    slots, stored, width = held.shape[1:]
    groups = query.shape[1] // width
    lanes = 8
    weight_copy = pltpu.make_async_copy(weight, weight_held, weight_sem)
    weight_copy.start()
    across = (((1,), (1,)), ((), ()))
    places = lax.broadcasted_iota(jnp.int32, (1, stored), 1)
    blank = jnp.zeros((1, HD), jnp.float32)
    new_keys = entries[0].astype(jnp.float32)
    new_values = entries[1].astype(jnp.float32)
    own_scores = []
    for s in range(slots):
        rows = []
        for j in range(heads):
            for g in range(groups):
                at = (j * groups + g) * HD
                part = query[s : s + 1, at : at + HD]
                rows.append(
                    jnp.concatenate([part if i == j else blank for i in range(heads)], axis=1)
                )
        rows.append(jnp.zeros((lanes - heads * groups, width), jnp.float32))
        rows = jnp.concatenate(rows, axis=0)
        own_scores.append(jnp.sum(rows * new_keys[s : s + 1], axis=-1, keepdims=True))
        old = lax.dot_general(
            rows.astype(jnp.bfloat16), held[0, s], across, preferred_element_type=jnp.float32
        )
        scores[s * lanes : (s + 1) * lanes, :] = jnp.where(
            places < lengths[s], old * scaling, NEGATIVE
        )
    old = scores[...]
    own = jnp.concatenate(own_scores, axis=0) * scaling
    top = jnp.maximum(jnp.max(old, axis=-1, keepdims=True), own)
    old = jnp.exp(old - top)
    own = jnp.exp(own - top)
    total = jnp.sum(old, axis=-1, keepdims=True) + own
    shares[...] = old / total
    own = (own / total).astype(jnp.bfloat16).astype(jnp.float32)
    attended = []
    for s in range(slots):
        here = slice(s * lanes, (s + 1) * lanes)
        mix = jnp.dot(
            shares[here, :].astype(jnp.bfloat16), held[1, s], preferred_element_type=jnp.float32
        )
        mix += own[here] * new_values[s : s + 1]
        parts = []
        for j in range(heads):
            for g in range(groups):
                row = j * groups + g
                parts.append(mix[row : row + 1, j * HD : (j + 1) * HD])
        attended.append(jnp.concatenate(parts, axis=1))
    if out.shape[0] > slots:
        attended.append(jnp.zeros((out.shape[0] - slots, query.shape[1]), jnp.float32))
    attended = jnp.concatenate(attended, axis=0).astype(jnp.bfloat16)
    weight_copy.wait()
    part = jnp.dot(attended, weight_held[...], preferred_element_type=jnp.float32)
    out[...] = part.astype(jnp.bfloat16)


def step_attend(lengths, query, entries, cache, weight, heads):
    slots, stored = cache.shape[1:3]
    padded = query.shape[0]
    rows = slots * 8
    return pl.pallas_call(
        functools.partial(step_kernel, heads),
        out_shape=jax.ShapeDtypeStruct((padded, weight.shape[1]), jnp.bfloat16),
        in_specs=[SMEM_WHOLE] + [VMEM_WHOLE] * 3 + [IN_PLACE],
        out_specs=VMEM_WHOLE,
        scratch_shapes=[
            pltpu.VMEM((rows, stored), jnp.float32),
            pltpu.VMEM((rows, stored), jnp.float32),
            pltpu.VMEM(weight.shape, jnp.bfloat16),
            pltpu.SemaphoreType.DMA(()),
        ],
        compiler_params=params(12),
        cost_estimate=cost(16 * cache.size, 2 * cache.size, rows * stored),
        name="step_attend",
    )(lengths, query, entries, cache, weight)


def out_kernel(place, mine, sib, weight, sib_weight, *refs):
    out = refs[-1]
    half = out.shape[1]
    cols = pl.ds(pl.multiple_of(place[0] * half, half), half)
    part = jnp.dot(mine[...], weight[:, cols], preferred_element_type=jnp.float32)
    part += jnp.dot(sib[...], sib_weight[:, cols], preferred_element_type=jnp.float32)
    out[...] = part.astype(jnp.bfloat16)


def out_project(place, mine, sib, weight, sib_weight, after=()):
    rows, depth = mine.shape
    half = weight.shape[1] // 2
    return pl.pallas_call(
        out_kernel,
        out_shape=jax.ShapeDtypeStruct((rows, half), jnp.bfloat16),
        in_specs=[SMEM_WHOLE] + [VMEM_WHOLE] * 4 + [IN_PLACE] * len(after),
        out_specs=VMEM_WHOLE,
        compiler_params=params(8),
        cost_estimate=cost(4 * rows * depth * half, 4 * depth * half + 6 * rows * half),
        name="out_project",
    )(place, mine, sib, weight, sib_weight, *after)


def forward_kernel(loads, chips, n_dec, n_weights, n_after, chunk, place, *refs):
    refs = list(refs)
    mine, sib = refs[:2]
    shares = refs[2 : 2 + 2 * chips]
    refs = refs[2 + 2 * chips :]
    if n_dec:
        dec, dec_shares = refs[0], refs[1 : 1 + 2 * chips]
        refs = refs[1 + 2 * chips :]
    split = n_weights == 2
    gain, *weights = refs[: 1 + n_weights]
    refs = refs[1 + n_weights + n_after :]
    if split:
        resid, hidden = refs[:2]
        held, inner = refs[2:]
    else:
        keep, give, resid = refs[:3]
        refs = refs[3:]
        if n_dec:
            dec_out, dec_resid = refs[:2]
            refs = refs[2:]
        if loads:
            sources, weights[1:], refs = weights[1:], refs[:2], refs[2:]
        held, inner, hidden = refs[:3]
    copies = {}
    if loads:
        arrived = refs[3]
        for w, source in enumerate(sources, 1):
            for i in range(weights[w].shape[0]):
                copies[w, i] = pltpu.make_async_copy(
                    source.at[:, pl.ds(i * chunk, chunk)], weights[w].at[i], arrived.at[w - 1, i]
                )
                copies[w, i].start()

    def ready(w, i):
        if (w, i) in copies:
            copies[w, i].wait()
        return weights[w][i]

    piece = mine.shape[0]
    half = shares[0].shape[1]
    core = place[0]
    for rows, at_rows, put in ((mine, core, 0), (sib, 1 - core, piece)):
        here = pl.ds(pl.multiple_of(at_rows * piece, piece), piece)
        for side in range(2):
            at = core if side == 0 else 1 - core
            cols = pl.ds(pl.multiple_of(at * half, half), half)
            added = shares[side][here, :].astype(jnp.float32)
            for k in range(1, chips):
                added += shares[2 * k + side][here, :].astype(jnp.float32)
            value = rows[:, cols].astype(jnp.float32) + added
            held[put : put + piece, cols] = value.astype(jnp.bfloat16)
    if n_dec:
        added = dec_shares[0][...].astype(jnp.float32)
        for share in dec_shares[1:]:
            added += share[...].astype(jnp.float32)
        held[2 * piece :, :] = (dec[...].astype(jnp.float32) + added).astype(jnp.bfloat16)
    for put in range(0, held.shape[0], piece):
        here = slice(put, min(put + piece, held.shape[0]))
        inner[here, :] = normed(held[here, :].astype(jnp.float32), gain[...])
    resid[...] = held[:piece, :]
    if n_dec:
        dec_resid[...] = held[2 * piece :, :]

    for i in range(weights[0].shape[0]):
        at = slice(i * chunk, (i + 1) * chunk)
        gated = jnp.dot(inner[...], ready(0, i), preferred_element_type=jnp.float32)
        raised = jnp.dot(inner[...], ready(1, i), preferred_element_type=jnp.float32)
        hidden[:, at] = (gated / (1.0 + jnp.exp(-gated)) * raised).astype(jnp.bfloat16)
    for i in range(0 if split else weights[2].shape[0]):
        at = slice(i * chunk, (i + 1) * chunk)
        part = jnp.dot(hidden[...], ready(2, i), preferred_element_type=jnp.float32)
        part = part.astype(jnp.bfloat16)
        keep[:, at] = part[:piece]
        give[:, at] = part[piece : 2 * piece]
        if n_dec:
            dec_out[:, at] = part[2 * piece :]


def lower_kernel(hidden, down, *refs):
    keep, give = refs[-2:]
    piece = keep.shape[0]
    chunk = down.shape[2]
    for i in range(down.shape[0]):
        at = slice(i * chunk, (i + 1) * chunk)
        part = jnp.dot(hidden[...], down[i], preferred_element_type=jnp.float32)
        part = part.astype(jnp.bfloat16)
        keep[:, at] = part[:piece]
        give[:, at] = part[piece:]


def lower(hidden, down, after):
    rows, units = hidden.shape
    width = down.shape[0] * down.shape[2]
    return pl.pallas_call(
        lower_kernel,
        out_shape=[jax.ShapeDtypeStruct((rows // 2, width), jnp.bfloat16)] * 2,
        in_specs=[VMEM_WHOLE] * 2 + [IN_PLACE] * len(after),
        out_specs=[VMEM_WHOLE] * 2,
        compiler_params=params(8),
        cost_estimate=cost(2 * rows * width * units, 2 * width * units),
        name="lower",
    )(hidden, down, *after)


def feed_forward(place, mine, sib, shares, gain, weights, loads, dec=None, dec_shares=None, after=()):
    piece, width = mine.shape
    chips = len(shares) // 2
    n_dec = 0 if dec is None else dec.shape[0]
    rows = 2 * piece + n_dec
    args = [mine, sib, *shares]
    if n_dec:
        args += [dec, *dec_shares]
    args += [gain]
    split = len(weights) == 2
    chunk = weights[0].shape[2]
    units = weights[0].shape[0] * chunk
    if split:
        shapes = [(piece, width), (rows, units)]
    else:
        shapes = [(n, width) for n in [piece] * 3 + [n_dec] * 2 * bool(n_dec)]
    out_shape = [jax.ShapeDtypeStruct(shape, jnp.bfloat16) for shape in shapes]
    scratch = [pltpu.VMEM((rows, width), jnp.bfloat16)] * 2
    if not split:
        scratch.append(pltpu.VMEM((rows, units), jnp.bfloat16))
    if loads:
        out_shape += [stays_in_vmem((units // chunk, width, chunk))]
        out_shape += [stays_in_vmem((width // chunk, units, chunk))]
        scratch.append(pltpu.SemaphoreType.DMA((2, max(units, width) // chunk)))
    return pl.pallas_call(
        functools.partial(forward_kernel, loads, chips, n_dec, len(weights), len(after), chunk),
        out_shape=out_shape,
        in_specs=[SMEM_WHOLE]
        + [VMEM_WHOLE] * (len(args) + 1)
        + [IN_PLACE if loads else VMEM_WHOLE] * (len(weights) - 1)
        + [IN_PLACE] * len(after),
        out_specs=[VMEM_WHOLE] * len(out_shape),
        scratch_shapes=scratch,
        compiler_params=params(9),
        cost_estimate=cost(6 * rows * width * units, 6 * width * units, rows * units),
        name="feed_forward",
    )(place, *args, *weights, *after)


def angle_tables(places):
    halfway = HD // 2
    powers = jnp.arange(halfway, dtype=jnp.float32) * (2.0 / HD)
    inverse = THETA ** (-powers)
    angles = places.astype(jnp.float32)[:, None] * inverse[None, :]
    cosine, sine = jnp.cos(angles), jnp.sin(angles)
    return jnp.concatenate([cosine, cosine], axis=-1), jnp.concatenate([-sine, sine], axis=-1)


def add(*values):
    total = values[0].astype(jnp.float32)
    for value in values[1:]:
        total = total + value.astype(jnp.float32)
    return total.astype(jnp.bfloat16)


def on_device(
    prefill_rows,
    decode_rows,
    deal_order,
    prefill_offset,
    cache_length,
    prefill_cache,
    decode_cache,
    qkv_weight,
    out_weight,
    attention_gain,
    forward_gain,
    gate_weight,
    up_weight,
    down_weight,
):
    tensor_count = lax.axis_size("tensor")
    dp_count = lax.axis_size("dp")
    chips = tensor_count // 2
    tensor_place = lax.axis_index("tensor")
    group_place = lax.axis_index("dp")
    chip, core = tensor_place // 2, tensor_place % 2
    piece, width = prefill_rows.shape
    per_device = decode_rows.shape[0]
    requests = deal_order.shape[0]
    slots = cache_length.shape[0]
    padded = -(-slots // 16) * 16
    heads = qkv_weight.shape[1]
    tokens = piece * tensor_count

    def place_of(k):
        spots = [core, (chip + k) % chips, prefill_offset[0]]
        return jnp.stack(spots + [(chip + j) % chips for j in range(chips)]).astype(jnp.int32)

    places = [place_of(k) for k in range(chips)]
    weight = in_hbm(qkv_weight.reshape(width, -1))
    gate_weight, up_weight, down_weight = map(in_hbm, (gate_weight, up_weight, down_weight))
    prefill_cache, decode_cache = in_hbm(prefill_cache), in_hbm(decode_cache)

    mines = [prefill_rows] + [from_chip(prefill_rows, k) for k in range(1, chips)]
    sibs = [swap_cores(rows) for rows in mines]

    low = max(dp_count // 4, 1)
    pool = [decode_rows] + [swap_groups(decode_rows, i) for i in range(1, low)]
    pool = jnp.concatenate(pool, axis=0)
    pool = [pool] + [swap_groups(pool, i * low) for i in range(1, dp_count // low)]
    pool = jnp.concatenate(pool, axis=0)
    index = jnp.arange(dp_count * per_device, dtype=jnp.int32)
    origin = jnp.bitwise_xor(group_place, index // per_device)
    request = (origin * tensor_count + tensor_place) * per_device + index % per_device
    slot_of = jnp.sum(
        jnp.where(
            request[:, None] == jnp.arange(requests, dtype=jnp.int32)[None, :],
            deal_order[None, :],
            0,
        ),
        axis=1,
    )
    in_group = slot_of - group_place * slots
    chooser = (jnp.arange(padded, dtype=jnp.int32)[:, None] == in_group[None, :]) & (
        in_group[None, :] < slots
    )
    dealt = jnp.dot(
        chooser.astype(jnp.bfloat16), pool, preferred_element_type=jnp.float32
    ).astype(jnp.bfloat16)

    gain = attention_gain.reshape(1, width)
    tables = angle_tables(prefill_offset[0] + jnp.arange(tokens, dtype=jnp.int32))
    dec_tables = angle_tables(jnp.pad(cache_length, (0, padded - slots)))
    queries, entries, everything = [None] * chips, [None] * chips, None
    for k in range(chips):
        last = k == chips - 1
        if last:
            others = from_rest(dealt)
            if k:
                *others, queries[k - 1] = lax.optimization_barrier((*others, queries[k - 1]))
            dealt = add(dealt, *others)
        got = project(
            places[k],
            in_hbm(mines[k]),
            in_hbm(sibs[k]),
            gain,
            weight,
            tables,
            heads,
            everything,
            dealt if last else None,
            dec_tables if last else None,
            slots,
            [queries[k - 1]] if k else [dealt],
        )
        queries[k], entries[k], everything = got[:3]
        if k == 0:
            weight = got[-1]
        if last:
            dec_query, dec_entries = got[3:5]

    out_share = in_hbm(out_weight)
    sib_weight, queries[-1] = lax.optimization_barrier((out_weight, queries[-1]))
    sib_weight = in_vmem(swap_cores(sib_weight))
    out_weight = in_vmem(out_weight)

    def finish(attended, place):
        return out_project(place, attended, swap_cores(attended), out_weight, sib_weight)

    parts = []
    dec_shares = []
    for k in range(chips):
        wanted = decode_cache if k == 0 else gate_weight if k == 1 else out_share
        attended, fetched = fill_attend(
            places[k],
            queries[k],
            prefill_cache,
            entries,
            heads,
            wanted,
            width // 2 if k else 0,
            dec_shares[:1],
        )
        if k == 1:
            held_gate = fetched
        parts.append(finish(attended, places[k]))
        if k == 0:
            lengths, parts[0] = lax.optimization_barrier((cache_length, parts[0]))
            dec_part = step_attend(
                lengths, dec_query, dec_entries, fetched, out_share, heads
            )
            dec_shares = [dec_part, *from_rest(dec_part)]

    def shares_of(own, others):
        pairs = []
        for value in [own, *others]:
            pairs += [value, swap_cores(value)]
        return pairs

    gain = forward_gain.reshape(1, width)
    order = [*range(1, chips), 0]

    def fetch(b):
        return [from_chip(parts[(b - j) % chips], j) for j in range(1, chips)]

    theirs, dec_shares[1:] = lax.optimization_barrier((fetch(order[0]), dec_shares[1:]))
    weights = [held_gate, up_weight, down_weight]
    arrived, sent = [], []
    for n, b in enumerate(order):
        got = feed_forward(
            places[b],
            mines[b],
            sibs[b],
            shares_of(parts[b], theirs),
            gain,
            weights if n + 1 < chips else weights[:2],
            n == 0,
            dealt if n == 0 else None,
            dec_shares if n == 0 else None,
            sent,
        )
        if n + 1 < chips:
            keep, give = got[:2]
            *theirs, keep = lax.optimization_barrier((*fetch(order[n + 1]), keep))
            both = add(keep, swap_cores(give))
            arrived.append(from_chip(both, chips - b))
            sent = [both]
        if n == 0:
            dec_sum, dec_resid, *weights[1:] = got[3:]
            dec_others = from_rest(dec_sum)
    resid, hidden = got
    dec_sum, hidden = lax.optimization_barrier((dec_sum, hidden))
    final = add(dec_resid, dec_sum, *dec_others)
    picker = in_group[:, None] == jnp.arange(padded, dtype=jnp.int32)[None, :]
    picker = picker & (in_group[:, None] < slots)
    routed = jnp.dot(
        picker.astype(jnp.bfloat16), final, preferred_element_type=jnp.float32
    ).astype(jnp.bfloat16)
    keep, give = lower(hidden, weights[2], [routed])
    low = max(dp_count // 4, 1)
    pairs = routed.reshape(dp_count // low, low * per_device, width)
    rows = add(
        pairs[0], *[swap_groups(pairs[i], i * low) for i in range(1, dp_count // low)]
    )
    *arrived, rows, give = lax.optimization_barrier((*arrived, rows, give))
    pairs = rows.reshape(low, per_device, width)
    others = [swap_groups(pairs[i], i) for i in range(1, low)]
    prefill_out = add(resid, keep, swap_cores(give), *arrived)
    others, prefill_out = lax.optimization_barrier((others, prefill_out))
    routed = add(pairs[0], *others)
    return (prefill_out, routed, everything, dec_entries)


def solution(mesh):
    placed = (
        P(("dp", "tensor"), None),
        P(("dp", "tensor"), None),
        P(),
        P("dp"),
        P("dp"),
        P(None, "dp", None, "tensor"),
        P(None, "dp", None, "tensor"),
        P(None, "tensor", None),
        P("tensor", None),
        P(),
        P(),
        P(None, "tensor"),
        P(None, "tensor"),
        P("tensor", None),
    )
    return jax.shard_map(
        on_device,
        mesh=mesh,
        in_specs=placed,
        out_specs=(
            P(("dp", "tensor"), None),
            P(("dp", "tensor"), None),
            P(None, "dp", "tensor"),
            P(None, "dp", "tensor"),
        ),
        check_vma=False,
    )
```
